32 devices in a mesh: dp: 4 (over z), seq: 8 (over y, x, core).
Axes of the slice: x: 2, y: 2, z: 4, core: 2. Of those that a mesh axis runs over, the one named last changes fastest.
Arguments:
- tokens: bfloat16 [8, 1024, 2048], P('dp', 'seq'), may hold values from -6 to 6
- lengths: int32 [8], P('dp'), may hold values from 256 to 1024, as said below
- second_queries: bfloat16 [8, 1024, 2048], P('dp', 'seq'), may hold values from -0.75 to 0.75
- cotangent: bfloat16 [8, 1024, 2048], P('dp', 'seq'), may hold values from -6 to 6
- second_cotangent: bfloat16 [8, 1024, 2048], P('dp', 'seq'), may hold values from -6 to 6
- gain_attn: bfloat16 [2048], P('seq'), may hold values from 0.5 to 1.5
- w_query: bfloat16 [2048, 2048], P('seq'), may hold values from -0.125 to 0.125
- w_key: bfloat16 [2048, 128], P('seq'), may hold values from -0.125 to 0.125
- w_value: bfloat16 [2048, 128], P('seq'), may hold values from -0.125 to 0.125
- w_out: bfloat16 [2048, 2048], P('seq'), may hold values from -0.5 to 0.5
- gain_mlp: bfloat16 [2048], P('seq'), may hold values from 0.5 to 1.5
- w_gate: bfloat16 [2048, 5632], P('seq'), may hold values from -0.125 to 0.125
- w_up: bfloat16 [2048, 5632], P('seq'), may hold values from -0.125 to 0.125
- w_down: bfloat16 [5632, 2048], P('seq'), may hold values from -0.078125 to 0.078125
Outputs:
- out: bfloat16 [8, 1024, 2048], P('dp', 'seq')
- grad_tokens: float32 [8, 1024, 2048], P('dp', 'seq')
- grad_second_queries: bfloat16 [8, 1024, 2048], P('dp', 'seq')
- grad_gain_attn: float32 [2048], P('seq')
- grad_w_query: float32 [2048, 2048], P('seq')
- grad_w_key: float32 [2048, 128], P('seq')
- grad_w_value: float32 [2048, 128], P('seq')
- grad_w_out: float32 [2048, 2048], P('seq')
- grad_gain_mlp: float32 [2048], P('seq')
- grad_w_gate: float32 [2048, 5632], P('seq')
- grad_w_up: float32 [2048, 5632], P('seq')
- grad_w_down: float32 [5632, 2048], P('seq')
The draws below stay inside these ranges and needn't reach their ends.
Inputs may be any that keep to these rules, and one draw needn't show every extreme that they name: `lengths`: in each group of 2 sequences of one index of dp, one is exactly 1024 long; in the first group another is exactly 256 long; positions at or past a sequence's length are padding.
All inputs are finite; a program needn't handle non-finite values.
Results may differ from the reference program's by a relative error of at most 0.023.
Values may be sent and summed in bfloat16 or wider, within the bound.
No kernel may reach another device: no remote copies, remote signals or barrier semaphores. Data moves between devices by JAX's collectives and lax.ppermute only.
A program may use at most 448 MiB of HBM per device.

```python
import math
import jax
import jax.numpy as jnp
from jax import lax

D = 2048
HEADS = 16
HEAD_DIM = 128
FF = 5632
SEQS = 2
SEQLEN = 1024
BATCH = 8


def draw_lengths(key, part):
    key = jax.random.fold_in(key, 11)
    first_key, second_key, third_key = jax.random.split(key, 3)
    groups = BATCH // SEQS
    drawn = jax.random.randint(first_key, (groups, SEQS), SEQLEN // 4, SEQLEN + 1)
    chosen = jax.random.randint(second_key, (groups, 1), 0, SEQS)
    shift = jax.random.randint(third_key, (1, 1), 1, SEQS)
    shortest_pos = (chosen[0:1] + shift) % SEQS
    columns = jnp.arange(SEQS)[None, :]
    first_group = jnp.arange(groups)[:, None] == 0
    shortest = first_group & (columns == shortest_pos)
    drawn = jnp.where(shortest, SEQLEN // 4, drawn)
    return jnp.where(columns == chosen, SEQLEN, drawn).reshape(groups * SEQS).astype(jnp.int32)


def shard_levels(own_key, shape, cuts, smallest, top_value):
    level = 1.0
    for dim, parts in cuts:
        steps = jax.random.uniform(jax.random.fold_in(jax.random.fold_in(own_key, 6), dim), (parts,), jnp.float32, smallest / len(cuts), top_value / len(cuts))
        level = level * jnp.repeat(jnp.exp(steps), shape[dim] // parts).reshape((-1,) + (1,) * (len(shape) - 1 - dim))
    return level


def centred(key, extent, spread, limit, shards=(), held_as=jnp.bfloat16):
    values = jax.random.normal(key, extent, jnp.float32) * spread
    if len(shards) > 0:
        values = shard_levels(key, extent, shards, -0.22, 0.18) * values
    return jnp.clip(values, min=-limit, max=limit).astype(held_as)


def setup_inputs(seed: int = 0) -> dict:
    seeds = jax.random.split(jax.random.key(seed), 15)
    tokens = centred(seeds[0], (BATCH, SEQLEN, D), 1.0, 6.0, ((0, 4), (1, 8)))
    lengths = draw_lengths(jax.random.fold_in(seeds[14], 71), 0)
    second_queries = centred(seeds[2], (BATCH, SEQLEN, HEADS * HEAD_DIM), 0.125, 0.75, ((0, 4), (1, 8)))
    cotangent = centred(seeds[3], (BATCH, SEQLEN, D), 1.0, 6.0, ((0, 4), (1, 8)))
    second_cotangent = centred(seeds[4], (BATCH, SEQLEN, HEADS * HEAD_DIM), 1.0, 6.0, ((0, 4), (1, 8)))
    gain_attn = jnp.clip(1.0 + 0.1 * jax.random.normal(seeds[5], (D,), jnp.float32), 0.5, 1.5).astype(jnp.bfloat16)
    w_query = centred(seeds[6], (D, HEADS * HEAD_DIM), D ** -0.5, 0.125, ((0, 8),))
    w_key = centred(seeds[7], (D, HEAD_DIM), D ** -0.5, 0.125, ((0, 8),))
    w_value = centred(seeds[8], (D, HEAD_DIM), D ** -0.5, 0.125, ((0, 8),))
    w_out = centred(seeds[9], (HEADS * HEAD_DIM, D), (HEADS * HEAD_DIM // 16) ** -0.5, 0.5, ((0, 8),))
    gain_mlp = jnp.clip(1.0 + 0.1 * jax.random.normal(seeds[10], (D,), jnp.float32), 0.5, 1.5).astype(jnp.bfloat16)
    w_gate = centred(seeds[11], (D, FF), D ** -0.5, 0.125, ((0, 8),))
    w_up = centred(seeds[12], (D, FF), D ** -0.5, 0.125, ((0, 8),))
    w_down = centred(seeds[13], (FF, D), FF ** -0.5, 0.078125, ((0, 8),))
    return {"tokens": tokens, "lengths": lengths, "second_queries": second_queries, "cotangent": cotangent, "second_cotangent": second_cotangent, "gain_attn": gain_attn, "w_query": w_query, "w_key": w_key, "w_value": w_value, "w_out": w_out, "gain_mlp": gain_mlp, "w_gate": w_gate, "w_up": w_up, "w_down": w_down}


EPSILON = 1e-05
HIGHEST_PRECISION = lax.Precision.HIGHEST

@jax.custom_vjp
def low(v):
    return lax.optimization_barrier(v.astype(jnp.bfloat16)).astype(jnp.float32)

@jax.custom_vjp
def low_back(v):
    return v

def low_keep(v):
    return (low(v), None)

def low_pass(kept, grad):
    return (grad,)

def back_keep(v):
    return (v, None)

def back_low(kept, grad):
    return (low(grad),)
low.defvjp(low_keep, low_pass)
low_back.defvjp(back_keep, back_low)

def round_both(value):
    return low(low_back(value))

def product(left, right):
    return jnp.dot(left, right, precision=HIGHEST_PRECISION)

def normalize(value, gain):
    return value * lax.rsqrt(lax.optimization_barrier(jnp.mean(value * value, -1, keepdims=True)) + EPSILON) * gain

def rope_tables(positions, head_width):
    half_width = head_width // 2
    spacing = jnp.exp(jnp.arange(half_width).astype(jnp.float32) * (-2.0 * math.log(10000.0) / head_width))
    angles = positions.astype(jnp.float32)[:, None] * spacing[None, :]
    angles = jnp.concatenate([angles, angles], 1)
    return (jnp.cos(angles), jnp.sin(angles))

def rotate(vector, cosine, sine_table):
    half_width = vector.shape[-1] // 2
    turned = jnp.concatenate([-vector[..., half_width:], vector[..., :half_width]], -1)
    return vector * cosine + turned * sine_table

def attend(queries, key_rows, value_rows, length):
    seq_len = key_rows.shape[0]
    block_rows = min(512, seq_len)
    block_count = seq_len // block_rows
    query_blocks = queries.reshape((block_count, block_rows) + queries.shape[1:])
    offsets = jnp.arange(block_count, dtype=jnp.int32) * block_rows
    key_pos = jnp.arange(seq_len, dtype=jnp.int32)

    def one_block(inputs):
        query_block, offset = inputs
        scores = low_back(jnp.einsum('qhd,kd->hqk', query_block, key_rows, precision=HIGHEST_PRECISION))
        query_pos = offset + jnp.arange(block_rows, dtype=jnp.int32)
        allowed = (key_pos[None, :] <= query_pos[:, None]) & (key_pos[None, :] < length)
        scores = jnp.where(allowed[None], scores, -jnp.inf)
        shifted = jnp.exp(scores - lax.optimization_barrier(jnp.max(scores, -1, keepdims=True)))
        probabilities = shifted / lax.optimization_barrier(jnp.sum(shifted, -1, keepdims=True))
        return jnp.einsum('hqk,kd->qhd', low(probabilities), value_rows, precision=HIGHEST_PRECISION)
    return lax.map(jax.checkpoint(one_block), (query_blocks, offsets)).reshape(queries.shape)

def layer_forward(params, inputs_f, second_f, length):
    gain_one, query_mat, key_mat, value_mat, out_mat, gain_two, gate_mat, up_mat, down_mat = params
    seq_len = inputs_f.shape[0]
    cosine, sine_table = rope_tables(jnp.arange(seq_len, dtype=jnp.int32), HEAD_DIM)
    normed_one = low(normalize(inputs_f, gain_one))
    q_linear = low_back(product(normed_one, query_mat)).reshape(seq_len, HEADS, HEAD_DIM)
    queries = round_both(rotate(q_linear, cosine[:, None, :], sine_table[:, None, :]) * (1.0 / math.sqrt(HEAD_DIM)))
    key_rows = round_both(rotate(low_back(product(normed_one, key_mat)), cosine, sine_table))
    value_rows = round_both(product(normed_one, value_mat))
    attn = round_both(attend(queries, key_rows, value_rows, length)).reshape(seq_len, HEADS * HEAD_DIM)
    middle = inputs_f + low_back(product(attn, out_mat))
    normed_two = low(normalize(middle, gain_two))
    gate_pre = low_back(product(normed_two, gate_mat))
    up_pre = low_back(product(normed_two, up_mat))
    hidden = low(jax.nn.silu(gate_pre) * up_pre)
    out_rows = middle + low_back(product(hidden, down_mat))
    second_heads = low_back(second_f).reshape(seq_len, HEADS, HEAD_DIM)
    second_out = attend(second_heads, key_rows, value_rows, length).reshape(seq_len, HEADS * HEAD_DIM)
    return (out_rows, second_out)

def reference(tokens, lengths, second_queries, cotangent, second_cotangent, gain_attn, w_query, w_key, w_value, w_out, gain_mlp, w_gate, w_up, w_down):
    params = tuple((weight.astype(jnp.float32) for weight in (gain_attn, w_query, w_key, w_value, w_out, gain_mlp, w_gate, w_up, w_down)))
    seq_len = tokens.shape[1]

    def per_sequence(totals, inputs):
        token_seq, second_seq, cot_seq, second_cot, length = inputs
        valid = (jnp.arange(seq_len, dtype=jnp.int32) < length).astype(jnp.float32)[:, None]

        def forward(weights, inputs_f, second_f):
            return layer_forward(weights, inputs_f, second_f, length)
        (out_rows, second_out), pull = jax.vjp(forward, params, token_seq.astype(jnp.float32), second_seq.astype(jnp.float32))
        grads, grad_inputs, grad_second = pull((cot_seq.astype(jnp.float32) * valid, second_cot.astype(jnp.float32) * valid))
        totals = jax.tree.map(lambda left, right: left + right, totals, grads)
        return (totals, (out_rows.astype(jnp.bfloat16), grad_inputs, grad_second.astype(jnp.bfloat16)))
    zero_grads = tuple((jnp.zeros(weight.shape, jnp.float32) for weight in params))
    totals, outputs = lax.scan(per_sequence, zero_grads, (tokens, second_queries, cotangent, second_cotangent, lengths))
    return (outputs[0], outputs[1], outputs[2], totals[0], totals[1], totals[2], totals[3], totals[4], totals[5], totals[6], totals[7], totals[8])
```

```python
import functools
import math

import jax
import jax.numpy as jnp
from jax import lax
from jax.experimental import pallas as pl
from jax.experimental.pallas import tpu as pltpu
from jax.sharding import PartitionSpec as P

EPSILON = 1e-05
BF = jnp.bfloat16
F32 = jnp.float32
QUERY_ROWS = 256
VMEM_BYTES = 32 * 1024 * 1024


def dot_nn(left, right):
    return jnp.dot(left, right, preferred_element_type=F32)


def dot_nt(left, right):
    return lax.dot_general(left, right, (((1,), (1,)), ((), ())), preferred_element_type=F32)


def dot_tn(left, right):
    return lax.dot_general(left, right, (((0,), (0,)), ((), ())), preferred_element_type=F32)


def is_cube(count):
    return count == 8


def order_key(count):
    rank = lax.axis_index("seq")
    return rank if is_cube(count) else jnp.zeros_like(rank)


def swap(array, bit):
    return lax.ppermute(array, "seq", [(i, i ^ bit) for i in range(8)])


def add_rounded(*terms):
    total = terms[0].astype(F32)
    for term in terms[1:]:
        total = total + term.astype(F32)
    return total.astype(BF)


def gather_pieces(piece, count):
    if not is_cube(count):
        return lax.all_gather(piece, "seq", axis=0, tiled=False)
    half = piece.shape[0] // 2
    from_x = swap(piece, 2)
    from_y = swap(piece, 4)
    from_core = swap(piece, 1)
    far_low = swap(from_x[:half], 4)
    far_high = swap(from_y[half:], 2)
    core_x = swap(from_x, 1)
    core_y = swap(from_y, 1)
    far = jnp.concatenate([far_low, far_high], 0)
    core_far = swap(far, 1)
    return jnp.stack([piece, from_core, from_x, core_x, from_y, core_y, far, core_far], 0)


def scatter_pieces(parts, count):
    if not is_cube(count):
        return lax.psum_scatter(parts, "seq", scatter_dimension=0, tiled=False)
    half = parts.shape[1] // 2
    far = add_rounded(parts[6], swap(parts[7], 1))
    far_x = swap(far[:half], 2)
    far_y = swap(far[half:], 4)
    near_x = add_rounded(parts[2], swap(parts[3], 1))
    near_y = add_rounded(parts[4], swap(parts[5], 1))
    near_y = jnp.concatenate([add_rounded(near_y[:half], far_x), near_y[half:]], 0)
    near_x = jnp.concatenate([near_x[:half], add_rounded(near_x[half:], far_y)], 0)
    got_x = swap(near_x, 2)
    got_y = swap(near_y, 4)
    own = add_rounded(parts[0], swap(parts[1], 1))
    return add_rounded(own, got_x, got_y)


def rows_to_columns(weight):
    return lax.all_to_all(weight, "seq", split_axis=1, concat_axis=0, tiled=True)


def columns_to_rows(weight):
    return lax.all_to_all(weight, "seq", split_axis=0, concat_axis=1, tiled=True)


def load_keys(key_ref, kv_ref, rows_ref, count, head, column):
    chunk = kv_ref.shape[2]
    for place in range(count):
        rows_ref[place * chunk : (place + 1) * chunk, :] = kv_ref[
            place ^ key_ref, 0, :, column * head : (column + 1) * head
        ]


def transpose_rows(rows_ref, turned_ref):
    step = 128
    for start in range(0, rows_ref.shape[0], step):
        turned_ref[:, start : start + step] = (
            rows_ref[start : start + step, :].astype(F32).T.astype(BF)
        )


def masked_scores(keys, queries, limit):
    scores = dot_nt(keys, queries)
    key_pos = lax.broadcasted_iota(jnp.int32, scores.shape, 0)
    return jnp.where(key_pos <= limit, scores, -jnp.inf)


def forward_kernel(
    lengths_ref, key_ref, q_ref, kv_ref, attn_ref, lse_ref, keys, values, values_t
):
    count, _, chunk, _ = q_ref.shape
    head = keys.shape[1]
    total = keys.shape[0]
    block = min(QUERY_ROWS, total)
    per_block = block // chunk
    key = key_ref[0]
    length = lengths_ref[pl.program_id(0)]
    load_keys(key, kv_ref, keys, count, head, 0)
    load_keys(key, kv_ref, values, count, head, 1)
    transpose_rows(values, values_t)
    for start in range(0, total, block):
        limit_row = start + lax.broadcasted_iota(jnp.int32, (1, block), 1)
        limit = jnp.minimum(limit_row, length - 1)
        seen = start + block
        places = [(start // chunk + i) ^ key for i in range(per_block)]
        for h in range(q_ref.shape[3] // head):
            columns = slice(h * head, (h + 1) * head)
            queries = jnp.concatenate([q_ref[p, 0, :, columns] for p in places], 0)
            scores = masked_scores(keys[:seen, :], queries, limit)
            top = jnp.max(scores, 0, keepdims=True)
            weights = jnp.exp(scores - top)
            norm = jnp.sum(weights, 0, keepdims=True)
            mixed = dot_nn(values_t[:, :seen], weights.astype(BF)) / norm
            rows = mixed.T.astype(BF)
            for i, p in enumerate(places):
                attn_ref[p, 0, :, columns] = rows[i * chunk : (i + 1) * chunk]
            lse_ref[0, h : h + 1, start : start + block] = top + jnp.log(norm)


def attend_forward(queries, key_values, lengths, key, head):
    count, seqs, chunk, width = queries.shape
    total = count * chunk
    heads = width // head
    whole = lambda s, *_: (0, s, 0, 0)
    return pl.pallas_call(
        forward_kernel,
        grid_spec=pltpu.PrefetchScalarGridSpec(
            num_scalar_prefetch=2,
            grid=(seqs,),
            in_specs=[
                pl.BlockSpec((count, 1, chunk, width), whole),
                pl.BlockSpec((count, 1, chunk, 2 * head), whole),
            ],
            out_specs=[
                pl.BlockSpec((count, 1, chunk, width), whole),
                pl.BlockSpec((1, heads, total), lambda s, *_: (s, 0, 0)),
            ],
            scratch_shapes=[
                pltpu.VMEM((total, head), BF),
                pltpu.VMEM((total, head), BF),
                pltpu.VMEM((head, total), BF),
            ],
        ),
        out_shape=[
            jax.ShapeDtypeStruct(queries.shape, BF),
            jax.ShapeDtypeStruct((seqs, heads, total), F32),
        ],
        compiler_params=pltpu.CompilerParams(vmem_limit_bytes=VMEM_BYTES),
        cost_estimate=pl.CostEstimate(
            flops=2 * seqs * heads * total * total * head,
            bytes_accessed=4 * queries.size + 2 * key_values.size,
            transcendentals=seqs * heads * total * total // 2,
        ),
    )(lengths, key, queries, key_values)


def second_kernel(
    lengths_ref, key_ref, q_ref, up_ref, kv_ref, dq_ref, dkv_ref, keys, values, keys_t, dk, dv
):
    _, chunk, width = q_ref.shape
    count = kv_ref.shape[0]
    head = keys.shape[1]
    total = keys.shape[0]
    block = min(QUERY_ROWS, total)
    per_block = block // chunk
    key = key_ref[0]
    rank = key_ref[1]
    length = lengths_ref[pl.program_id(0)]
    load_keys(key, kv_ref, keys, count, head, 0)
    load_keys(key, kv_ref, values, count, head, 1)
    transpose_rows(keys, keys_t)
    dk[...] = jnp.zeros_like(dk)
    dv[...] = jnp.zeros_like(dv)
    own = rank * chunk + lax.broadcasted_iota(jnp.int32, (1, block), 1) % chunk
    limit = jnp.minimum(own, length - 1)
    live = rank * chunk + lax.broadcasted_iota(jnp.int32, (chunk, head), 0) < length
    for first in range(0, width // head, per_block):
        spans = [slice((first + i) * head, (first + i + 1) * head) for i in range(per_block)]
        queries = jnp.concatenate([q_ref[0, :, s] for s in spans], 0)
        upstream = jnp.concatenate(
            [jnp.where(live, up_ref[0, :, s].astype(F32), 0.0).astype(BF) for s in spans], 0
        )
        scores = masked_scores(keys[...], queries, limit)
        weights = jnp.exp(scores - jnp.max(scores, 0, keepdims=True))
        probs = weights * (1.0 / jnp.sum(weights, 0, keepdims=True))
        product = probs * dot_nt(values[...], upstream)
        d_scores = (product - probs * jnp.sum(product, 0, keepdims=True)).astype(BF)
        d_queries = dot_nn(keys_t[...], d_scores).T.astype(BF)
        for i, s in enumerate(spans):
            dq_ref[0, :, s] = d_queries[i * chunk : (i + 1) * chunk]
        dk[...] += dot_nn(d_scores, queries)
        dv[...] += dot_nn(probs.astype(BF), upstream)
    for place in range(count):
        rows = slice(place * chunk, (place + 1) * chunk)
        dkv_ref[place ^ key, 0, :, :head] = dk[rows, :]
        dkv_ref[place ^ key, 0, :, head:] = dv[rows, :]


def attend_second(queries, upstream, key_values, lengths, key, head):
    seqs, chunk, width = queries.shape
    count = key_values.shape[0]
    total = count * chunk
    whole = lambda s, *_: (0, s, 0, 0)
    local = pl.BlockSpec((1, chunk, width), lambda s, *_: (s, 0, 0))
    return pl.pallas_call(
        second_kernel,
        grid_spec=pltpu.PrefetchScalarGridSpec(
            num_scalar_prefetch=2,
            grid=(seqs,),
            in_specs=[local, local, pl.BlockSpec((count, 1, chunk, 2 * head), whole)],
            out_specs=[local, pl.BlockSpec((count, 1, chunk, 2 * head), whole)],
            scratch_shapes=[
                pltpu.VMEM((total, head), BF),
                pltpu.VMEM((total, head), BF),
                pltpu.VMEM((head, total), BF),
                pltpu.VMEM((total, head), F32),
                pltpu.VMEM((total, head), F32),
            ],
        ),
        out_shape=[
            jax.ShapeDtypeStruct(queries.shape, BF),
            jax.ShapeDtypeStruct(key_values.shape, F32),
        ],
        compiler_params=pltpu.CompilerParams(vmem_limit_bytes=VMEM_BYTES),
        cost_estimate=pl.CostEstimate(
            flops=20 * seqs * chunk * width * total // 2,
            bytes_accessed=6 * queries.size + 6 * key_values.size,
            transcendentals=seqs * chunk * width * total // head,
        ),
    )(lengths, key, queries, upstream, key_values)


def backward_kernel(
    lengths_ref,
    key_ref,
    q_ref,
    up_ref,
    attn_ref,
    kv_ref,
    lse_ref,
    more_ref,
    dq_ref,
    dkv_ref,
    keys,
    values,
    keys_t,
    dk,
    dv,
):
    count, _, chunk, width = q_ref.shape
    head = keys.shape[1]
    total = keys.shape[0]
    block = min(QUERY_ROWS, total)
    per_block = block // chunk
    key = key_ref[0]
    length = lengths_ref[pl.program_id(0)]
    load_keys(key, kv_ref, keys, count, head, 0)
    load_keys(key, kv_ref, values, count, head, 1)
    transpose_rows(keys, keys_t)
    for place in range(count):
        rows = slice(place * chunk, (place + 1) * chunk)
        dk[rows, :] = more_ref[place ^ key, 0, :, :head]
        dv[rows, :] = more_ref[place ^ key, 0, :, head:]
    for start in range(0, total, block):
        limit_row = start + lax.broadcasted_iota(jnp.int32, (1, block), 1)
        limit = jnp.minimum(limit_row, length - 1)
        seen = start + block
        places = [(start // chunk + i) ^ key for i in range(per_block)]
        for h in range(width // head):
            columns = slice(h * head, (h + 1) * head)
            queries = jnp.concatenate([q_ref[p, 0, :, columns] for p in places], 0)
            upstream = jnp.concatenate([up_ref[p, 0, :, columns] for p in places], 0)
            attn = jnp.concatenate([attn_ref[p, 0, :, columns] for p in places], 0)
            centre = jnp.sum((upstream.astype(F32) * attn.astype(F32)).T, 0, keepdims=True)
            scores = masked_scores(keys[:seen, :], queries, limit)
            probs = jnp.exp(scores - lse_ref[0, h : h + 1, start : start + block])
            d_probs = dot_nt(values[:seen, :], upstream)
            d_scores = (probs * (d_probs - centre)).astype(BF)
            d_queries = dot_nn(keys_t[:, :seen], d_scores).T.astype(BF)
            for i, p in enumerate(places):
                dq_ref[p, 0, :, columns] = d_queries[i * chunk : (i + 1) * chunk]
            dk[:seen, :] += dot_nn(d_scores, queries)
            dv[:seen, :] += dot_nn(probs.astype(BF), upstream)
    for place in range(count):
        rows = slice(place * chunk, (place + 1) * chunk)
        dkv_ref[place ^ key, 0, :, :head] = dk[rows, :].astype(BF)
        dkv_ref[place ^ key, 0, :, head:] = dv[rows, :].astype(BF)


def attend_backward(queries, upstream, attn, key_values, lse, more, lengths, key, head):
    count, seqs, chunk, width = queries.shape
    total = count * chunk
    heads = width // head
    whole = lambda s, *_: (0, s, 0, 0)
    by_head = pl.BlockSpec((count, 1, chunk, width), whole)
    shared = pl.BlockSpec((count, 1, chunk, 2 * head), whole)
    return pl.pallas_call(
        backward_kernel,
        grid_spec=pltpu.PrefetchScalarGridSpec(
            num_scalar_prefetch=2,
            grid=(seqs,),
            in_specs=[
                by_head,
                by_head,
                by_head,
                shared,
                pl.BlockSpec((1, heads, total), lambda s, *_: (s, 0, 0)),
                shared,
            ],
            out_specs=[by_head, shared],
            scratch_shapes=[
                pltpu.VMEM((total, head), BF),
                pltpu.VMEM((total, head), BF),
                pltpu.VMEM((head, total), BF),
                pltpu.VMEM((total, head), F32),
                pltpu.VMEM((total, head), F32),
            ],
        ),
        out_shape=[
            jax.ShapeDtypeStruct(queries.shape, BF),
            jax.ShapeDtypeStruct(key_values.shape, BF),
        ],
        compiler_params=pltpu.CompilerParams(vmem_limit_bytes=VMEM_BYTES),
        cost_estimate=pl.CostEstimate(
            flops=5 * seqs * heads * total * total * head,
            bytes_accessed=8 * queries.size + 8 * key_values.size,
            transcendentals=seqs * heads * total * total // 2,
        ),
    )(lengths, key, queries, upstream, attn, key_values, lse, more)


def rope_tables(positions, head_width):
    half_width = head_width // 2
    spacing = jnp.exp(
        jnp.arange(half_width).astype(F32) * (-2.0 * math.log(10000.0) / head_width)
    )
    angles = positions.astype(F32)[..., None] * spacing
    angles = jnp.concatenate([angles, angles], -1)
    return (jnp.cos(angles), jnp.sin(angles))


def rotate(vector, cosine, sine_table):
    half_width = vector.shape[-1] // 2
    turned = jnp.concatenate([-vector[..., half_width:], vector[..., :half_width]], -1)
    return vector * cosine + turned * sine_table


def rotate_back(gradient, cosine, sine_table):
    half_width = gradient.shape[-1] // 2
    scaled = gradient * sine_table
    turned = jnp.concatenate([scaled[..., half_width:], -scaled[..., :half_width]], -1)
    return gradient * cosine + turned


def rms_scale(values_in):
    return lax.rsqrt(jnp.mean(values_in * values_in, -1, keepdims=True) + EPSILON)


def norm_back(grad_normed, inputs, scale_rows, gain):
    weighted = grad_normed * gain
    cubed = scale_rows * scale_rows * scale_rows
    return scale_rows * weighted - inputs * cubed * jnp.mean(weighted * inputs, -1, keepdims=True)


def body(
    tokens,
    lengths,
    second_queries,
    cotangent,
    second_cotangent,
    gain_attn,
    w_query,
    w_key,
    w_value,
    w_out,
    gain_mlp,
    w_gate,
    w_up,
    w_down,
):
    count = lax.axis_size("seq")
    rank = lax.axis_index("seq")
    key = order_key(count)
    keys_of = jnp.stack([key, rank]).astype(jnp.int32)
    seqs, chunk, width = tokens.shape
    head = w_key.shape[1]
    rows = seqs * chunk
    all_rows = count * rows
    local_heads = w_query.shape[1] // head // count
    scale = 1.0 / math.sqrt(head)
    bf_sum = lambda share: lax.psum(share.astype(BF), "dp").astype(F32)

    gains = lax.all_gather(jnp.stack([gain_attn, gain_mlp]), "seq", axis=1, tiled=True).astype(F32)
    gain_one, gain_two = gains[0], gains[1]
    kv_mat = lax.all_gather(jnp.concatenate([w_key, w_value], 1), "seq", axis=0, tiled=True)
    query_cols = rows_to_columns(w_query)
    gate_cols = rows_to_columns(w_gate)
    up_cols = rows_to_columns(w_up)

    local_pos = rank * chunk + jnp.arange(chunk, dtype=jnp.int32)
    valid = (local_pos[None, :] < lengths[:, None]).astype(F32).reshape(rows, 1)
    owners = jnp.arange(count, dtype=jnp.int32) ^ key
    all_pos = owners[:, None] * chunk + jnp.arange(chunk, dtype=jnp.int32)[None, :]
    cosine, sine_table = rope_tables(all_pos, head)
    cos_kv, sin_kv = cosine[:, None], sine_table[:, None]
    cos_q, sin_q = cosine[:, None, :, None], sine_table[:, None, :, None]
    cos_own, sin_own = rope_tables(local_pos, head)

    inputs = tokens.reshape(rows, width)
    inputs_f = inputs.astype(F32)
    scale_one = rms_scale(inputs_f)
    all_inputs = gather_pieces(inputs, count).reshape(all_rows, width).astype(F32)
    normed_one = (all_inputs * rms_scale(all_inputs) * gain_one).astype(BF)
    q_linear = dot_nn(normed_one, query_cols).reshape(count, seqs, chunk, local_heads, head)
    queries = (rotate(q_linear, cos_q, sin_q) * scale).astype(BF)
    queries = queries.reshape(count, seqs, chunk, local_heads * head)
    kv_linear = dot_nn(normed_one, kv_mat).reshape(count, seqs, chunk, 2 * head)
    key_values = jnp.concatenate(
        [
            rotate(kv_linear[..., :head], cos_kv, sin_kv).astype(BF),
            kv_linear[..., head:].astype(BF),
        ],
        -1,
    )
    attn, lse = attend_forward(queries, key_values, lengths, keys_of, head)
    attn_rows = attn.reshape(all_rows, local_heads * head)
    proj_parts = dot_nn(attn_rows, w_out).astype(BF).reshape(count, rows, width)
    middle = inputs_f + scatter_pieces(proj_parts, count).astype(F32)

    grad_second, dkv_second = attend_second(
        second_queries, second_cotangent, key_values, lengths, keys_of, head
    )

    grad_out = cotangent.reshape(rows, width).astype(F32) * valid
    grad_branch = gather_pieces(grad_out.astype(BF), count).reshape(all_rows, width)
    scale_two = rms_scale(middle)
    normed_two_own = (middle * scale_two * gain_two).astype(BF)
    normed_two = gather_pieces(normed_two_own, count).reshape(all_rows, width)
    gate_pre = dot_nn(normed_two, gate_cols)
    up_pre = dot_nn(normed_two, up_cols)
    sigma = jax.nn.sigmoid(gate_pre)
    silu_gate = gate_pre * sigma
    hidden = (silu_gate * up_pre).astype(BF)
    grad_hidden = dot_nt(grad_branch, w_down)
    grad_gate_pre = (grad_hidden * up_pre * (sigma * (1.0 + gate_pre * (1.0 - sigma)))).astype(BF)
    grad_up_pre = (grad_hidden * silu_gate).astype(BF)
    normed_parts = (dot_nt(grad_gate_pre, gate_cols) + dot_nt(grad_up_pre, up_cols)).astype(BF)
    grad_normed_two = scatter_pieces(normed_parts.reshape(count, rows, width), count).astype(F32)
    grad_middle = grad_out + norm_back(grad_normed_two, middle, scale_two, gain_two)
    down_parts = dot_nn(hidden, w_down).astype(BF).reshape(count, rows, width)
    out = (middle + scatter_pieces(down_parts, count).astype(F32)).astype(BF)

    grad_w_down = bf_sum(dot_tn(hidden, grad_branch))
    grad_w_gate = bf_sum(columns_to_rows(dot_tn(normed_two, grad_gate_pre).astype(BF)))
    grad_w_up = bf_sum(columns_to_rows(dot_tn(normed_two, grad_up_pre).astype(BF)))

    grad_proj = gather_pieces(grad_middle.astype(BF), count).reshape(all_rows, width)
    grad_w_out = bf_sum(dot_tn(attn_rows, grad_proj))
    grad_attn = dot_nt(grad_proj, w_out).astype(BF).reshape(queries.shape)
    grad_q, dkv_parts = attend_backward(
        queries, grad_attn, attn, key_values, lse, dkv_second, lengths, keys_of, head
    )
    grad_q = grad_q.reshape(count, seqs, chunk, local_heads, head).astype(F32) * scale
    grad_q_linear = rotate_back(grad_q, cos_q, sin_q).astype(BF).reshape(all_rows, -1)
    grad_w_query = bf_sum(columns_to_rows(dot_tn(normed_one, grad_q_linear).astype(BF)))
    one_parts = dot_nt(grad_q_linear, query_cols).astype(BF).reshape(count, rows, width)
    dkv_own = scatter_pieces(dkv_parts.reshape(count, rows, 2 * head), count)
    dkv_own = dkv_own.reshape(seqs, chunk, 2 * head)
    grad_k_linear = rotate_back(dkv_own[..., :head].astype(F32), cos_own, sin_own).astype(BF)
    grad_kv_own = jnp.concatenate([grad_k_linear, dkv_own[..., head:]], -1).reshape(rows, 2 * head)
    grad_kv = gather_pieces(grad_kv_own, count).reshape(all_rows, 2 * head)
    own_columns = w_query.shape[0]
    normed_slice = lax.dynamic_slice_in_dim(normed_one, rank * own_columns, own_columns, 1)
    grad_w_kv = bf_sum(dot_tn(normed_slice, grad_kv))
    grad_normed_one = scatter_pieces(one_parts, count).astype(F32) + dot_nt(grad_kv_own, kv_mat)
    grad_tokens = grad_middle + norm_back(grad_normed_one, inputs_f, scale_one, gain_one)

    gain_shares = jnp.stack(
        [
            jnp.sum(grad_normed_one * (inputs_f * scale_one), 0),
            jnp.sum(grad_normed_two * (middle * scale_two), 0),
        ]
    )
    gain_sums = lax.psum(gain_shares, ("seq", "dp"))
    own_gain = gain_attn.shape[0]
    grad_gains = lax.dynamic_slice_in_dim(gain_sums, rank * own_gain, own_gain, 1)

    return (
        out.reshape(tokens.shape),
        grad_tokens.reshape(tokens.shape),
        grad_second,
        grad_gains[0],
        grad_w_query,
        grad_w_kv[:, :head],
        grad_w_kv[:, head:],
        grad_w_out,
        grad_gains[1],
        grad_w_gate,
        grad_w_up,
        grad_w_down,
    )


def solution(mesh):
    return jax.shard_map(
        body,
        mesh=mesh,
        in_specs=(
            P("dp", "seq", None),
            P("dp"),
            P("dp", "seq", None),
            P("dp", "seq", None),
            P("dp", "seq", None),
            P("seq"),
            P("seq", None),
            P("seq", None),
            P("seq", None),
            P("seq", None),
            P("seq"),
            P("seq", None),
            P("seq", None),
            P("seq", None),
        ),
        out_specs=(
            P("dp", "seq", None),
            P("dp", "seq", None),
            P("dp", "seq", None),
            P("seq"),
            P("seq", None),
            P("seq", None),
            P("seq", None),
            P("seq", None),
            P("seq"),
            P("seq", None),
            P("seq", None),
            P("seq", None),
        ),
        check_vma=False,
    )
```

```python
import functools
import math

import jax
import jax.numpy as jnp
from jax import lax
from jax.experimental import pallas as pl
from jax.experimental.pallas import tpu as pltpu
from jax.sharding import PartitionSpec as P

EPSILON = 1e-05
BF = jnp.bfloat16
F32 = jnp.float32
QUERY_ROWS = 256
VMEM_BYTES = 32 * 1024 * 1024
LIGHT = pl.CostEstimate(flops=1000, bytes_accessed=1000, transcendentals=0)
MLP_VMEM_BYTES = 48 * 1024 * 1024


def dot_nn(left, right):
    return jnp.dot(left, right, preferred_element_type=F32)


def dot_nt(left, right):
    return lax.dot_general(left, right, (((1,), (1,)), ((), ())), preferred_element_type=F32)


def dot_tn(left, right):
    return lax.dot_general(left, right, (((0,), (0,)), ((), ())), preferred_element_type=F32)


def is_cube(count):
    return count == 8


def order_key(count):
    rank = lax.axis_index("seq")
    return rank if is_cube(count) else jnp.zeros_like(rank)


def swap(array, bit):
    return lax.ppermute(array, "seq", [(i, i ^ bit) for i in range(8)])


def add_rounded(*terms):
    total = terms[0].astype(F32)
    for term in terms[1:]:
        total = total + term.astype(F32)
    return total.astype(BF)


def after(value, *others):
    return lax.optimization_barrier((value, others))[0]


def gather_near(piece, count, *between):
    if not is_cube(count):
        gathered = lax.all_gather(piece, "seq", axis=0, tiled=False)
        return [gathered[j] for j in range(count)]
    from_x = swap(piece, 2)
    from_y = swap(piece, 4)
    from_core = swap(piece, 1)
    if between:
        from_x, from_y = after([from_x, from_y], *between)
    return [piece, from_core, from_x, swap(from_x, 1), from_y, swap(from_y, 1)]


def gather_far(near, count):
    if not is_cube(count):
        return near[-2]
    half = near[0].shape[0] // 2
    return jnp.concatenate([swap(near[2][:half], 4), swap(near[4][half:], 2)], 0)


def gather_last(near, far, count):
    return swap(far, 1) if is_cube(count) else near[-1]


def gather_pieces(piece, count):
    near = gather_near(piece, count)
    far = gather_far(near, count)
    last = gather_last(near, far, count)
    return (near if is_cube(count) else near[:-2]) + [far, last]


def scatter_far(parts, count):
    if not is_cube(count):
        return parts
    half = parts[0].shape[0] // 2
    far = add_rounded(parts[6], swap(parts[7], 1))
    far_x = swap(far[:half], 2)
    far_y = swap(far[half:], 4)
    near_x = add_rounded(parts[2], swap(parts[3], 1))
    near_y = add_rounded(parts[4], swap(parts[5], 1))
    near_y = jnp.concatenate([add_rounded(near_y[:half], far_x), near_y[half:]], 0)
    near_x = jnp.concatenate([near_x[:half], add_rounded(near_x[half:], far_y)], 0)
    own = add_rounded(parts[0], swap(parts[1], 1))
    return [own, near_x, near_y]


def scatter_near(sums, count, *window):
    if not is_cube(count):
        return lax.psum_scatter(jnp.stack(sums), "seq", scatter_dimension=0, tiled=False)
    own, near_x, near_y = sums
    got_x = swap(near_x, 2)
    got_y = swap(near_y, 4)
    return add_rounded(after(own, *window), got_x, got_y)


def scatter_pieces(parts, count, *window):
    return scatter_near(scatter_far(parts, count), count, *window)


def gather_ordered(piece, count):
    if not is_cube(count):
        return lax.all_gather(piece, "seq", axis=0, tiled=False)
    rank = lax.axis_index("seq")
    held = piece
    for bit in (4, 2, 1):
        other = swap(held, bit)
        upper = (rank & bit) != 0
        held = jnp.stack([jnp.where(upper, other, held), jnp.where(upper, held, other)])
    held = held.transpose(2, 1, 0, *range(3, held.ndim))
    return held.reshape(count, *piece.shape)


def rows_to_columns(weight):
    return lax.all_to_all(weight, "seq", split_axis=1, concat_axis=0, tiled=True)


def columns_to_rows(weight):
    return lax.all_to_all(weight, "seq", split_axis=0, concat_axis=1, tiled=True)


def send_dp(array, pairs):
    return lax.ppermute(array, "dp", pairs)


def line_share(array):
    return lax.psum_scatter(array, "dp", scatter_dimension=0, tiled=True)


def line_gather(share, *windows):
    if lax.axis_size("dp") != 4:
        gathered = lax.all_gather(share, "dp", axis=0, tiled=False)
        return [[gathered[m]] for m in range(gathered.shape[0])]
    ups, downs = [share], [share]
    for step in range(3):
        up, down = ups[-1], downs[-1]
        if step and len(windows) >= step:
            up, down = after([up, down], windows[step - 1])
        ups.append(send_dp(up, [(i, i + 1) for i in range(step, 3)]))
        downs.append(send_dp(down, [(i + 1, i) for i in range(3 - step)]))
    return [[ups[k - m] if k > m else downs[m - k] for k in range(4)] for m in range(4)]


def choose(options, place):
    chosen = options[-1]
    for k in range(len(options) - 2, -1, -1):
        chosen = jnp.where(place == k, options[k], chosen)
    return chosen


def line_rows(gathered):
    place = lax.axis_index("dp")
    return jnp.concatenate([choose(options, place) for options in gathered], 0).astype(F32)


def stage(always, work, *operands):
    shapes = jax.eval_shape(work, *operands)
    empty = lambda *_: jax.tree.map(lambda leaf: jnp.zeros(leaf.shape, leaf.dtype), shapes)
    return lax.cond(always, work, empty, *operands)


def small_sum(share, count):
    if not is_cube(count) or lax.axis_size("dp") != 4:
        own = lax.psum_scatter(share, "seq", scatter_dimension=0, tiled=False)
        return lax.psum(own, "dp")
    rank = lax.axis_index("seq")
    kept = share
    for bit in (4, 2, 1):
        upper = (rank & bit) != 0
        low, high = kept[:bit], kept[bit:]
        kept = add_rounded(jnp.where(upper, high, low), swap(jnp.where(upper, low, high), bit))
    kept = kept[0]
    for bit in (1, 2):
        kept = add_rounded(kept, send_dp(kept, [(i, i ^ bit) for i in range(4)]))
    return kept


def load_keys(key_ref, kv_ref, rows_ref, count, head, column):
    chunk = kv_ref.shape[2]
    for place in range(count):
        rows_ref[place * chunk : (place + 1) * chunk, :] = kv_ref[
            place ^ key_ref, 0, :, column * head : (column + 1) * head
        ]


def transpose_rows(rows_ref, turned_ref):
    step = 128
    for start in range(0, rows_ref.shape[0], step):
        turned_ref[:, start : start + step] = (
            rows_ref[start : start + step, :].astype(F32).T.astype(BF)
        )


def masked_scores(keys, queries, limit):
    scores = dot_nt(keys, queries)
    key_pos = lax.broadcasted_iota(jnp.int32, scores.shape, 0)
    return jnp.where(key_pos <= limit, scores, -jnp.inf)


def forward_kernel(
    lengths_ref, key_ref, q_ref, kv_ref, attn_ref, lse_ref, keys, values, values_t
):
    count, _, chunk, _ = q_ref.shape
    head = keys.shape[1]
    total = keys.shape[0]
    block = min(QUERY_ROWS, total)
    per_block = block // chunk
    key = key_ref[0]
    length = lengths_ref[pl.program_id(0)]
    load_keys(key, kv_ref, keys, count, head, 0)
    load_keys(key, kv_ref, values, count, head, 1)
    transpose_rows(values, values_t)
    for start in range(0, total, block):
        limit_row = start + lax.broadcasted_iota(jnp.int32, (1, block), 1)
        limit = jnp.minimum(limit_row, length - 1)
        seen = start + block
        places = [(start // chunk + i) ^ key for i in range(per_block)]
        for h in range(q_ref.shape[3] // head):
            columns = slice(h * head, (h + 1) * head)
            queries = jnp.concatenate([q_ref[p, 0, :, columns] for p in places], 0)
            scores = masked_scores(keys[:seen, :], queries, limit)
            top = jnp.max(scores, 0, keepdims=True)
            weights = jnp.exp(scores - top)
            norm = jnp.sum(weights, 0, keepdims=True)
            mixed = dot_nn(values_t[:, :seen], weights.astype(BF)) / norm
            rows = mixed.T.astype(BF)
            for i, p in enumerate(places):
                attn_ref[p, 0, :, columns] = rows[i * chunk : (i + 1) * chunk]
            lse_ref[0, h : h + 1, start : start + block] = top + jnp.log(norm)


def attend_forward(queries, key_values, lengths, key, head):
    count, seqs, chunk, width = queries.shape
    total = count * chunk
    heads = width // head
    whole = lambda s, *_: (0, s, 0, 0)
    return pl.pallas_call(
        forward_kernel,
        grid_spec=pltpu.PrefetchScalarGridSpec(
            num_scalar_prefetch=2,
            grid=(seqs,),
            in_specs=[
                pl.BlockSpec((count, 1, chunk, width), whole),
                pl.BlockSpec((count, 1, chunk, 2 * head), whole),
            ],
            out_specs=[
                pl.BlockSpec((count, 1, chunk, width), whole),
                pl.BlockSpec((1, heads, total), lambda s, *_: (s, 0, 0)),
            ],
            scratch_shapes=[
                pltpu.VMEM((total, head), BF),
                pltpu.VMEM((total, head), BF),
                pltpu.VMEM((head, total), BF),
            ],
        ),
        out_shape=[
            jax.ShapeDtypeStruct(queries.shape, BF),
            jax.ShapeDtypeStruct((seqs, heads, total), F32),
        ],
        compiler_params=pltpu.CompilerParams(vmem_limit_bytes=VMEM_BYTES),
        cost_estimate=LIGHT,
    )(lengths, key, queries, key_values)


def second_kernel(
    lengths_ref, key_ref, q_ref, up_ref, kv_ref, dq_ref, dkv_ref, keys, values, keys_t, dk, dv
):
    _, chunk, width = q_ref.shape
    count = kv_ref.shape[0]
    head = keys.shape[1]
    total = keys.shape[0]
    block = min(QUERY_ROWS, total)
    per_block = block // chunk
    key = key_ref[0]
    rank = key_ref[1]
    length = lengths_ref[pl.program_id(0)]
    load_keys(key, kv_ref, keys, count, head, 0)
    load_keys(key, kv_ref, values, count, head, 1)
    transpose_rows(keys, keys_t)
    dk[...] = jnp.zeros_like(dk)
    dv[...] = jnp.zeros_like(dv)
    own = rank * chunk + lax.broadcasted_iota(jnp.int32, (1, block), 1) % chunk
    limit = jnp.minimum(own, length - 1)
    live = rank * chunk + lax.broadcasted_iota(jnp.int32, (chunk, head), 0) < length
    for first in range(0, width // head, per_block):
        spans = [slice((first + i) * head, (first + i + 1) * head) for i in range(per_block)]
        queries = jnp.concatenate([q_ref[0, :, s] for s in spans], 0)
        upstream = jnp.concatenate(
            [jnp.where(live, up_ref[0, :, s].astype(F32), 0.0).astype(BF) for s in spans], 0
        )
        scores = masked_scores(keys[...], queries, limit)
        weights = jnp.exp(scores - jnp.max(scores, 0, keepdims=True))
        probs = weights * (1.0 / jnp.sum(weights, 0, keepdims=True))
        product = probs * dot_nt(values[...], upstream)
        d_scores = (product - probs * jnp.sum(product, 0, keepdims=True)).astype(BF)
        d_queries = dot_nn(keys_t[...], d_scores).T.astype(BF)
        for i, s in enumerate(spans):
            dq_ref[0, :, s] = d_queries[i * chunk : (i + 1) * chunk]
        dk[...] += dot_nn(d_scores, queries)
        dv[...] += dot_nn(probs.astype(BF), upstream)
    for place in range(count):
        rows = slice(place * chunk, (place + 1) * chunk)
        dkv_ref[place ^ key, 0, :, :head] = dk[rows, :]
        dkv_ref[place ^ key, 0, :, head:] = dv[rows, :]


def attend_second(queries, upstream, key_values, lengths, key, head):
    seqs, chunk, width = queries.shape
    count = key_values.shape[0]
    total = count * chunk
    whole = lambda s, *_: (0, s, 0, 0)
    local = pl.BlockSpec((1, chunk, width), lambda s, *_: (s, 0, 0))
    return pl.pallas_call(
        second_kernel,
        grid_spec=pltpu.PrefetchScalarGridSpec(
            num_scalar_prefetch=2,
            grid=(seqs,),
            in_specs=[local, local, pl.BlockSpec((count, 1, chunk, 2 * head), whole)],
            out_specs=[local, pl.BlockSpec((count, 1, chunk, 2 * head), whole)],
            scratch_shapes=[
                pltpu.VMEM((total, head), BF),
                pltpu.VMEM((total, head), BF),
                pltpu.VMEM((head, total), BF),
                pltpu.VMEM((total, head), F32),
                pltpu.VMEM((total, head), F32),
            ],
        ),
        out_shape=[
            jax.ShapeDtypeStruct(queries.shape, BF),
            jax.ShapeDtypeStruct(key_values.shape, F32),
        ],
        compiler_params=pltpu.CompilerParams(vmem_limit_bytes=VMEM_BYTES),
        cost_estimate=LIGHT,
    )(lengths, key, queries, upstream, key_values)


def backward_kernel(
    lengths_ref,
    key_ref,
    q_ref,
    up_ref,
    attn_ref,
    kv_ref,
    lse_ref,
    more_ref,
    cos_ref,
    sin_ref,
    grads_ref,
    keys,
    values,
    keys_t,
    dk,
    dv,
):
    count, _, chunk, width = q_ref.shape
    head = keys.shape[1]
    total = keys.shape[0]
    block = min(QUERY_ROWS, total)
    per_block = block // chunk
    key = key_ref[0]
    length = lengths_ref[pl.program_id(0)]
    scale = 1.0 / math.sqrt(head)
    load_keys(key, kv_ref, keys, count, head, 0)
    load_keys(key, kv_ref, values, count, head, 1)
    transpose_rows(keys, keys_t)
    for place in range(count):
        rows = slice(place * chunk, (place + 1) * chunk)
        dk[rows, :] = more_ref[place ^ key, 0, :, :head]
        dv[rows, :] = more_ref[place ^ key, 0, :, head:]
    for start in range(0, total, block):
        limit_row = start + lax.broadcasted_iota(jnp.int32, (1, block), 1)
        limit = jnp.minimum(limit_row, length - 1)
        seen = start + block
        places = [(start // chunk + i) ^ key for i in range(per_block)]
        for h in range(width // head):
            columns = slice(h * head, (h + 1) * head)
            queries = jnp.concatenate([q_ref[p, 0, :, columns] for p in places], 0)
            upstream = jnp.concatenate([up_ref[p, 0, :, columns] for p in places], 0)
            attn = jnp.concatenate([attn_ref[p, 0, :, columns] for p in places], 0)
            centre = jnp.sum((upstream.astype(F32) * attn.astype(F32)).T, 0, keepdims=True)
            scores = masked_scores(keys[:seen, :], queries, limit)
            probs = jnp.exp(scores - lse_ref[0, h : h + 1, start : start + block])
            d_probs = dot_nt(values[:seen, :], upstream)
            d_scores = (probs * (d_probs - centre)).astype(BF)
            d_queries = dot_nn(keys_t[:, :seen], d_scores).T.astype(BF).astype(F32) * scale
            span = slice(start, start + block)
            d_queries = (
                d_queries * cos_ref[span, :]
                - pltpu.roll(d_queries, head // 2, 1) * sin_ref[span, :]
            ).astype(BF)
            for i, p in enumerate(places):
                grads_ref[p, 0, :, columns] = d_queries[i * chunk : (i + 1) * chunk]
            dk[:seen, :] += dot_nn(d_scores, queries)
            dv[:seen, :] += dot_nn(probs.astype(BF), upstream)
    for place in range(count):
        rows = slice(place * chunk, (place + 1) * chunk)
        turned = dk[rows, :] * cos_ref[rows, :] - pltpu.roll(dk[rows, :], head // 2, 1) * sin_ref[rows, :]
        grads_ref[place ^ key, 0, :, width : width + head] = turned.astype(BF)
        grads_ref[place ^ key, 0, :, width + head :] = dv[rows, :].astype(BF)


def attend_backward(queries, upstream, attn, key_values, lse, more, tables, lengths, key, head):
    count, seqs, chunk, width = queries.shape
    total = count * chunk
    heads = width // head
    whole = lambda s, *_: (0, s, 0, 0)
    by_head = pl.BlockSpec((count, 1, chunk, width), whole)
    shared = pl.BlockSpec((count, 1, chunk, 2 * head), whole)
    return pl.pallas_call(
        backward_kernel,
        grid_spec=pltpu.PrefetchScalarGridSpec(
            num_scalar_prefetch=2,
            grid=(seqs,),
            in_specs=[
                by_head,
                by_head,
                by_head,
                shared,
                pl.BlockSpec((1, heads, total), lambda s, *_: (s, 0, 0)),
                shared,
                pl.BlockSpec((total, head), lambda s, *_: (0, 0)),
                pl.BlockSpec((total, head), lambda s, *_: (0, 0)),
            ],
            out_specs=pl.BlockSpec((count, 1, chunk, width + 2 * head), whole),
            scratch_shapes=[
                pltpu.VMEM((total, head), BF),
                pltpu.VMEM((total, head), BF),
                pltpu.VMEM((head, total), BF),
                pltpu.VMEM((total, head), F32),
                pltpu.VMEM((total, head), F32),
            ],
        ),
        out_shape=jax.ShapeDtypeStruct((count, seqs, chunk, width + 2 * head), BF),
        compiler_params=pltpu.CompilerParams(vmem_limit_bytes=VMEM_BYTES),
        cost_estimate=LIGHT,
    )(lengths, key, queries, upstream, attn, key_values, lse, more, *tables)


def front_kernel(key_ref, a_ref, b_ref, gain_ref, wq_ref, wkv_ref, cos_ref, sin_ref, *rest, first):
    na_ref, nb_ref, q_ref, kv_ref = rest[-4:]
    _, seqs, chunk, width = q_ref.shape
    head = kv_ref.shape[3] // 2
    scale = 1.0 / math.sqrt(head)
    for i, piece in enumerate((a_ref, b_ref)):
        inputs = piece[...].astype(F32)
        normed = (
            inputs
            * lax.rsqrt(jnp.mean(inputs * inputs, -1, keepdims=True) + EPSILON)
            * gain_ref[...]
        ).astype(BF)
        (na_ref, nb_ref)[i][...] = normed
        q_linear = dot_nn(normed, wq_ref[...])
        kv_linear = dot_nn(normed, wkv_ref[...])
        span = pl.ds(pl.multiple_of(((first + i) ^ key_ref[0]) * chunk, chunk), chunk)
        cosine, sine = cos_ref[span, :], sin_ref[span, :]
        turn = lambda v: v * cosine + pltpu.roll(v, head // 2, 1) * sine
        for s in range(seqs):
            rows = slice(s * chunk, (s + 1) * chunk)
            for h in range(width // head):
                columns = slice(h * head, (h + 1) * head)
                q_ref[i, s, :, columns] = (turn(q_linear[rows, columns]) * scale).astype(BF)
            kv_ref[i, s, :, :head] = turn(kv_linear[rows, :head]).astype(BF)
            kv_ref[i, s, :, head:] = kv_linear[rows, head:].astype(BF)


def whole_spec(array):
    return pl.BlockSpec(array.shape, lambda *_: (0,) * array.ndim)


def pair_spec(shape, pair):
    return pl.BlockSpec((2, *shape[1:]), lambda *_: (pair,) + (0,) * (len(shape) - 1))


def front_pair(key, pieces, pair, gain, wq, wkv, tables, seqs, count, before):
    rows, width = pieces[0].shape
    chunk = rows // seqs
    shapes = [
        (count, seqs, chunk, wq.shape[1]),
        (count, seqs, chunk, wkv.shape[1]),
    ]
    given = [*pieces, gain, wq, wkv, *tables]
    return pl.pallas_call(
        functools.partial(front_kernel, first=2 * pair),
        grid_spec=pltpu.PrefetchScalarGridSpec(
            num_scalar_prefetch=1,
            grid=(1,),
            in_specs=[whole_spec(a) for a in given] + [pl.BlockSpec(memory_space=pl.ANY)] * len(before),
            out_specs=[whole_spec(pieces[0])] * 2 + [pair_spec(shape, pair) for shape in shapes],
        ),
        out_shape=[jax.ShapeDtypeStruct((rows, width), BF)] * 2
        + [jax.ShapeDtypeStruct(shape, BF) for shape in shapes],
        input_output_aliases={1 + len(given) + i: 2 + i for i in range(len(before))},
        compiler_params=pltpu.CompilerParams(vmem_limit_bytes=VMEM_BYTES),
        cost_estimate=LIGHT,
    )(key, *given, *before)


def mlp_kernel(na_hbm, nb_hbm, ga_hbm, gb_hbm, shares_hbm, down_hbm, *rest, first):
    hidden_hbm, dgate_hbm, dup_hbm, pa_hbm, pb_hbm, oa_hbm, ob_hbm = rest[-18:-11]
    normed, branch, both, down, hidden, dgate, dup, parts, outs, in_sems, out_sems = rest[-11:]
    rows = na_hbm.shape[0]
    low, high = pl.ds(0, rows), pl.ds(rows, rows)
    lines, inner = shares_hbm.shape[0], down_hbm.shape[0]
    places = [(shares_hbm.at[i], both.at[:, i]) for i in range(lines)]
    places += [(na_hbm, normed.at[low]), (nb_hbm, normed.at[high])]
    places += [(ga_hbm, branch.at[low]), (gb_hbm, branch.at[high]), (down_hbm, down)]
    loads = [pltpu.make_async_copy(a, b, in_sems.at[i]) for i, (a, b) in enumerate(places)]
    places = []
    for stack, target in ((hidden, hidden_hbm), (dgate, dgate_hbm), (dup, dup_hbm)):
        places += [(stack.at[low], target.at[first]), (stack.at[high], target.at[first + 1])]
    places += [(outs.at[low], oa_hbm), (outs.at[high], ob_hbm)]
    places += [(parts.at[low], pa_hbm), (parts.at[high], pb_hbm)]
    stores = [pltpu.make_async_copy(a, b, out_sems.at[i]) for i, (a, b) in enumerate(places)]
    for load in loads:
        load.start()
    for load in loads[: lines + 2]:
        load.wait()
    both_cols = both[...].reshape(-1, 2 * inner)
    gate_up = dot_nn(normed[...], both_cols)
    gate_pre, up_pre = gate_up[:, :inner], gate_up[:, inner:]
    sigma = jax.nn.sigmoid(gate_pre)
    silu_gate = gate_pre * sigma
    slope = sigma * (1.0 + gate_pre * (1.0 - sigma))
    hidden[...] = (silu_gate * up_pre).astype(BF)
    stores[0].start()
    stores[1].start()
    for load in loads[lines + 2 :]:
        load.wait()
    grad_hidden = dot_nt(branch[...], down[...])
    dgate[...] = (grad_hidden * up_pre * slope).astype(BF)
    dup[...] = (grad_hidden * silu_gate).astype(BF)
    for store in stores[2:6]:
        store.start()
    outs[...] = dot_nn(hidden[...], down[...]).astype(BF)
    for store in stores[6:8]:
        store.start()
    for start, store in ((0, stores[8]), (rows, stores[9])):
        span = slice(start, start + rows)
        grads = dot_nt(jnp.concatenate([dgate[span, :], dup[span, :]], 1), both_cols)
        parts[span, :] = grads.astype(BF)
        store.start()
    for store in stores:
        store.wait()


def mlp_pair(normed, branch, pair, shares, down, count, before):
    rows, width = normed[0].shape
    inner = down.shape[0]
    lines, _, share_rows, _ = shares.shape
    given = [*normed, *branch, shares, down]
    anywhere = pl.BlockSpec(memory_space=pl.ANY)
    stacked = jax.ShapeDtypeStruct((count, rows, inner), BF)
    apart = jax.ShapeDtypeStruct((rows, width), BF)
    return pl.pallas_call(
        functools.partial(mlp_kernel, first=2 * pair),
        in_specs=[anywhere] * (6 + len(before)),
        out_specs=[anywhere] * 7,
        out_shape=[stacked] * 3 + [apart] * 4,
        scratch_shapes=[pltpu.VMEM((2 * rows, width), BF)] * 2
        + [pltpu.VMEM((count, lines, share_rows, 2 * inner), BF), pltpu.VMEM(down.shape, BF)]
        + [pltpu.VMEM((2 * rows, inner), BF)] * 3
        + [pltpu.VMEM((2 * rows, width), BF)] * 2
        + [pltpu.SemaphoreType.DMA((lines + 5,)), pltpu.SemaphoreType.DMA((10,))],
        input_output_aliases={6 + i: i for i in range(len(before))},
        compiler_params=pltpu.CompilerParams(vmem_limit_bytes=MLP_VMEM_BYTES),
        cost_estimate=LIGHT,
    )(*given, *before)


def proj_kernel(a_ref, b_ref, w_ref, attn_ref, *rest, last):
    dattn_ref, total_ref = rest[-2:]
    seqs, chunk = attn_ref.shape[1:3]
    total = None if len(rest) == 2 else rest[1][...]
    for i, piece in enumerate((a_ref, b_ref)):
        grads = piece[...]
        d_attn = dot_nt(grads, w_ref[...]).astype(BF)
        for s in range(seqs):
            rows = slice(s * chunk, (s + 1) * chunk)
            dattn_ref[i, s] = d_attn[rows]
            share = dot_tn(attn_ref[i, s], grads[rows])
            total = share if total is None else total + share
    total_ref[...] = total.astype(total_ref.dtype)


def proj_pair(pieces, pair, w_out, attn, count, before):
    last = 2 * pair + 2 == count
    rows, width = pieces[0].shape
    given = [*pieces, w_out]
    extra_specs = []
    aliases = {}
    if before:
        extra_specs = [pl.BlockSpec(memory_space=pl.ANY), whole_spec(before[1])]
        aliases = {4: 0} if last else {4: 0, 5: 1}
    total = jax.ShapeDtypeStruct(w_out.shape, BF if last else F32)
    return pl.pallas_call(
        functools.partial(proj_kernel, last=last),
        grid=(1,),
        in_specs=[whole_spec(a) for a in given] + [pair_spec(attn.shape, pair)] + extra_specs,
        out_specs=[pair_spec(attn.shape, pair), whole_spec(total)],
        out_shape=[jax.ShapeDtypeStruct(attn.shape, BF), total],
        input_output_aliases=aliases,
        compiler_params=pltpu.CompilerParams(vmem_limit_bytes=VMEM_BYTES),
        cost_estimate=LIGHT,
    )(*given, attn, *before)


def parts_kernel(*refs, count, turned):
    lefts, weights = refs[: len(turned)], refs[len(turned) : 2 * len(turned)]
    outs, (buffer, sems) = refs[2 * len(turned) : -2], refs[-2:]
    order = (6, 7, 2, 3, 4, 5, 0, 1) if count == 8 else range(count)
    stores = []
    for j in order:
        total = None
        for left, weight, turn in zip(lefts, weights, turned):
            share = (dot_nt if turn else dot_nn)(left[j], weight[...])
            total = share if total is None else total + share
        buffer[j] = total.astype(BF)
        stores.append(pltpu.make_async_copy(buffer.at[j], outs[j], sems.at[j]))
        stores[-1].start()
    for store in stores:
        store.wait()


def parts_of(lefts, weights, turned):
    count, rows = lefts[0].shape[:2]
    width = weights[0].shape[0 if turned[0] else 1]
    return pl.pallas_call(
        functools.partial(parts_kernel, count=count, turned=turned),
        grid=(1,),
        in_specs=[whole_spec(a) for a in (*lefts, *weights)],
        out_specs=[pl.BlockSpec(memory_space=pl.ANY)] * count,
        out_shape=[jax.ShapeDtypeStruct((rows, width), BF)] * count,
        scratch_shapes=[
            pltpu.VMEM((count, rows, width), BF),
            pltpu.SemaphoreType.DMA((count,)),
        ],
        compiler_params=pltpu.CompilerParams(vmem_limit_bytes=VMEM_BYTES),
        cost_estimate=LIGHT,
    )(*lefts, *weights)


def outer_kernel(*refs, count, rights):
    left = jnp.concatenate([ref[...] for ref in refs[:count]], 0)
    left_t = left.T
    for right, out in zip(refs[count : count + rights], refs[count + rights :]):
        out[...] = dot_nn(left_t, right[...]).astype(BF)


def outer_of(pieces, rights):
    count = len(pieces)
    rows, width = pieces[0].shape
    step = min(256, width)
    return pl.pallas_call(
        functools.partial(outer_kernel, count=count, rights=len(rights)),
        grid=(width // step,),
        in_specs=[pl.BlockSpec((rows, step), lambda i: (0, i))] * count
        + [pl.BlockSpec(right.shape, lambda i: (0, 0)) for right in rights],
        out_specs=[pl.BlockSpec((step, right.shape[1]), lambda i: (i, 0)) for right in rights],
        out_shape=[jax.ShapeDtypeStruct((width, right.shape[1]), BF) for right in rights],
        compiler_params=pltpu.CompilerParams(vmem_limit_bytes=VMEM_BYTES),
        cost_estimate=LIGHT,
    )(*pieces, *rights)


def inner_kernel(*refs, count, lefts):
    pieces = refs[lefts : lefts + count]
    outs, lefts_t = refs[lefts + count : 2 * lefts + count], refs[2 * lefts + count :]
    rows = pieces[0].shape[0]

    @pl.when(pl.program_id(0) == 0)
    def _():
        for left, left_t in zip(refs[:lefts], lefts_t):
            for j in range(count):
                span = slice(j * rows, (j + 1) * rows)
                left_t[:, span] = left[span, :].T

    right = jnp.concatenate([piece[...] for piece in pieces], 0)
    for out, left_t in zip(outs, lefts_t):
        out[...] = dot_nn(left_t[...], right).astype(BF)


def inner_of(lefts, pieces):
    count = len(pieces)
    rows, width = pieces[0].shape
    step = min(256, width)
    columns = lefts[0].shape[1]
    return pl.pallas_call(
        functools.partial(inner_kernel, count=count, lefts=len(lefts)),
        grid=(width // step,),
        in_specs=[pl.BlockSpec(left.shape, lambda i: (0, 0)) for left in lefts]
        + [pl.BlockSpec((rows, step), lambda i: (0, i))] * count,
        out_specs=[pl.BlockSpec((columns, step), lambda i: (0, i))] * len(lefts),
        out_shape=[jax.ShapeDtypeStruct((columns, width), BF)] * len(lefts),
        scratch_shapes=[pltpu.VMEM((columns, count * rows), BF)] * len(lefts),
        compiler_params=pltpu.CompilerParams(vmem_limit_bytes=VMEM_BYTES),
        cost_estimate=LIGHT,
    )(*lefts, *pieces)


def turn_kernel(place_ref, *refs, lines):
    options = len(refs) // lines
    out_ref = refs[-1]
    place = place_ref[0]
    blocks = []
    for m in range(lines):
        blocks.append(choose([ref[...] for ref in refs[m * options : (m + 1) * options]], place))
    turned = []
    for j in range(blocks[0].shape[0]):
        turned.append(jnp.concatenate([block[j].astype(F32) for block in blocks], 0).T)
    out_ref[...] = jnp.concatenate(turned, 1)


def turn_blocks(gathered):
    lines = len(gathered)
    count, columns, rows = gathered[0][0].shape
    step = min(128, rows)
    given = [option for options in gathered for option in options]
    place = lax.axis_index("dp").astype(jnp.int32).reshape(1)
    return pl.pallas_call(
        functools.partial(turn_kernel, lines=lines),
        grid_spec=pltpu.PrefetchScalarGridSpec(
            num_scalar_prefetch=1,
            grid=(rows // step,),
            in_specs=[pl.BlockSpec((count, columns, step), lambda i, *_: (0, 0, i))] * len(given),
            out_specs=pl.BlockSpec((step, count * lines * columns), lambda i, *_: (i, 0)),
        ),
        out_shape=jax.ShapeDtypeStruct((rows, count * lines * columns), F32),
        compiler_params=pltpu.CompilerParams(vmem_limit_bytes=VMEM_BYTES),
        cost_estimate=LIGHT,
    )(place, *given)


def spread_rows(share_t, count):
    columns, rows = share_t.shape
    blocks = share_t.reshape(columns, count, rows // count).transpose(1, 0, 2)
    return lax.all_to_all(blocks, "seq", split_axis=0, concat_axis=0, tiled=True)


def pack_kernel(place_ref, gate_ref, up_ref, query_ref, out_ref):
    count, rows, _ = out_ref.shape
    inner = gate_ref.shape[1] // count
    own = query_ref.shape[1] // count
    gate, up = gate_ref[...], up_ref[...]
    for j in range(count):
        columns = slice(j * inner, (j + 1) * inner)
        out_ref[j, :, : 2 * inner] = jnp.concatenate([gate[:, columns], up[:, columns]], 1)
        for g in range(query_ref.shape[0] // rows):
            start = 2 * inner + g * own
            out_ref[j, :, start : start + own] = query_ref[
                g * rows : (g + 1) * rows, j * own : (j + 1) * own
            ]


def pack_weights(w_gate, w_up, w_query, count):
    lines = lax.axis_size("dp")
    rows, columns = w_gate.shape[0] // lines, w_gate.shape[1]
    place = lax.axis_index("dp").astype(jnp.int32).reshape(1)
    share = pl.BlockSpec((rows, columns), lambda i, place: (place[0], 0))
    shape = (count, rows, (2 * columns + lines * w_query.shape[1]) // count)
    return pl.pallas_call(
        pack_kernel,
        grid_spec=pltpu.PrefetchScalarGridSpec(
            num_scalar_prefetch=1,
            grid=(1,),
            in_specs=[share, share, whole_spec(w_query)],
            out_specs=pl.BlockSpec(shape, lambda i, place: (0, 0, 0)),
        ),
        out_shape=jax.ShapeDtypeStruct(shape, BF),
        compiler_params=pltpu.CompilerParams(vmem_limit_bytes=VMEM_BYTES),
        cost_estimate=LIGHT,
    )(place, w_gate, w_up, w_query)


def share_weights(w_gate, w_up, w_query, count):
    lines = lax.axis_size("dp")
    inner = w_gate.shape[1] // count
    own = w_query.shape[1] // count
    packed = pack_weights(w_gate, w_up, w_query, count)
    packed = lax.all_to_all(packed, "seq", split_axis=0, concat_axis=0, tiled=True)
    rows = packed.shape[1]
    query = packed[:, :, 2 * inner :].reshape(count, rows, lines, own).transpose(0, 2, 1, 3)
    shares = lax.all_gather(packed[:, :, : 2 * inner], "dp", axis=0, tiled=False)
    return query.reshape(count * lines * rows, own), shares


def rope_tables(positions, head_width):
    half_width = head_width // 2
    spacing = jnp.exp(
        jnp.arange(half_width).astype(F32) * (-2.0 * math.log(10000.0) / head_width)
    )
    angles = positions.astype(F32)[:, None] * spacing[None, :]
    sines = jnp.sin(angles)
    cosines = jnp.cos(angles)
    return (jnp.concatenate([cosines, cosines], 1), jnp.concatenate([-sines, sines], 1))


def rms_scale(values_in):
    return lax.rsqrt(jnp.mean(values_in * values_in, -1, keepdims=True) + EPSILON)


def norm_back(grad_normed, inputs, scale_rows, gain):
    weighted = grad_normed * gain
    cubed = scale_rows * scale_rows * scale_rows
    return scale_rows * weighted - inputs * cubed * jnp.mean(weighted * inputs, -1, keepdims=True)


def body(
    tokens,
    lengths,
    second_queries,
    cotangent,
    second_cotangent,
    gain_attn,
    w_query,
    w_key,
    w_value,
    w_out,
    gain_mlp,
    w_gate,
    w_up,
    w_down,
):
    count = lax.axis_size("seq")
    rank = lax.axis_index("seq")
    key = order_key(count)
    keys_of = jnp.stack([key, rank]).astype(jnp.int32)
    seqs, chunk, width = tokens.shape
    head = w_key.shape[1]
    rows = seqs * chunk
    all_rows = count * rows
    own_columns = w_query.shape[0]

    query_cols, shares = share_weights(w_gate, w_up, w_query, count)
    gain_rows = jnp.zeros((16, 2 * head), BF)
    gain_rows = gain_rows.at[:2, :own_columns].set(jnp.stack([gain_attn, gain_mlp]))
    packed = jnp.concatenate([jnp.concatenate([w_key, w_value], 1), gain_rows], 0)
    packed = gather_ordered(packed, count)
    kv_mat = packed[:, :own_columns].reshape(width, 2 * head)
    gain_one = packed[:, own_columns, :own_columns].reshape(1, width).astype(F32)
    gain_two = packed[:, own_columns + 1, :own_columns].reshape(1, width).astype(F32)

    local_pos = rank * chunk + jnp.arange(chunk, dtype=jnp.int32)
    valid = (local_pos[None, :] < lengths[:, None]).astype(F32).reshape(rows, 1)
    tables = rope_tables(jnp.arange(count * chunk, dtype=jnp.int32), head)

    last_pair = count // 2 - 1
    inputs = tokens.reshape(rows, width)
    front_of = lambda pair, two, before: front_pair(
        keys_of, two, pair, gain_one, query_cols, kv_mat, tables, seqs, count, before
    )
    near = gather_near(inputs, count)
    normed_one = []
    stacks = []
    far = gather_far(near, count)
    for pair in range(last_pair):
        *normed, queries, key_values = front_of(pair, near[2 * pair : 2 * pair + 2], stacks)
        normed_one += normed
        stacks = [queries, key_values]
    last = gather_last(near, far, count)
    grad_out = cotangent.reshape(rows, width).astype(F32) * valid
    branch_near = gather_near(after(grad_out.astype(BF), far), count, stacks)
    branch_far = gather_far(after(branch_near, stacks), count)
    *normed, queries, key_values = front_of(last_pair, [far, last], stacks)
    normed_one += normed
    attn, lse = attend_forward(queries, key_values, lengths, keys_of, head)
    attn, branch_far = lax.optimization_barrier((attn, branch_far))
    proj_parts = parts_of([attn.reshape(count, rows, -1)], [w_out], (False,))
    inputs_f = inputs.astype(F32)
    scale_one = rms_scale(inputs_f)

    branch_last = gather_last(branch_near, branch_far, count)
    branch = (branch_near if is_cube(count) else branch_near[:-2]) + [branch_far, branch_last]
    grad_second, dkv_second = attend_second(
        after(second_queries, proj_parts), second_cotangent, key_values, lengths, keys_of, head
    )
    proj_sum = scatter_pieces(proj_parts, count, dkv_second)
    proj_sum, shares = lax.optimization_barrier((proj_sum, shares))
    middle = inputs_f + proj_sum.astype(F32)

    scale_two = rms_scale(middle)
    mlp_of = lambda pair, two, before: mlp_pair(
        two, branch[2 * pair : 2 * pair + 2], pair, shares, w_down, count, before
    )
    near = gather_near((middle * scale_two * gain_two).astype(BF), count)
    done = [mlp_of(0, near[:2], [])]
    far = gather_far(after(near, done[-1][0]), count)
    for pair in range(1, last_pair):
        done.append(mlp_of(pair, near[2 * pair : 2 * pair + 2], done[-1][:3]))
        if pair == 1:
            far = after(far, done[-1][0])
            last = gather_last(near, far, count)
    done.append(mlp_of(last_pair, [far, last], done[-1][:3]))
    hidden, grad_gate, grad_up = [stack.reshape(all_rows, -1) for stack in done[-1][:3]]
    normed_parts = [part for step in done for part in step[3:5]]
    out_parts = [part for step in done for part in step[5:]]
    normed_two = (near if is_cube(count) else near[:-2]) + [far, last]
    sync = lax.optimization_barrier
    always = lengths[0] > 0
    w_gate_share, w_up_share = inner_of([grad_gate, grad_up], normed_two)
    split = queries.shape[-1]
    gate_share = line_share(w_gate_share)

    def sum_mlp_back(normed_parts, hidden, w_up_share):
        two_sums = scatter_far(normed_parts, count)
        (w_down_share,) = inner_of([hidden], branch)
        grad_normed_two = scatter_near(two_sums, count, w_down_share).astype(F32)
        grad_middle = grad_out + norm_back(grad_normed_two, middle, scale_two, gain_two)
        gain_share = jnp.sum(grad_normed_two * (middle * scale_two), 0)
        return grad_middle, gain_share, w_down_share, w_up_share

    grad_middle, gain_share, w_down_share, w_up_share = stage(
        always, sum_mlp_back, normed_parts, hidden, w_up_share
    )
    w_up_share, gate_share = sync((w_up_share, gate_share))
    up_share = line_share(w_up_share)

    def project_back(grad_middle, gate_share, w_down_share):
        near = gather_near(grad_middle.astype(BF), count)
        gate_blocks = spread_rows(gate_share, count)
        proj_of = lambda pair, two, before: proj_pair(two, pair, w_out, attn, count, before)
        state = proj_of(0, near[:2], [])
        far = gather_far(after(near, state[0]), count)
        for pair in range(1, last_pair):
            state = proj_of(pair, near[2 * pair : 2 * pair + 2], state)
        last = gather_last(near, far, count)
        grad_attn, w_out_share = proj_of(last_pair, [far, last], state)
        return grad_attn, w_out_share, gate_blocks, w_down_share

    grad_attn, w_out_share, gate_blocks, w_down_share = stage(
        always, project_back, grad_middle, gate_share, w_down_share
    )
    w_down_share, up_share = sync((w_down_share, up_share))
    down_share = line_share(w_down_share)

    def attention_back(grad_attn, up_share, gate_blocks, out_parts, w_out_share):
        out_sums = scatter_far(out_parts, count)
        up_blocks = spread_rows(up_share, count)
        grads = attend_backward(
            queries, grad_attn, attn, key_values, lse, dkv_second, tables, lengths, keys_of, head
        )
        gate_blocks = line_gather(gate_blocks, grads)
        grads = grads.reshape(count, rows, -1)
        one_parts = parts_of(
            [grads[..., :split], grads[..., split:]], [query_cols, kv_mat], (True, True)
        )
        (w_one_share,) = outer_of(normed_one, [grads.reshape(all_rows, -1)])
        w_query_rows = columns_to_rows(after(w_one_share[:, :split], up_blocks))
        lines = lax.axis_size("dp")
        late = jnp.concatenate(
            [w.reshape(lines, -1, w.shape[1]) for w in (w_out_share, w_query_rows)], 1
        )
        return one_parts, out_sums, w_one_share, late.reshape(-1, width), gate_blocks, up_blocks

    one_parts, out_sums, w_one_share, late, gate_blocks, up_blocks = stage(
        always, attention_back, grad_attn, up_share, gate_blocks, out_parts, w_out_share
    )
    late, down_share = sync((late, down_share))
    late_share = line_share(late)

    def sum_attention_back(one_parts, out_sums, up_blocks):
        one_sums = scatter_far(one_parts, count)
        out = (middle + scatter_near(out_sums, count).astype(F32)).astype(BF)
        up_blocks = line_gather(up_blocks, one_sums)
        grad_normed_one = scatter_near(one_sums, count).astype(F32)
        grad_tokens = grad_middle + norm_back(grad_normed_one, inputs_f, scale_one, gain_one)
        gain_share = jnp.sum(grad_normed_one * (inputs_f * scale_one), 0)
        return out, grad_tokens, gain_share, up_blocks

    out, grad_tokens, first_gain_share, up_blocks = stage(
        always, sum_attention_back, one_parts, out_sums, up_blocks
    )
    late_share, down_share, up_blocks, first_gain_share = sync(
        (late_share, down_share, up_blocks, first_gain_share)
    )
    down_blocks = line_gather(down_share)
    late_blocks = line_gather(late_share)
    own_gain = gain_attn.shape[0]
    gain_shares = jnp.stack([first_gain_share, gain_share])
    gain_shares = gain_shares.astype(BF).reshape(2, count, own_gain).transpose(1, 0, 2)
    gain_shares = jnp.pad(gain_shares, ((0, 0), (0, 14), (0, 2 * head - own_gain)))
    kv_shares = w_one_share[:, split:].reshape(count, own_columns, 2 * head)
    small = small_sum(jnp.concatenate([kv_shares, gain_shares], 1), count).astype(F32)
    grad_w_kv, grad_gains = small[:own_columns], small[own_columns : own_columns + 2, :own_gain]
    grad_w_gate = turn_blocks(gate_blocks)
    grad_w_up = turn_blocks(up_blocks)
    grad_w_down = line_rows(down_blocks)
    late_rows = line_rows(late_blocks).reshape(len(late_blocks), 2, -1, width)
    w_out_sum = late_rows[:, 0].reshape(-1, width)
    grad_w_query = late_rows[:, 1].reshape(-1, width)

    return (
        out.reshape(tokens.shape),
        grad_tokens.reshape(tokens.shape),
        grad_second,
        grad_gains[0],
        grad_w_query,
        grad_w_kv[:, :head],
        grad_w_kv[:, head:],
        w_out_sum.astype(F32),
        grad_gains[1],
        grad_w_gate,
        grad_w_up,
        grad_w_down,
    )


def solution(mesh):
    return jax.shard_map(
        body,
        mesh=mesh,
        in_specs=(
            P("dp", "seq", None),
            P("dp"),
            P("dp", "seq", None),
            P("dp", "seq", None),
            P("dp", "seq", None),
            P("seq"),
            P("seq", None),
            P("seq", None),
            P("seq", None),
            P("seq", None),
            P("seq"),
            P("seq", None),
            P("seq", None),
            P("seq", None),
        ),
        out_specs=(
            P("dp", "seq", None),
            P("dp", "seq", None),
            P("dp", "seq", None),
            P("seq"),
            P("seq", None),
            P("seq", None),
            P("seq", None),
            P("seq", None),
            P("seq"),
            P("seq", None),
            P("seq", None),
            P("seq", None),
        ),
        check_vma=False,
    )
```

```python
import functools
import math

import jax
import jax.numpy as jnp
from jax import lax
from jax.experimental import pallas as pl
from jax.experimental.pallas import tpu as pltpu
from jax.sharding import PartitionSpec as P

EPSILON = 1e-05
BF = jnp.bfloat16
F32 = jnp.float32
QUERY_ROWS = 256
VMEM_BYTES = 32 * 1024 * 1024
LIGHT = pl.CostEstimate(flops=1000, bytes_accessed=1000, transcendentals=0)
MLP_VMEM_BYTES = 48 * 1024 * 1024


def dot_nn(left, right):
    return jnp.dot(left, right, preferred_element_type=F32)


def dot_nt(left, right):
    return lax.dot_general(left, right, (((1,), (1,)), ((), ())), preferred_element_type=F32)


def dot_tn(left, right):
    return lax.dot_general(left, right, (((0,), (0,)), ((), ())), preferred_element_type=F32)


def is_cube(count):
    return count == 8


def order_key(count):
    rank = lax.axis_index("seq")
    return rank if is_cube(count) else jnp.zeros_like(rank)


def swap(array, bit):
    return lax.ppermute(array, "seq", [(i, i ^ bit) for i in range(8)])


def add_rounded(*terms):
    total = terms[0].astype(F32)
    for term in terms[1:]:
        total = total + term.astype(F32)
    return total.astype(BF)


def after(value, *others):
    return lax.optimization_barrier((value, others))[0]


def gather_near(piece, count, *between):
    if not is_cube(count):
        gathered = lax.all_gather(piece, "seq", axis=0, tiled=False)
        return [gathered[j] for j in range(count)]
    from_x = swap(piece, 2)
    from_y = swap(piece, 4)
    from_core = swap(piece, 1)
    from_x, from_y = after([from_x, from_y], *between)
    return [piece, from_core, from_x, swap(from_x, 1), from_y, swap(from_y, 1)]


def far_halves(near):
    half = near[0].shape[0] // 2
    return [swap(near[2][:half], 4), swap(near[4][half:], 2)]


def gather_far(near, count, *window):
    if not is_cube(count):
        return near[-2]
    return jnp.concatenate(after(far_halves(near), *window), 0)


def gather_last(near, far, count):
    return swap(far, 1) if is_cube(count) else near[-1]


def gather_pieces(piece, count):
    near = gather_near(piece, count)
    far = gather_far(near, count)
    last = gather_last(near, far, count)
    return (near if is_cube(count) else near[:-2]) + [far, last]


def scatter_far(parts, count, *window):
    if not is_cube(count):
        return parts
    half = parts[0].shape[0] // 2
    far = add_rounded(parts[6], swap(parts[7], 1))
    far_x = swap(far[:half], 2)
    far_y = swap(far[half:], 4)
    far_x, far_y = after([far_x, far_y], *window)
    near_x = add_rounded(parts[2], swap(parts[3], 1))
    near_y = add_rounded(parts[4], swap(parts[5], 1))
    near_y = jnp.concatenate([add_rounded(near_y[:half], far_x), near_y[half:]], 0)
    near_x = jnp.concatenate([near_x[:half], add_rounded(near_x[half:], far_y)], 0)
    own = add_rounded(parts[0], swap(parts[1], 1))
    return [own, near_x, near_y]


def scatter_near(sums, count, *window):
    if not is_cube(count):
        return lax.psum_scatter(jnp.stack(sums), "seq", scatter_dimension=0, tiled=False)
    own, near_x, near_y = sums
    got_x = swap(near_x, 2)
    got_y = swap(near_y, 4)
    return add_rounded(after(own, *window), got_x, got_y)


def scatter_pieces(parts, count, *window):
    return scatter_near(scatter_far(parts, count), count, *window)


def gather_ordered(piece, count):
    if not is_cube(count):
        return lax.all_gather(piece, "seq", axis=0, tiled=False)
    rank = lax.axis_index("seq")
    held = piece
    for bit in (4, 2, 1):
        other = swap(held, bit)
        upper = (rank & bit) != 0
        held = jnp.stack([jnp.where(upper, other, held), jnp.where(upper, held, other)])
    held = held.transpose(2, 1, 0, *range(3, held.ndim))
    return held.reshape(count, *piece.shape)


def rows_to_columns(weight):
    return lax.all_to_all(weight, "seq", split_axis=1, concat_axis=0, tiled=True)


def columns_to_rows(weight):
    return lax.all_to_all(weight, "seq", split_axis=0, concat_axis=1, tiled=True)


def stage(always, work, *operands):
    shapes = jax.eval_shape(work, *operands)
    empty = lambda *_: jax.tree.map(lambda leaf: jnp.zeros(leaf.shape, leaf.dtype), shapes)
    return lax.cond(always, work, empty, *operands)


def small_scatter(share, count):
    if not is_cube(count):
        return lax.psum_scatter(share, "seq", scatter_dimension=0, tiled=False)
    rank = lax.axis_index("seq")
    for bit in (1, 2, 4):
        upper = (rank & bit) != 0
        pairs = share.reshape(-1, 2, *share.shape[1:])
        low, high = pairs[:, 0], pairs[:, 1]
        share = add_rounded(jnp.where(upper, high, low), swap(jnp.where(upper, low, high), bit))
    return share[0]


def load_keys(key_ref, kv_ref, rows_ref, count, head, column):
    chunk = kv_ref.shape[2]
    for place in range(count):
        rows_ref[place * chunk : (place + 1) * chunk, :] = kv_ref[
            place ^ key_ref, 0, :, column * head : (column + 1) * head
        ]


def transpose_rows(rows_ref, turned_ref):
    step = 128
    for start in range(0, rows_ref.shape[0], step):
        turned_ref[:, start : start + step] = (
            rows_ref[start : start + step, :].astype(F32).T.astype(BF)
        )


def masked_scores(keys, queries, limit):
    scores = dot_nt(keys, queries)
    key_pos = lax.broadcasted_iota(jnp.int32, scores.shape, 0)
    return jnp.where(key_pos <= limit, scores, -jnp.inf)


def forward_kernel(
    lengths_ref, key_ref, q_ref, kv_ref, attn_ref, lse_ref, keys, values, values_t
):
    count, _, chunk, _ = q_ref.shape
    head = keys.shape[1]
    total = keys.shape[0]
    block = min(QUERY_ROWS, total)
    per_block = block // chunk
    key = key_ref[0]
    length = lengths_ref[pl.program_id(0)]
    load_keys(key, kv_ref, keys, count, head, 0)
    load_keys(key, kv_ref, values, count, head, 1)
    transpose_rows(values, values_t)
    for start in range(0, total, block):
        limit_row = start + lax.broadcasted_iota(jnp.int32, (1, block), 1)
        limit = jnp.minimum(limit_row, length - 1)
        seen = start + block
        places = [(start // chunk + i) ^ key for i in range(per_block)]
        for h in range(q_ref.shape[3] // head):
            columns = slice(h * head, (h + 1) * head)
            queries = jnp.concatenate([q_ref[p, 0, :, columns] for p in places], 0)
            scores = masked_scores(keys[:seen, :], queries, limit)
            top = jnp.max(scores, 0, keepdims=True)
            weights = jnp.exp(scores - top)
            norm = jnp.sum(weights, 0, keepdims=True)
            mixed = dot_nn(values_t[:, :seen], weights.astype(BF)) / norm
            rows = mixed.T.astype(BF)
            for i, p in enumerate(places):
                attn_ref[p, 0, :, columns] = rows[i * chunk : (i + 1) * chunk]
            lse_ref[0, h : h + 1, start : start + block] = top + jnp.log(norm)


def attend_forward(queries, key_values, lengths, key, head):
    count, seqs, chunk, width = queries.shape
    total = count * chunk
    heads = width // head
    whole = lambda s, *_: (0, s, 0, 0)
    return pl.pallas_call(
        forward_kernel,
        grid_spec=pltpu.PrefetchScalarGridSpec(
            num_scalar_prefetch=2,
            grid=(seqs,),
            in_specs=[
                pl.BlockSpec((count, 1, chunk, width), whole),
                pl.BlockSpec((count, 1, chunk, 2 * head), whole),
            ],
            out_specs=[
                pl.BlockSpec((count, 1, chunk, width), whole),
                pl.BlockSpec((1, heads, total), lambda s, *_: (s, 0, 0)),
            ],
            scratch_shapes=[
                pltpu.VMEM((total, head), BF),
                pltpu.VMEM((total, head), BF),
                pltpu.VMEM((head, total), BF),
            ],
        ),
        out_shape=[
            jax.ShapeDtypeStruct(queries.shape, BF),
            jax.ShapeDtypeStruct((seqs, heads, total), F32),
        ],
        compiler_params=pltpu.CompilerParams(vmem_limit_bytes=VMEM_BYTES),
        cost_estimate=LIGHT,
    )(lengths, key, queries, key_values)


def second_kernel(
    lengths_ref, key_ref, q_ref, up_ref, kv_ref, dq_ref, dkv_ref, keys, values, keys_t, dk, dv
):
    _, chunk, width = q_ref.shape
    count = kv_ref.shape[0]
    head = keys.shape[1]
    total = keys.shape[0]
    block = min(QUERY_ROWS, total)
    per_block = block // chunk
    key = key_ref[0]
    rank = key_ref[1]
    length = lengths_ref[pl.program_id(0)]
    load_keys(key, kv_ref, keys, count, head, 0)
    load_keys(key, kv_ref, values, count, head, 1)
    transpose_rows(keys, keys_t)
    dk[...] = jnp.zeros_like(dk)
    dv[...] = jnp.zeros_like(dv)
    own = rank * chunk + lax.broadcasted_iota(jnp.int32, (1, block), 1) % chunk
    limit = jnp.minimum(own, length - 1)
    live = rank * chunk + lax.broadcasted_iota(jnp.int32, (chunk, head), 0) < length
    for first in range(0, width // head, per_block):
        spans = [slice((first + i) * head, (first + i + 1) * head) for i in range(per_block)]
        queries = jnp.concatenate([q_ref[0, :, s] for s in spans], 0)
        upstream = jnp.concatenate(
            [jnp.where(live, up_ref[0, :, s].astype(F32), 0.0).astype(BF) for s in spans], 0
        )
        scores = masked_scores(keys[...], queries, limit)
        weights = jnp.exp(scores - jnp.max(scores, 0, keepdims=True))
        probs = weights * (1.0 / jnp.sum(weights, 0, keepdims=True))
        product = probs * dot_nt(values[...], upstream)
        d_scores = (product - probs * jnp.sum(product, 0, keepdims=True)).astype(BF)
        d_queries = dot_nn(keys_t[...], d_scores).T.astype(BF)
        for i, s in enumerate(spans):
            dq_ref[0, :, s] = d_queries[i * chunk : (i + 1) * chunk]
        dk[...] += dot_nn(d_scores, queries)
        dv[...] += dot_nn(probs.astype(BF), upstream)
    for place in range(count):
        rows = slice(place * chunk, (place + 1) * chunk)
        dkv_ref[place ^ key, 0, :, :head] = dk[rows, :]
        dkv_ref[place ^ key, 0, :, head:] = dv[rows, :]


def attend_second(queries, upstream, key_values, lengths, key, head):
    seqs, chunk, width = queries.shape
    count = key_values.shape[0]
    total = count * chunk
    whole = lambda s, *_: (0, s, 0, 0)
    local = pl.BlockSpec((1, chunk, width), lambda s, *_: (s, 0, 0))
    return pl.pallas_call(
        second_kernel,
        grid_spec=pltpu.PrefetchScalarGridSpec(
            num_scalar_prefetch=2,
            grid=(seqs,),
            in_specs=[local, local, pl.BlockSpec((count, 1, chunk, 2 * head), whole)],
            out_specs=[local, pl.BlockSpec((count, 1, chunk, 2 * head), whole)],
            scratch_shapes=[
                pltpu.VMEM((total, head), BF),
                pltpu.VMEM((total, head), BF),
                pltpu.VMEM((head, total), BF),
                pltpu.VMEM((total, head), F32),
                pltpu.VMEM((total, head), F32),
            ],
        ),
        out_shape=[
            jax.ShapeDtypeStruct(queries.shape, BF),
            jax.ShapeDtypeStruct(key_values.shape, F32),
        ],
        compiler_params=pltpu.CompilerParams(vmem_limit_bytes=VMEM_BYTES),
        cost_estimate=LIGHT,
    )(lengths, key, queries, upstream, key_values)


def backward_kernel(
    lengths_ref,
    key_ref,
    q_ref,
    up_ref,
    attn_ref,
    kv_ref,
    lse_ref,
    more_ref,
    cos_ref,
    sin_ref,
    grads_ref,
    keys,
    values,
    keys_t,
    dk,
    dv,
):
    count, _, chunk, width = q_ref.shape
    head = keys.shape[1]
    total = keys.shape[0]
    block = min(QUERY_ROWS, total)
    per_block = block // chunk
    key = key_ref[0]
    length = lengths_ref[pl.program_id(0)]
    scale = 1.0 / math.sqrt(head)
    load_keys(key, kv_ref, keys, count, head, 0)
    load_keys(key, kv_ref, values, count, head, 1)
    transpose_rows(keys, keys_t)
    for place in range(count):
        rows = slice(place * chunk, (place + 1) * chunk)
        dk[rows, :] = more_ref[place ^ key, 0, :, :head]
        dv[rows, :] = more_ref[place ^ key, 0, :, head:]
    for start in range(0, total, block):
        limit_row = start + lax.broadcasted_iota(jnp.int32, (1, block), 1)
        limit = jnp.minimum(limit_row, length - 1)
        seen = start + block
        places = [(start // chunk + i) ^ key for i in range(per_block)]
        for h in range(width // head):
            columns = slice(h * head, (h + 1) * head)
            queries = jnp.concatenate([q_ref[p, 0, :, columns] for p in places], 0)
            upstream = jnp.concatenate([up_ref[p, 0, :, columns] for p in places], 0)
            attn = jnp.concatenate([attn_ref[p, 0, :, columns] for p in places], 0)
            centre = jnp.sum((upstream.astype(F32) * attn.astype(F32)).T, 0, keepdims=True)
            scores = masked_scores(keys[:seen, :], queries, limit)
            probs = jnp.exp(scores - lse_ref[0, h : h + 1, start : start + block])
            d_probs = dot_nt(values[:seen, :], upstream)
            d_scores = (probs * (d_probs - centre)).astype(BF)
            d_queries = dot_nn(keys_t[:, :seen], d_scores).T.astype(BF).astype(F32) * scale
            span = slice(start, start + block)
            d_queries = (
                d_queries * cos_ref[span, :]
                - pltpu.roll(d_queries, head // 2, 1) * sin_ref[span, :]
            ).astype(BF)
            for i, p in enumerate(places):
                grads_ref[p, 0, :, columns] = d_queries[i * chunk : (i + 1) * chunk]
            dk[:seen, :] += dot_nn(d_scores, queries)
            dv[:seen, :] += dot_nn(probs.astype(BF), upstream)
    for place in range(count):
        rows = slice(place * chunk, (place + 1) * chunk)
        turned = dk[rows, :] * cos_ref[rows, :] - pltpu.roll(dk[rows, :], head // 2, 1) * sin_ref[rows, :]
        grads_ref[place ^ key, 0, :, width : width + head] = turned.astype(BF)
        grads_ref[place ^ key, 0, :, width + head :] = dv[rows, :].astype(BF)


def attend_backward(queries, upstream, attn, key_values, lse, more, tables, lengths, key, head):
    count, seqs, chunk, width = queries.shape
    total = count * chunk
    heads = width // head
    whole = lambda s, *_: (0, s, 0, 0)
    by_head = pl.BlockSpec((count, 1, chunk, width), whole)
    shared = pl.BlockSpec((count, 1, chunk, 2 * head), whole)
    return pl.pallas_call(
        backward_kernel,
        grid_spec=pltpu.PrefetchScalarGridSpec(
            num_scalar_prefetch=2,
            grid=(seqs,),
            in_specs=[
                by_head,
                by_head,
                by_head,
                shared,
                pl.BlockSpec((1, heads, total), lambda s, *_: (s, 0, 0)),
                shared,
                pl.BlockSpec((total, head), lambda s, *_: (0, 0)),
                pl.BlockSpec((total, head), lambda s, *_: (0, 0)),
            ],
            out_specs=pl.BlockSpec((count, 1, chunk, width + 2 * head), whole),
            scratch_shapes=[
                pltpu.VMEM((total, head), BF),
                pltpu.VMEM((total, head), BF),
                pltpu.VMEM((head, total), BF),
                pltpu.VMEM((total, head), F32),
                pltpu.VMEM((total, head), F32),
            ],
        ),
        out_shape=jax.ShapeDtypeStruct((count, seqs, chunk, width + 2 * head), BF),
        compiler_params=pltpu.CompilerParams(vmem_limit_bytes=VMEM_BYTES),
        cost_estimate=LIGHT,
    )(lengths, key, queries, upstream, attn, key_values, lse, more, *tables)


def front_kernel(key_ref, a_ref, b_ref, gain_ref, wq_ref, wkv_ref, cos_ref, sin_ref, *rest, first):
    na_ref, nb_ref, q_ref, kv_ref = rest[-4:]
    _, seqs, chunk, width = q_ref.shape
    head = kv_ref.shape[3] // 2
    scale = 1.0 / math.sqrt(head)
    for i, piece in enumerate((a_ref, b_ref)):
        inputs = piece[...].astype(F32)
        normed = (
            inputs
            * lax.rsqrt(jnp.mean(inputs * inputs, -1, keepdims=True) + EPSILON)
            * gain_ref[...]
        ).astype(BF)
        (na_ref, nb_ref)[i][...] = normed
        q_linear = dot_nn(normed, wq_ref[...])
        kv_linear = dot_nn(normed, wkv_ref[...])
        span = pl.ds(pl.multiple_of(((first + i) ^ key_ref[0]) * chunk, chunk), chunk)
        cosine, sine = cos_ref[span, :], sin_ref[span, :]
        turn = lambda v: v * cosine + pltpu.roll(v, head // 2, 1) * sine
        for s in range(seqs):
            rows = slice(s * chunk, (s + 1) * chunk)
            for h in range(width // head):
                columns = slice(h * head, (h + 1) * head)
                q_ref[i, s, :, columns] = (turn(q_linear[rows, columns]) * scale).astype(BF)
            kv_ref[i, s, :, :head] = turn(kv_linear[rows, :head]).astype(BF)
            kv_ref[i, s, :, head:] = kv_linear[rows, head:].astype(BF)


def whole_spec(array):
    return pl.BlockSpec(array.shape, lambda *_: (0,) * array.ndim)


def pair_spec(shape, pair):
    return pl.BlockSpec((2, *shape[1:]), lambda *_: (pair,) + (0,) * (len(shape) - 1))


def front_pair(key, pieces, pair, gain, wq, wkv, tables, seqs, count, before):
    rows, width = pieces[0].shape
    chunk = rows // seqs
    shapes = [
        (count, seqs, chunk, wq.shape[1]),
        (count, seqs, chunk, wkv.shape[1]),
    ]
    given = [*pieces, gain, wq, wkv, *tables]
    return pl.pallas_call(
        functools.partial(front_kernel, first=2 * pair),
        grid_spec=pltpu.PrefetchScalarGridSpec(
            num_scalar_prefetch=1,
            grid=(1,),
            in_specs=[whole_spec(a) for a in given] + [pl.BlockSpec(memory_space=pl.ANY)] * len(before),
            out_specs=[whole_spec(pieces[0])] * 2 + [pair_spec(shape, pair) for shape in shapes],
        ),
        out_shape=[jax.ShapeDtypeStruct((rows, width), BF)] * 2
        + [jax.ShapeDtypeStruct(shape, BF) for shape in shapes],
        input_output_aliases={1 + len(given) + i: 2 + i for i in range(len(before))},
        compiler_params=pltpu.CompilerParams(vmem_limit_bytes=VMEM_BYTES),
        cost_estimate=LIGHT,
    )(key, *given, *before)


def hidden_kernel(na_hbm, nb_hbm, ga_hbm, gb_hbm, shares_hbm, down_hbm, *rest, first):
    hidden_hbm, dgate_hbm, dup_hbm = rest[-11:-8]
    normed, branch, both, down, hidden, dgate, dup, sems = rest[-8:]
    rows = na_hbm.shape[0]
    lines, inner = shares_hbm.shape[0], down_hbm.shape[0]
    low, high = pl.ds(0, rows), pl.ds(rows, rows)
    places = [(shares_hbm.at[i], both.at[:, i]) for i in range(lines)]
    places += [(na_hbm, normed.at[low]), (nb_hbm, normed.at[high])]
    places += [(ga_hbm, branch.at[low]), (gb_hbm, branch.at[high]), (down_hbm, down)]
    loads = [pltpu.make_async_copy(a, b, sems.at[i]) for i, (a, b) in enumerate(places)]
    places = []
    for stack, target in ((hidden, hidden_hbm), (dgate, dgate_hbm), (dup, dup_hbm)):
        places += [(stack.at[low], target.at[first]), (stack.at[high], target.at[first + 1])]
    stores = [
        pltpu.make_async_copy(a, b, sems.at[len(loads) + i]) for i, (a, b) in enumerate(places)
    ]
    for load in loads:
        load.start()
    for load in loads[: lines + 2]:
        load.wait()
    gate_up = dot_nn(normed[...], both[...].reshape(-1, 2 * inner))
    gate_pre, up_pre = gate_up[:, :inner], gate_up[:, inner:]
    sigma = jax.nn.sigmoid(gate_pre)
    silu_gate = gate_pre * sigma
    slope = sigma * (1.0 + gate_pre * (1.0 - sigma))
    hidden[...] = (silu_gate * up_pre).astype(BF)
    for store in stores[:2]:
        store.start()
    for load in loads[lines + 2 :]:
        load.wait()
    grad_hidden = dot_nt(branch[...], down[...])
    dgate[...] = (grad_hidden * up_pre * slope).astype(BF)
    dup[...] = (grad_hidden * silu_gate).astype(BF)
    for store in stores[2:]:
        store.start()
    for store in stores:
        store.wait()


def hidden_pair(normed, branch, pair, shares, down, count, before):
    rows, width = normed[0].shape
    inner = down.shape[0]
    lines, _, share_rows, _ = shares.shape
    given = [*normed, *branch, shares, down]
    anywhere = pl.BlockSpec(memory_space=pl.ANY)
    stacked = jax.ShapeDtypeStruct((count, rows, inner), BF)
    return pl.pallas_call(
        functools.partial(hidden_kernel, first=2 * pair),
        in_specs=[anywhere] * (6 + len(before)),
        out_specs=[anywhere] * 3,
        out_shape=[stacked] * 3,
        scratch_shapes=[pltpu.VMEM((2 * rows, width), BF)] * 2
        + [pltpu.VMEM((count, lines, share_rows, 2 * inner), BF), pltpu.VMEM(down.shape, BF)]
        + [pltpu.VMEM((2 * rows, inner), BF)] * 3
        + [pltpu.SemaphoreType.DMA((lines + 11,))],
        input_output_aliases={6 + i: i for i in range(len(before))},
        compiler_params=pltpu.CompilerParams(vmem_limit_bytes=MLP_VMEM_BYTES),
        cost_estimate=pl.CostEstimate(
            flops=20 * rows * width * inner,
            bytes_accessed=6 * width * inner + 12 * rows * width,
            transcendentals=2 * rows * inner,
        ),
    )(*given, *before)


def mlp_parts_kernel(hidden_hbm, dgate_hbm, dup_hbm, shares_hbm, down_hbm, *rest, first):
    pa_hbm, pb_hbm, oa_hbm, ob_hbm = rest[:4]
    hidden, dgate, dup, both, down, parts, outs, sems = rest[4:]
    rows = pa_hbm.shape[0]
    lines, inner = shares_hbm.shape[0], down_hbm.shape[0]
    low, high = pl.ds(0, rows), pl.ds(rows, rows)
    both_stacks = ((dgate_hbm, dgate), (dup_hbm, dup), (hidden_hbm, hidden))
    places = [(stack.at[pl.ds(first, 2)], target) for stack, target in both_stacks]
    places += [(shares_hbm.at[i], both.at[:, i]) for i in range(lines)]
    places += [(down_hbm, down)]
    loads = [pltpu.make_async_copy(a, b, sems.at[i]) for i, (a, b) in enumerate(places)]
    places = [(parts.at[low], pa_hbm), (parts.at[high], pb_hbm)]
    places += [(outs.at[low], oa_hbm), (outs.at[high], ob_hbm)]
    stores = [
        pltpu.make_async_copy(a, b, sems.at[len(loads) + i]) for i, (a, b) in enumerate(places)
    ]
    for load in loads:
        load.start()
    for load in loads[: lines + 3]:
        load.wait()
    both_cols = both[...].reshape(-1, 2 * inner)
    for i in range(2):
        grads = dot_nt(jnp.concatenate([dgate[i], dup[i]], 1), both_cols)
        parts[i * rows : (i + 1) * rows, :] = grads.astype(BF)
        stores[i].start()
    loads[-1].wait()
    for i in range(2):
        outs[i * rows : (i + 1) * rows, :] = dot_nn(hidden[i], down[...]).astype(BF)
        stores[2 + i].start()
    for store in stores:
        store.wait()


def mlp_parts(stacks, pair, shares, down):
    count, rows, inner = stacks[0].shape
    width = down.shape[1]
    lines, _, share_rows, _ = shares.shape
    anywhere = pl.BlockSpec(memory_space=pl.ANY)
    apart = jax.ShapeDtypeStruct((rows, width), BF)
    return pl.pallas_call(
        functools.partial(mlp_parts_kernel, first=2 * pair),
        in_specs=[anywhere] * 5,
        out_specs=[anywhere] * 4,
        out_shape=[apart] * 4,
        scratch_shapes=[pltpu.VMEM((2, rows, inner), BF)] * 3
        + [pltpu.VMEM((count, lines, share_rows, 2 * inner), BF), pltpu.VMEM(down.shape, BF)]
        + [pltpu.VMEM((2 * rows, width), BF)] * 2
        + [pltpu.SemaphoreType.DMA((lines + 8,))],
        compiler_params=pltpu.CompilerParams(vmem_limit_bytes=MLP_VMEM_BYTES),
        cost_estimate=pl.CostEstimate(
            flops=20 * rows * width * inner,
            bytes_accessed=6 * width * inner + 12 * rows * width,
            transcendentals=0,
        ),
    )(*stacks, shares, down)


def proj_kernel(a_ref, b_ref, w_ref, attn_ref, *rest, last):
    dattn_ref, total_ref = rest[-2:]
    seqs, chunk = attn_ref.shape[1:3]
    total = None if len(rest) == 2 else rest[1][...]
    for i, piece in enumerate((a_ref, b_ref)):
        grads = piece[...]
        d_attn = dot_nt(grads, w_ref[...]).astype(BF)
        for s in range(seqs):
            rows = slice(s * chunk, (s + 1) * chunk)
            dattn_ref[i, s] = d_attn[rows]
            share = dot_tn(attn_ref[i, s], grads[rows])
            total = share if total is None else total + share
    total_ref[...] = total.astype(total_ref.dtype)


def proj_pair(pieces, pair, w_out, attn, count, before):
    last = 2 * pair + 2 == count
    rows, width = pieces[0].shape
    given = [*pieces, w_out]
    extra_specs = []
    aliases = {}
    if before:
        extra_specs = [pl.BlockSpec(memory_space=pl.ANY), whole_spec(before[1])]
        aliases = {4: 0} if last else {4: 0, 5: 1}
    total = jax.ShapeDtypeStruct(w_out.shape, BF if last else F32)
    return pl.pallas_call(
        functools.partial(proj_kernel, last=last),
        grid=(1,),
        in_specs=[whole_spec(a) for a in given] + [pair_spec(attn.shape, pair)] + extra_specs,
        out_specs=[pair_spec(attn.shape, pair), whole_spec(total)],
        out_shape=[jax.ShapeDtypeStruct(attn.shape, BF), total],
        input_output_aliases=aliases,
        compiler_params=pltpu.CompilerParams(vmem_limit_bytes=VMEM_BYTES),
        cost_estimate=LIGHT,
    )(*given, attn, *before)


def parts_kernel(*refs, count, turned):
    lefts, weights = refs[: len(turned)], refs[len(turned) : 2 * len(turned)]
    outs, (buffer, sems) = refs[2 * len(turned) : -2], refs[-2:]
    order = (6, 7, 2, 3, 4, 5, 0, 1) if count == 8 else range(count)
    stores = []
    for j in order:
        total = None
        for left, weight, turn in zip(lefts, weights, turned):
            share = (dot_nt if turn else dot_nn)(left[j], weight[...])
            total = share if total is None else total + share
        buffer[j] = total.astype(BF)
        stores.append(pltpu.make_async_copy(buffer.at[j], outs[j], sems.at[j]))
        stores[-1].start()
    for store in stores:
        store.wait()


def parts_of(lefts, weights, turned):
    count, rows = lefts[0].shape[:2]
    width = weights[0].shape[0 if turned[0] else 1]
    return pl.pallas_call(
        functools.partial(parts_kernel, count=count, turned=turned),
        grid=(1,),
        in_specs=[whole_spec(a) for a in (*lefts, *weights)],
        out_specs=[pl.BlockSpec(memory_space=pl.ANY)] * count,
        out_shape=[jax.ShapeDtypeStruct((rows, width), BF)] * count,
        scratch_shapes=[
            pltpu.VMEM((count, rows, width), BF),
            pltpu.SemaphoreType.DMA((count,)),
        ],
        compiler_params=pltpu.CompilerParams(vmem_limit_bytes=VMEM_BYTES),
        cost_estimate=LIGHT,
    )(*lefts, *weights)


def outer_kernel(*refs, count, rights):
    left = jnp.concatenate([ref[...] for ref in refs[:count]], 0)
    left_t = left.T
    for right, out in zip(refs[count : count + rights], refs[count + rights :]):
        out[...] = dot_nn(left_t, right[...]).astype(BF)


def outer_of(pieces, rights):
    count = len(pieces)
    rows, width = pieces[0].shape
    step = min(256, width)
    return pl.pallas_call(
        functools.partial(outer_kernel, count=count, rights=len(rights)),
        grid=(width // step,),
        in_specs=[pl.BlockSpec((rows, step), lambda i: (0, i))] * count
        + [pl.BlockSpec(right.shape, lambda i: (0, 0)) for right in rights],
        out_specs=[pl.BlockSpec((step, right.shape[1]), lambda i: (i, 0)) for right in rights],
        out_shape=[jax.ShapeDtypeStruct((width, right.shape[1]), BF) for right in rights],
        compiler_params=pltpu.CompilerParams(vmem_limit_bytes=VMEM_BYTES),
        cost_estimate=LIGHT,
    )(*pieces, *rights)


def inner_kernel(*refs, count, lefts):
    pieces = refs[lefts : lefts + count]
    outs, lefts_t = refs[lefts + count : 2 * lefts + count], refs[2 * lefts + count :]
    rows = pieces[0].shape[0]

    @pl.when(pl.program_id(0) == 0)
    def _():
        for left, left_t in zip(refs[:lefts], lefts_t):
            for j in range(count):
                span = slice(j * rows, (j + 1) * rows)
                left_t[:, span] = left[span, :].T

    right = jnp.concatenate([piece[...] for piece in pieces], 0)
    for out, left_t in zip(outs, lefts_t):
        out[...] = dot_nn(left_t[...], right).astype(BF)


def inner_of(lefts, pieces):
    count = len(pieces)
    rows, width = pieces[0].shape
    step = min(256, width)
    columns = lefts[0].shape[1]
    return pl.pallas_call(
        functools.partial(inner_kernel, count=count, lefts=len(lefts)),
        grid=(width // step,),
        in_specs=[pl.BlockSpec(left.shape, lambda i: (0, 0)) for left in lefts]
        + [pl.BlockSpec((rows, step), lambda i: (0, i))] * count,
        out_specs=[pl.BlockSpec((columns, step), lambda i: (0, i))] * len(lefts),
        out_shape=[jax.ShapeDtypeStruct((columns, width), BF)] * len(lefts),
        scratch_shapes=[pltpu.VMEM((columns, count * rows), BF)] * len(lefts),
        compiler_params=pltpu.CompilerParams(vmem_limit_bytes=VMEM_BYTES),
        cost_estimate=LIGHT,
    )(*lefts, *pieces)


def turn_kernel(blocks_ref, out_ref):
    turned = [blocks_ref[j].astype(F32).T for j in range(blocks_ref.shape[0])]
    out_ref[...] = jnp.concatenate(turned, 1)


def turn_blocks(blocks):
    count, columns, rows = blocks.shape
    step = min(128, rows)
    return pl.pallas_call(
        turn_kernel,
        grid=(rows // step,),
        in_specs=[pl.BlockSpec((count, columns, step), lambda i: (0, 0, i))],
        out_specs=pl.BlockSpec((step, count * columns), lambda i: (i, 0)),
        out_shape=jax.ShapeDtypeStruct((rows, count * columns), F32),
        compiler_params=pltpu.CompilerParams(vmem_limit_bytes=VMEM_BYTES),
        cost_estimate=LIGHT,
    )(blocks)


def spread_rows(share_t, count):
    columns, rows = share_t.shape
    blocks = share_t.reshape(columns, count, rows // count).transpose(1, 0, 2)
    return lax.all_to_all(blocks, "seq", split_axis=0, concat_axis=0, tiled=True)


def pack_kernel(place_ref, gate_ref, up_ref, out_ref):
    count = out_ref.shape[0]
    inner = gate_ref.shape[1] // count
    gate, up = gate_ref[...], up_ref[...]
    for j in range(count):
        columns = slice(j * inner, (j + 1) * inner)
        out_ref[j] = jnp.concatenate([gate[:, columns], up[:, columns]], 1)


def pack_weights(w_gate, w_up, count):
    lines = lax.axis_size("dp")
    rows, columns = w_gate.shape[0] // lines, w_gate.shape[1]
    place = lax.axis_index("dp").astype(jnp.int32).reshape(1)
    share = pl.BlockSpec((rows, columns), lambda i, place: (place[0], 0))
    shape = (count, rows, 2 * columns // count)
    return pl.pallas_call(
        pack_kernel,
        grid_spec=pltpu.PrefetchScalarGridSpec(
            num_scalar_prefetch=1,
            grid=(1,),
            in_specs=[share, share],
            out_specs=pl.BlockSpec(shape, lambda i, place: (0, 0, 0)),
        ),
        out_shape=jax.ShapeDtypeStruct(shape, BF),
        compiler_params=pltpu.CompilerParams(vmem_limit_bytes=VMEM_BYTES),
        cost_estimate=LIGHT,
    )(place, w_gate, w_up)


def share_weights(w_gate, w_up, w_query, count):
    packed = pack_weights(w_gate, w_up, count)
    packed = lax.all_to_all(packed, "seq", split_axis=0, concat_axis=0, tiled=True)
    query = rows_to_columns(w_query + packed[0, 0, 0] * 0)
    return query, lax.all_gather(packed, "dp", axis=0, tiled=False)


def rope_tables(positions, head_width):
    half_width = head_width // 2
    spacing = jnp.exp(
        jnp.arange(half_width).astype(F32) * (-2.0 * math.log(10000.0) / head_width)
    )
    angles = positions.astype(F32)[:, None] * spacing[None, :]
    sines = jnp.sin(angles)
    cosines = jnp.cos(angles)
    return (jnp.concatenate([cosines, cosines], 1), jnp.concatenate([-sines, sines], 1))


def rms_scale(values_in):
    return lax.rsqrt(jnp.mean(values_in * values_in, -1, keepdims=True) + EPSILON)


def norm_back(grad_normed, inputs, scale_rows, gain):
    weighted = grad_normed * gain
    cubed = scale_rows * scale_rows * scale_rows
    return scale_rows * weighted - inputs * cubed * jnp.mean(weighted * inputs, -1, keepdims=True)


def body(
    tokens,
    lengths,
    second_queries,
    cotangent,
    second_cotangent,
    gain_attn,
    w_query,
    w_key,
    w_value,
    w_out,
    gain_mlp,
    w_gate,
    w_up,
    w_down,
):
    count = lax.axis_size("seq")
    rank = lax.axis_index("seq")
    key = order_key(count)
    keys_of = jnp.stack([key, rank]).astype(jnp.int32)
    seqs, chunk, width = tokens.shape
    head = w_key.shape[1]
    rows = seqs * chunk
    all_rows = count * rows
    own_columns = w_query.shape[0]

    query_cols, shares = share_weights(w_gate, w_up, w_query, count)
    gain_rows = jnp.zeros((16, 2 * head), BF)
    gain_rows = gain_rows.at[:2, :own_columns].set(jnp.stack([gain_attn, gain_mlp]))
    packed = jnp.concatenate([jnp.concatenate([w_key, w_value], 1), gain_rows], 0)
    packed = gather_ordered(packed, count)
    kv_mat = packed[:, :own_columns].reshape(width, 2 * head)
    gain_one = packed[:, own_columns, :own_columns].reshape(1, width).astype(F32)
    gain_two = packed[:, own_columns + 1, :own_columns].reshape(1, width).astype(F32)

    local_pos = rank * chunk + jnp.arange(chunk, dtype=jnp.int32)
    valid = (local_pos[None, :] < lengths[:, None]).astype(F32).reshape(rows, 1)
    tables = rope_tables(jnp.arange(count * chunk, dtype=jnp.int32), head)

    last_pair = count // 2 - 1
    inputs = tokens.reshape(rows, width)
    front_of = lambda pair, two, before: front_pair(
        keys_of, two, pair, gain_one, query_cols, kv_mat, tables, seqs, count, before
    )
    near = gather_near(inputs, count)
    normed_one = []
    stacks = []
    far = gather_far(near, count)
    for pair in range(last_pair):
        *normed, queries, key_values = front_of(pair, near[2 * pair : 2 * pair + 2], stacks)
        normed_one += normed
        stacks = [queries, key_values]
    last = gather_last(near, far, count)
    grad_out = cotangent.reshape(rows, width).astype(F32) * valid
    branch_near = gather_near(after(grad_out.astype(BF), far), count, stacks)
    *normed, queries, key_values = front_of(last_pair, [far, last], stacks)
    normed_one += normed
    attn, lse = attend_forward(queries, key_values, lengths, keys_of, head)
    attn, branch_near = lax.optimization_barrier((attn, branch_near))
    proj_parts = parts_of([attn.reshape(count, rows, -1)], [w_out], (False,))
    inputs_f = inputs.astype(F32)
    scale_one = rms_scale(inputs_f)

    grad_second, dkv_second = attend_second(
        after(second_queries, proj_parts), second_cotangent, key_values, lengths, keys_of, head
    )
    proj_sum = scatter_pieces(proj_parts, count, dkv_second)
    proj_sum, shares = lax.optimization_barrier((proj_sum, shares))
    middle = inputs_f + proj_sum.astype(F32)

    scale_two = rms_scale(middle)
    sync = lax.optimization_barrier
    always = lengths[0] > 0
    hidden_of = lambda pair, two, before: tuple(
        hidden_pair(two, branch[2 * pair : 2 * pair + 2], pair, shares, w_down, count, before)
    )
    normed_own = (middle * scale_two * gain_two).astype(BF)
    branch = list(branch_near)

    def middle_pairs(near, stacks):
        for pair in range(1, last_pair):
            stacks = hidden_of(pair, near[2 * pair : 2 * pair + 2], stacks)
        return tuple(stacks)

    if is_cube(count):
        from_x, from_y, from_core = swap(normed_own, 2), swap(normed_own, 4), swap(normed_own, 1)
        stacks = stage(always, lambda *two: hidden_of(0, two, []), normed_own, from_core)
        from_x, from_y, stacks = sync((from_x, from_y, stacks))
        near = [normed_own, from_core, from_x, swap(from_x, 1), from_y, swap(from_y, 1)]
        halves, branch_halves = far_halves(near), far_halves(after(branch_near, stacks))
        stacks = stage(always, middle_pairs, near, stacks)
        halves, branch_halves, stacks = sync((halves, branch_halves, stacks))
        far, branch_far = jnp.concatenate(halves, 0), jnp.concatenate(branch_halves, 0)
        last = swap(far, 1)
        branch += [branch_far, swap(branch_far, 1)]
    else:
        near = gather_near(normed_own, count)
        stacks = middle_pairs(near, hidden_of(0, near[:2], []))
        far, last = near[-2:]
    stacks = hidden_of(last_pair, [far, last], list(stacks))
    hidden, grad_gate, grad_up = [stack.reshape(all_rows, -1) for stack in stacks]
    normed_two = (near if is_cube(count) else near[:-2]) + [far, last]
    split = queries.shape[-1]
    (w_gate_share,) = inner_of([grad_gate], normed_two)
    gate_sum = lax.psum(w_gate_share, "dp")

    def parts_mlp(stacks, grad_up):
        (w_up_share,) = inner_of([grad_up], normed_two)
        parts = [mlp_parts(stacks, pair, shares, w_down) for pair in range(last_pair + 1)]
        normed_parts = [part for step in parts for part in step[:2]]
        return w_up_share, normed_parts, [part for step in parts for part in step[2:]]

    w_up_share, normed_parts, out_parts = stage(always, parts_mlp, stacks, grad_up)

    def scatter_mlp(normed_parts, hidden):
        return scatter_far(normed_parts, count), inner_of([hidden], branch)[0]

    two_sums, w_down_share = stage(always, scatter_mlp, normed_parts, hidden)
    def sum_mlp(two_sums):
        grad_normed_two = scatter_near(two_sums, count).astype(F32)
        grad_middle = grad_out + norm_back(grad_normed_two, middle, scale_two, gain_two)
        return grad_middle, jnp.sum(grad_normed_two * (middle * scale_two), 0)

    grad_middle, gain_share = stage(always, sum_mlp, two_sums)
    grad_middle, w_up_share, w_down_share, gate_sum = sync(
        (grad_middle, w_up_share, w_down_share, gate_sum)
    )
    up_sum, down_sum = lax.psum((w_up_share, w_down_share), "dp")
    proj_of = lambda pair, two, before: proj_pair(two, pair, w_out, attn, count, before)

    def gather_middle(grad_middle):
        near = gather_near(grad_middle.astype(BF), count)
        return near, proj_of(0, near[:2], [])

    near, state = stage(always, gather_middle, grad_middle)

    def project_back(near, state):
        far = gather_far(near, count)
        for pair in range(1, last_pair):
            state = proj_of(pair, near[2 * pair : 2 * pair + 2], state)
        last = gather_last(near, far, count)
        return proj_of(last_pair, [far, last], state)

    grad_attn, w_out_share = stage(always, project_back, near, state)
    grad_attn, gate_sum = sync((grad_attn, gate_sum))
    gate_blocks = spread_rows(gate_sum, count)

    def attention_back(grad_attn, out_parts):
        out_sums = scatter_far(out_parts, count)
        grads = attend_backward(
            queries, grad_attn, attn, key_values, lse, dkv_second, tables, lengths, keys_of, head
        )
        grads = grads.reshape(count, rows, -1)
        one_parts = parts_of(
            [grads[..., :split], grads[..., split:]], [query_cols, kv_mat], (True, True)
        )
        return out_sums, one_parts, grads

    out_sums, one_parts, grads = stage(always, attention_back, grad_attn, out_parts)
    one_parts, grads, gate_blocks = sync((one_parts, grads, gate_blocks))

    def scatter_attention(one_parts, grads):
        (w_one_share,) = outer_of(normed_one, [grads.reshape(all_rows, -1)])
        return scatter_far(one_parts, count), w_one_share

    one_sums, w_one_share = stage(always, scatter_attention, one_parts, grads)
    w_query_share = w_one_share[:, :split].reshape(count, own_columns, split)
    w_query_share = lax.all_to_all(w_query_share, "seq", split_axis=0, concat_axis=0, tiled=True)
    own_gain = gain_attn.shape[0]

    def sum_attention(one_sums, w_one_share):
        kv_shares = w_one_share[:, split:].reshape(count, own_columns, 2 * head)
        w_kv_share = small_scatter(kv_shares, count)
        grad_normed_one = scatter_near(one_sums, count).astype(F32)
        grad_tokens = grad_middle + norm_back(grad_normed_one, inputs_f, scale_one, gain_one)
        gain_shares = jnp.stack([jnp.sum(grad_normed_one * (inputs_f * scale_one), 0), gain_share])
        gain_shares = gain_shares.astype(BF).reshape(2, count, own_gain).transpose(1, 0, 2)
        gain_shares = jnp.pad(gain_shares, ((0, 0), (0, 14), (0, 2 * head - own_gain)))
        small = jnp.concatenate([w_kv_share, small_scatter(gain_shares, count)], 0)
        return grad_tokens, small

    grad_tokens, small = stage(always, sum_attention, one_sums, w_one_share)
    small, w_query_share, w_out_share, up_sum, down_sum = sync(
        (small, w_query_share, w_out_share, up_sum, down_sum)
    )
    late = lax.psum((w_out_share, w_query_share.reshape(-1, split), small), "dp")
    up_blocks = spread_rows(up_sum, count)

    def sum_rest(out_sums, gate_blocks, down_sum):
        out = (middle + scatter_near(out_sums, count).astype(F32)).astype(BF)
        return out, turn_blocks(gate_blocks), down_sum.astype(F32)

    out, grad_w_gate, grad_w_down = stage(always, sum_rest, out_sums, gate_blocks, down_sum)
    out, up_blocks = sync((out, up_blocks))
    grad_w_up = turn_blocks(up_blocks)
    late, grad_w_up = sync((late, grad_w_up))
    w_out_sum, grad_w_query, small = [each.astype(F32) for each in late]
    grad_w_query = grad_w_query.reshape(count, own_columns, split).transpose(1, 0, 2)
    grad_w_query = grad_w_query.reshape(own_columns, -1)
    grad_w_kv, grad_gains = small[:own_columns], small[own_columns : own_columns + 2, :own_gain]

    return (
        out.reshape(tokens.shape),
        grad_tokens.reshape(tokens.shape),
        grad_second,
        grad_gains[0],
        grad_w_query,
        grad_w_kv[:, :head],
        grad_w_kv[:, head:],
        w_out_sum.astype(F32),
        grad_gains[1],
        grad_w_gate,
        grad_w_up,
        grad_w_down,
    )


def solution(mesh):
    return jax.shard_map(
        body,
        mesh=mesh,
        in_specs=(
            P("dp", "seq", None),
            P("dp"),
            P("dp", "seq", None),
            P("dp", "seq", None),
            P("dp", "seq", None),
            P("seq"),
            P("seq", None),
            P("seq", None),
            P("seq", None),
            P("seq", None),
            P("seq"),
            P("seq", None),
            P("seq", None),
            P("seq", None),
        ),
        out_specs=(
            P("dp", "seq", None),
            P("dp", "seq", None),
            P("dp", "seq", None),
            P("seq"),
            P("seq", None),
            P("seq", None),
            P("seq", None),
            P("seq", None),
            P("seq"),
            P("seq", None),
            P("seq", None),
            P("seq", None),
        ),
        check_vma=False,
    )
```

```python
import functools
import math

import jax
import jax.numpy as jnp
from jax import lax
from jax.experimental import pallas as pl
from jax.experimental.pallas import tpu as pltpu
from jax.sharding import PartitionSpec as P

EPSILON = 1e-05
BF = jnp.bfloat16
F32 = jnp.float32
QUERY_ROWS = 256
VMEM_BYTES = 32 * 1024 * 1024
LIGHT = pl.CostEstimate(flops=1000, bytes_accessed=1000, transcendentals=0)
MLP_VMEM_BYTES = 48 * 1024 * 1024


def dot_nn(left, right):
    return jnp.dot(left, right, preferred_element_type=F32)


def dot_nt(left, right):
    return lax.dot_general(left, right, (((1,), (1,)), ((), ())), preferred_element_type=F32)


def dot_tn(left, right):
    return lax.dot_general(left, right, (((0,), (0,)), ((), ())), preferred_element_type=F32)


def is_cube(count):
    return count == 8


def order_key(count):
    rank = lax.axis_index("seq")
    return rank if is_cube(count) else jnp.zeros_like(rank)


def swap(array, bit):
    return lax.ppermute(array, "seq", [(i, i ^ bit) for i in range(8)])


def add_rounded(*terms):
    total = terms[0].astype(F32)
    for term in terms[1:]:
        total = total + term.astype(F32)
    return total.astype(BF)


def after(value, *others):
    return lax.optimization_barrier((value, others))[0]


def gather_near(piece, count, *between):
    if not is_cube(count):
        gathered = lax.all_gather(piece, "seq", axis=0, tiled=False)
        return [gathered[j] for j in range(count)]
    from_x = swap(piece, 2)
    from_y = swap(piece, 4)
    from_core = swap(piece, 1)
    from_x, from_y = after([from_x, from_y], *between)
    return [piece, from_core, from_x, swap(from_x, 1), from_y, swap(from_y, 1)]


def far_halves(near):
    half = near[0].shape[0] // 2
    return [swap(near[2][:half], 4), swap(near[4][half:], 2)]


def gather_far(near, count, *window):
    if not is_cube(count):
        return near[-2]
    return jnp.concatenate(after(far_halves(near), *window), 0)


def gather_last(near, far, count):
    return swap(far, 1) if is_cube(count) else near[-1]


def gather_pieces(piece, count):
    near = gather_near(piece, count)
    far = gather_far(near, count)
    last = gather_last(near, far, count)
    return (near if is_cube(count) else near[:-2]) + [far, last]


def scatter_far(parts, count, *window):
    if not is_cube(count):
        return parts
    half = parts[0].shape[0] // 2
    far = add_rounded(parts[6], swap(parts[7], 1))
    far_x = swap(far[:half], 2)
    far_y = swap(far[half:], 4)
    far_x, far_y = after([far_x, far_y], *window)
    near_x = add_rounded(parts[2], swap(parts[3], 1))
    near_y = add_rounded(parts[4], swap(parts[5], 1))
    near_y = jnp.concatenate([add_rounded(near_y[:half], far_x), near_y[half:]], 0)
    near_x = jnp.concatenate([near_x[:half], add_rounded(near_x[half:], far_y)], 0)
    own = add_rounded(parts[0], swap(parts[1], 1))
    return [own, near_x, near_y]


def scatter_near(sums, count, *window):
    if not is_cube(count):
        return lax.psum_scatter(jnp.stack(sums), "seq", scatter_dimension=0, tiled=False)
    own, near_x, near_y = sums
    got_x = swap(near_x, 2)
    got_y = swap(near_y, 4)
    return add_rounded(after(own, *window), got_x, got_y)


def scatter_pieces(parts, count, *window):
    return scatter_near(scatter_far(parts, count), count, *window)


def gather_ordered(piece, count):
    if not is_cube(count):
        return lax.all_gather(piece, "seq", axis=0, tiled=False)
    rank = lax.axis_index("seq")
    held = piece
    for bit in (4, 2, 1):
        other = swap(held, bit)
        upper = (rank & bit) != 0
        held = jnp.stack([jnp.where(upper, other, held), jnp.where(upper, held, other)])
    held = held.transpose(2, 1, 0, *range(3, held.ndim))
    return held.reshape(count, *piece.shape)


def rows_to_columns(weight):
    return lax.all_to_all(weight, "seq", split_axis=1, concat_axis=0, tiled=True)


def columns_to_rows(weight):
    return lax.all_to_all(weight, "seq", split_axis=0, concat_axis=1, tiled=True)


def stage(always, work, *operands):
    shapes = jax.eval_shape(work, *operands)
    empty = lambda *_: jax.tree.map(lambda leaf: jnp.zeros(leaf.shape, leaf.dtype), shapes)
    return lax.cond(always, work, empty, *operands)


def small_scatter(share, count):
    if not is_cube(count):
        return lax.psum_scatter(share, "seq", scatter_dimension=0, tiled=False)
    rank = lax.axis_index("seq")
    for bit in (1, 2, 4):
        upper = (rank & bit) != 0
        pairs = share.reshape(-1, 2, *share.shape[1:])
        low, high = pairs[:, 0], pairs[:, 1]
        share = add_rounded(jnp.where(upper, high, low), swap(jnp.where(upper, low, high), bit))
    return share[0]


def load_keys(key_ref, kv_ref, rows_ref, count, head, column):
    chunk = kv_ref.shape[2]
    for place in range(count):
        rows_ref[place * chunk : (place + 1) * chunk, :] = kv_ref[
            place ^ key_ref, 0, :, column * head : (column + 1) * head
        ]


def transpose_rows(rows_ref, turned_ref):
    step = 128
    for start in range(0, rows_ref.shape[0], step):
        turned_ref[:, start : start + step] = (
            rows_ref[start : start + step, :].astype(F32).T.astype(BF)
        )


def masked_scores(keys, queries, limit):
    scores = dot_nt(keys, queries)
    key_pos = lax.broadcasted_iota(jnp.int32, scores.shape, 0)
    return jnp.where(key_pos <= limit, scores, -jnp.inf)


def forward_kernel(
    lengths_ref, key_ref, q_ref, kv_ref, attn_ref, lse_ref, keys, values, values_t
):
    count, _, chunk, _ = q_ref.shape
    head = keys.shape[1]
    total = keys.shape[0]
    block = min(QUERY_ROWS, total)
    per_block = block // chunk
    key = key_ref[0]
    length = lengths_ref[pl.program_id(0)]
    load_keys(key, kv_ref, keys, count, head, 0)
    load_keys(key, kv_ref, values, count, head, 1)
    transpose_rows(values, values_t)
    for start in range(0, total, block):
        limit_row = start + lax.broadcasted_iota(jnp.int32, (1, block), 1)
        limit = jnp.minimum(limit_row, length - 1)
        seen = start + block
        places = [(start // chunk + i) ^ key for i in range(per_block)]
        for h in range(q_ref.shape[3] // head):
            columns = slice(h * head, (h + 1) * head)
            queries = jnp.concatenate([q_ref[p, 0, :, columns] for p in places], 0)
            scores = masked_scores(keys[:seen, :], queries, limit)
            top = jnp.max(scores, 0, keepdims=True)
            weights = jnp.exp(scores - top)
            norm = jnp.sum(weights, 0, keepdims=True)
            mixed = dot_nn(values_t[:, :seen], weights.astype(BF)) / norm
            rows = mixed.T.astype(BF)
            for i, p in enumerate(places):
                attn_ref[p, 0, :, columns] = rows[i * chunk : (i + 1) * chunk]
            lse_ref[0, h : h + 1, start : start + block] = top + jnp.log(norm)


def attend_forward(queries, key_values, lengths, key, head):
    count, seqs, chunk, width = queries.shape
    total = count * chunk
    heads = width // head
    whole = lambda s, *_: (0, s, 0, 0)
    return pl.pallas_call(
        forward_kernel,
        grid_spec=pltpu.PrefetchScalarGridSpec(
            num_scalar_prefetch=2,
            grid=(seqs,),
            in_specs=[
                pl.BlockSpec((count, 1, chunk, width), whole),
                pl.BlockSpec((count, 1, chunk, 2 * head), whole),
            ],
            out_specs=[
                pl.BlockSpec((count, 1, chunk, width), whole),
                pl.BlockSpec((1, heads, total), lambda s, *_: (s, 0, 0)),
            ],
            scratch_shapes=[
                pltpu.VMEM((total, head), BF),
                pltpu.VMEM((total, head), BF),
                pltpu.VMEM((head, total), BF),
            ],
        ),
        out_shape=[
            jax.ShapeDtypeStruct(queries.shape, BF),
            jax.ShapeDtypeStruct((seqs, heads, total), F32),
        ],
        compiler_params=pltpu.CompilerParams(vmem_limit_bytes=VMEM_BYTES),
        cost_estimate=LIGHT,
    )(lengths, key, queries, key_values)


def second_kernel(
    lengths_ref, key_ref, q_ref, up_ref, kv_ref, dq_ref, dkv_ref, keys, values, keys_t, dk, dv
):
    _, chunk, width = q_ref.shape
    count = kv_ref.shape[0]
    head = keys.shape[1]
    total = keys.shape[0]
    block = min(QUERY_ROWS, total)
    per_block = block // chunk
    key = key_ref[0]
    rank = key_ref[1]
    length = lengths_ref[pl.program_id(0)]
    load_keys(key, kv_ref, keys, count, head, 0)
    load_keys(key, kv_ref, values, count, head, 1)
    transpose_rows(keys, keys_t)
    dk[...] = jnp.zeros_like(dk)
    dv[...] = jnp.zeros_like(dv)
    own = rank * chunk + lax.broadcasted_iota(jnp.int32, (1, block), 1) % chunk
    limit = jnp.minimum(own, length - 1)
    live = rank * chunk + lax.broadcasted_iota(jnp.int32, (chunk, head), 0) < length
    for first in range(0, width // head, per_block):
        spans = [slice((first + i) * head, (first + i + 1) * head) for i in range(per_block)]
        queries = jnp.concatenate([q_ref[0, :, s] for s in spans], 0)
        upstream = jnp.concatenate(
            [jnp.where(live, up_ref[0, :, s].astype(F32), 0.0).astype(BF) for s in spans], 0
        )
        scores = masked_scores(keys[...], queries, limit)
        weights = jnp.exp(scores - jnp.max(scores, 0, keepdims=True))
        probs = weights * (1.0 / jnp.sum(weights, 0, keepdims=True))
        product = probs * dot_nt(values[...], upstream)
        d_scores = (product - probs * jnp.sum(product, 0, keepdims=True)).astype(BF)
        d_queries = dot_nn(keys_t[...], d_scores).T.astype(BF)
        for i, s in enumerate(spans):
            dq_ref[0, :, s] = d_queries[i * chunk : (i + 1) * chunk]
        dk[...] += dot_nn(d_scores, queries)
        dv[...] += dot_nn(probs.astype(BF), upstream)
    for place in range(count):
        rows = slice(place * chunk, (place + 1) * chunk)
        dkv_ref[place ^ key, 0, :, :head] = dk[rows, :]
        dkv_ref[place ^ key, 0, :, head:] = dv[rows, :]


def attend_second(queries, upstream, key_values, lengths, key, head):
    seqs, chunk, width = queries.shape
    count = key_values.shape[0]
    total = count * chunk
    whole = lambda s, *_: (0, s, 0, 0)
    local = pl.BlockSpec((1, chunk, width), lambda s, *_: (s, 0, 0))
    return pl.pallas_call(
        second_kernel,
        grid_spec=pltpu.PrefetchScalarGridSpec(
            num_scalar_prefetch=2,
            grid=(seqs,),
            in_specs=[local, local, pl.BlockSpec((count, 1, chunk, 2 * head), whole)],
            out_specs=[local, pl.BlockSpec((count, 1, chunk, 2 * head), whole)],
            scratch_shapes=[
                pltpu.VMEM((total, head), BF),
                pltpu.VMEM((total, head), BF),
                pltpu.VMEM((head, total), BF),
                pltpu.VMEM((total, head), F32),
                pltpu.VMEM((total, head), F32),
            ],
        ),
        out_shape=[
            jax.ShapeDtypeStruct(queries.shape, BF),
            jax.ShapeDtypeStruct(key_values.shape, F32),
        ],
        compiler_params=pltpu.CompilerParams(vmem_limit_bytes=VMEM_BYTES),
        cost_estimate=LIGHT,
    )(lengths, key, queries, upstream, key_values)


def backward_kernel(
    lengths_ref,
    key_ref,
    q_ref,
    up_ref,
    attn_ref,
    kv_ref,
    lse_ref,
    more_ref,
    cos_ref,
    sin_ref,
    grads_ref,
    keys,
    values,
    keys_t,
    dk,
    dv,
):
    count, _, chunk, width = q_ref.shape
    head = keys.shape[1]
    total = keys.shape[0]
    block = min(QUERY_ROWS, total)
    per_block = block // chunk
    key = key_ref[0]
    length = lengths_ref[pl.program_id(0)]
    scale = 1.0 / math.sqrt(head)
    load_keys(key, kv_ref, keys, count, head, 0)
    load_keys(key, kv_ref, values, count, head, 1)
    transpose_rows(keys, keys_t)
    for place in range(count):
        rows = slice(place * chunk, (place + 1) * chunk)
        dk[rows, :] = more_ref[place ^ key, 0, :, :head]
        dv[rows, :] = more_ref[place ^ key, 0, :, head:]
    for start in range(0, total, block):
        limit_row = start + lax.broadcasted_iota(jnp.int32, (1, block), 1)
        limit = jnp.minimum(limit_row, length - 1)
        seen = start + block
        places = [(start // chunk + i) ^ key for i in range(per_block)]
        for h in range(width // head):
            columns = slice(h * head, (h + 1) * head)
            queries = jnp.concatenate([q_ref[p, 0, :, columns] for p in places], 0)
            upstream = jnp.concatenate([up_ref[p, 0, :, columns] for p in places], 0)
            attn = jnp.concatenate([attn_ref[p, 0, :, columns] for p in places], 0)
            centre = jnp.sum((upstream.astype(F32) * attn.astype(F32)).T, 0, keepdims=True)
            scores = masked_scores(keys[:seen, :], queries, limit)
            probs = jnp.exp(scores - lse_ref[0, h : h + 1, start : start + block])
            d_probs = dot_nt(values[:seen, :], upstream)
            d_scores = (probs * (d_probs - centre)).astype(BF)
            d_queries = dot_nn(keys_t[:, :seen], d_scores).T.astype(BF).astype(F32) * scale
            span = slice(start, start + block)
            d_queries = (
                d_queries * cos_ref[span, :]
                - pltpu.roll(d_queries, head // 2, 1) * sin_ref[span, :]
            ).astype(BF)
            for i, p in enumerate(places):
                grads_ref[p, 0, :, columns] = d_queries[i * chunk : (i + 1) * chunk]
            dk[:seen, :] += dot_nn(d_scores, queries)
            dv[:seen, :] += dot_nn(probs.astype(BF), upstream)
    for place in range(count):
        rows = slice(place * chunk, (place + 1) * chunk)
        turned = dk[rows, :] * cos_ref[rows, :] - pltpu.roll(dk[rows, :], head // 2, 1) * sin_ref[rows, :]
        grads_ref[place ^ key, 0, :, width : width + head] = turned.astype(BF)
        grads_ref[place ^ key, 0, :, width + head :] = dv[rows, :].astype(BF)


def attend_backward(queries, upstream, attn, key_values, lse, more, tables, lengths, key, head):
    count, seqs, chunk, width = queries.shape
    total = count * chunk
    heads = width // head
    whole = lambda s, *_: (0, s, 0, 0)
    by_head = pl.BlockSpec((count, 1, chunk, width), whole)
    shared = pl.BlockSpec((count, 1, chunk, 2 * head), whole)
    return pl.pallas_call(
        backward_kernel,
        grid_spec=pltpu.PrefetchScalarGridSpec(
            num_scalar_prefetch=2,
            grid=(seqs,),
            in_specs=[
                by_head,
                by_head,
                by_head,
                shared,
                pl.BlockSpec((1, heads, total), lambda s, *_: (s, 0, 0)),
                shared,
                pl.BlockSpec((total, head), lambda s, *_: (0, 0)),
                pl.BlockSpec((total, head), lambda s, *_: (0, 0)),
            ],
            out_specs=pl.BlockSpec((count, 1, chunk, width + 2 * head), whole),
            scratch_shapes=[
                pltpu.VMEM((total, head), BF),
                pltpu.VMEM((total, head), BF),
                pltpu.VMEM((head, total), BF),
                pltpu.VMEM((total, head), F32),
                pltpu.VMEM((total, head), F32),
            ],
        ),
        out_shape=jax.ShapeDtypeStruct((count, seqs, chunk, width + 2 * head), BF),
        compiler_params=pltpu.CompilerParams(vmem_limit_bytes=VMEM_BYTES),
        cost_estimate=LIGHT,
    )(lengths, key, queries, upstream, attn, key_values, lse, more, *tables)


def front_kernel(key_ref, a_ref, b_ref, gain_ref, wq_ref, wkv_ref, cos_ref, sin_ref, *rest, first):
    na_ref, nb_ref, q_ref, kv_ref = rest[-4:]
    _, seqs, chunk, width = q_ref.shape
    head = kv_ref.shape[3] // 2
    scale = 1.0 / math.sqrt(head)
    for i, piece in enumerate((a_ref, b_ref)):
        inputs = piece[...].astype(F32)
        normed = (
            inputs
            * lax.rsqrt(jnp.mean(inputs * inputs, -1, keepdims=True) + EPSILON)
            * gain_ref[...]
        ).astype(BF)
        (na_ref, nb_ref)[i][...] = normed
        q_linear = dot_nn(normed, wq_ref[...])
        kv_linear = dot_nn(normed, wkv_ref[...])
        span = pl.ds(pl.multiple_of(((first + i) ^ key_ref[0]) * chunk, chunk), chunk)
        cosine, sine = cos_ref[span, :], sin_ref[span, :]
        turn = lambda v: v * cosine + pltpu.roll(v, head // 2, 1) * sine
        for s in range(seqs):
            rows = slice(s * chunk, (s + 1) * chunk)
            for h in range(width // head):
                columns = slice(h * head, (h + 1) * head)
                q_ref[i, s, :, columns] = (turn(q_linear[rows, columns]) * scale).astype(BF)
            kv_ref[i, s, :, :head] = turn(kv_linear[rows, :head]).astype(BF)
            kv_ref[i, s, :, head:] = kv_linear[rows, head:].astype(BF)


def whole_spec(array):
    return pl.BlockSpec(array.shape, lambda *_: (0,) * array.ndim)


def pair_spec(shape, pair):
    return pl.BlockSpec((2, *shape[1:]), lambda *_: (pair,) + (0,) * (len(shape) - 1))


def front_pair(key, pieces, pair, gain, wq, wkv, tables, seqs, count, before):
    rows, width = pieces[0].shape
    chunk = rows // seqs
    shapes = [
        (count, seqs, chunk, wq.shape[1]),
        (count, seqs, chunk, wkv.shape[1]),
    ]
    given = [*pieces, gain, wq, wkv, *tables]
    return pl.pallas_call(
        functools.partial(front_kernel, first=2 * pair),
        grid_spec=pltpu.PrefetchScalarGridSpec(
            num_scalar_prefetch=1,
            grid=(1,),
            in_specs=[whole_spec(a) for a in given] + [pl.BlockSpec(memory_space=pl.ANY)] * len(before),
            out_specs=[whole_spec(pieces[0])] * 2 + [pair_spec(shape, pair) for shape in shapes],
        ),
        out_shape=[jax.ShapeDtypeStruct((rows, width), BF)] * 2
        + [jax.ShapeDtypeStruct(shape, BF) for shape in shapes],
        input_output_aliases={1 + len(given) + i: 2 + i for i in range(len(before))},
        compiler_params=pltpu.CompilerParams(vmem_limit_bytes=VMEM_BYTES),
        cost_estimate=LIGHT,
    )(key, *given, *before)


def hidden_kernel(na_hbm, nb_hbm, ga_hbm, gb_hbm, shares_hbm, down_hbm, *rest, first):
    hidden_hbm, dgate_hbm, dup_hbm = rest[-11:-8]
    normed, branch, both, down, hidden, dgate, dup, sems = rest[-8:]
    rows = na_hbm.shape[0]
    lines, inner = shares_hbm.shape[0], down_hbm.shape[0]
    low, high = pl.ds(0, rows), pl.ds(rows, rows)
    places = [(shares_hbm.at[i], both.at[:, i]) for i in range(lines)]
    places += [(na_hbm, normed.at[low]), (nb_hbm, normed.at[high])]
    places += [(ga_hbm, branch.at[low]), (gb_hbm, branch.at[high]), (down_hbm, down)]
    loads = [pltpu.make_async_copy(a, b, sems.at[i]) for i, (a, b) in enumerate(places)]
    places = []
    for stack, target in ((hidden, hidden_hbm), (dgate, dgate_hbm), (dup, dup_hbm)):
        places += [(stack.at[low], target.at[first]), (stack.at[high], target.at[first + 1])]
    stores = [
        pltpu.make_async_copy(a, b, sems.at[len(loads) + i]) for i, (a, b) in enumerate(places)
    ]
    for load in loads:
        load.start()
    for load in loads[: lines + 2]:
        load.wait()
    gate_up = dot_nn(normed[...], both[...].reshape(-1, 2 * inner))
    gate_pre, up_pre = gate_up[:, :inner], gate_up[:, inner:]
    sigma = jax.nn.sigmoid(gate_pre)
    silu_gate = gate_pre * sigma
    slope = sigma * (1.0 + gate_pre * (1.0 - sigma))
    hidden[...] = (silu_gate * up_pre).astype(BF)
    for store in stores[:2]:
        store.start()
    for load in loads[lines + 2 :]:
        load.wait()
    grad_hidden = dot_nt(branch[...], down[...])
    dgate[...] = (grad_hidden * up_pre * slope).astype(BF)
    dup[...] = (grad_hidden * silu_gate).astype(BF)
    for store in stores[2:]:
        store.start()
    for store in stores:
        store.wait()


def hidden_pair(normed, branch, pair, shares, down, count, before):
    rows, width = normed[0].shape
    inner = down.shape[0]
    lines, _, share_rows, _ = shares.shape
    given = [*normed, *branch, shares, down]
    anywhere = pl.BlockSpec(memory_space=pl.ANY)
    stacked = jax.ShapeDtypeStruct((count, rows, inner), BF)
    return pl.pallas_call(
        functools.partial(hidden_kernel, first=2 * pair),
        in_specs=[anywhere] * (6 + len(before)),
        out_specs=[anywhere] * 3,
        out_shape=[stacked] * 3,
        scratch_shapes=[pltpu.VMEM((2 * rows, width), BF)] * 2
        + [pltpu.VMEM((count, lines, share_rows, 2 * inner), BF), pltpu.VMEM(down.shape, BF)]
        + [pltpu.VMEM((2 * rows, inner), BF)] * 3
        + [pltpu.SemaphoreType.DMA((lines + 11,))],
        input_output_aliases={6 + i: i for i in range(len(before))},
        compiler_params=pltpu.CompilerParams(vmem_limit_bytes=MLP_VMEM_BYTES),
        cost_estimate=pl.CostEstimate(
            flops=20 * rows * width * inner,
            bytes_accessed=6 * width * inner + 12 * rows * width,
            transcendentals=2 * rows * inner,
        ),
    )(*given, *before)


def mlp_parts_kernel(hidden_hbm, dgate_hbm, dup_hbm, shares_hbm, down_hbm, *rest, first):
    pa_hbm, pb_hbm, oa_hbm, ob_hbm = rest[:4]
    hidden, dgate, dup, both, down, parts, outs, sems = rest[4:]
    rows = pa_hbm.shape[0]
    lines, inner = shares_hbm.shape[0], down_hbm.shape[0]
    low, high = pl.ds(0, rows), pl.ds(rows, rows)
    both_stacks = ((dgate_hbm, dgate), (dup_hbm, dup), (hidden_hbm, hidden))
    places = [(stack.at[pl.ds(first, 2)], target) for stack, target in both_stacks]
    places += [(shares_hbm.at[i], both.at[:, i]) for i in range(lines)]
    places += [(down_hbm, down)]
    loads = [pltpu.make_async_copy(a, b, sems.at[i]) for i, (a, b) in enumerate(places)]
    places = [(parts.at[low], pa_hbm), (parts.at[high], pb_hbm)]
    places += [(outs.at[low], oa_hbm), (outs.at[high], ob_hbm)]
    stores = [
        pltpu.make_async_copy(a, b, sems.at[len(loads) + i]) for i, (a, b) in enumerate(places)
    ]
    for load in loads:
        load.start()
    for load in loads[: lines + 3]:
        load.wait()
    both_cols = both[...].reshape(-1, 2 * inner)
    for i in range(2):
        grads = dot_nt(jnp.concatenate([dgate[i], dup[i]], 1), both_cols)
        parts[i * rows : (i + 1) * rows, :] = grads.astype(BF)
        stores[i].start()
    loads[-1].wait()
    for i in range(2):
        outs[i * rows : (i + 1) * rows, :] = dot_nn(hidden[i], down[...]).astype(BF)
        stores[2 + i].start()
    for store in stores:
        store.wait()


def mlp_parts(stacks, pair, shares, down):
    count, rows, inner = stacks[0].shape
    width = down.shape[1]
    lines, _, share_rows, _ = shares.shape
    anywhere = pl.BlockSpec(memory_space=pl.ANY)
    apart = jax.ShapeDtypeStruct((rows, width), BF)
    return pl.pallas_call(
        functools.partial(mlp_parts_kernel, first=2 * pair),
        in_specs=[anywhere] * 5,
        out_specs=[anywhere] * 4,
        out_shape=[apart] * 4,
        scratch_shapes=[pltpu.VMEM((2, rows, inner), BF)] * 3
        + [pltpu.VMEM((count, lines, share_rows, 2 * inner), BF), pltpu.VMEM(down.shape, BF)]
        + [pltpu.VMEM((2 * rows, width), BF)] * 2
        + [pltpu.SemaphoreType.DMA((lines + 8,))],
        compiler_params=pltpu.CompilerParams(vmem_limit_bytes=MLP_VMEM_BYTES),
        cost_estimate=pl.CostEstimate(
            flops=20 * rows * width * inner,
            bytes_accessed=6 * width * inner + 12 * rows * width,
            transcendentals=0,
        ),
    )(*stacks, shares, down)


def proj_kernel(a_ref, b_ref, w_ref, attn_ref, *rest, last):
    dattn_ref, total_ref = rest[-2:]
    seqs, chunk = attn_ref.shape[1:3]
    total = None if len(rest) == 2 else rest[1][...]
    for i, piece in enumerate((a_ref, b_ref)):
        grads = piece[...]
        d_attn = dot_nt(grads, w_ref[...]).astype(BF)
        for s in range(seqs):
            rows = slice(s * chunk, (s + 1) * chunk)
            dattn_ref[i, s] = d_attn[rows]
            share = dot_tn(attn_ref[i, s], grads[rows])
            total = share if total is None else total + share
    total_ref[...] = total.astype(total_ref.dtype)


def proj_pair(pieces, pair, w_out, attn, count, before):
    last = 2 * pair + 2 == count
    rows, width = pieces[0].shape
    given = [*pieces, w_out]
    extra_specs = []
    aliases = {}
    if before:
        extra_specs = [pl.BlockSpec(memory_space=pl.ANY), whole_spec(before[1])]
        aliases = {4: 0} if last else {4: 0, 5: 1}
    total = jax.ShapeDtypeStruct(w_out.shape, BF if last else F32)
    return pl.pallas_call(
        functools.partial(proj_kernel, last=last),
        grid=(1,),
        in_specs=[whole_spec(a) for a in given] + [pair_spec(attn.shape, pair)] + extra_specs,
        out_specs=[pair_spec(attn.shape, pair), whole_spec(total)],
        out_shape=[jax.ShapeDtypeStruct(attn.shape, BF), total],
        input_output_aliases=aliases,
        compiler_params=pltpu.CompilerParams(vmem_limit_bytes=VMEM_BYTES),
        cost_estimate=LIGHT,
    )(*given, attn, *before)


def parts_kernel(*refs, count, turned):
    lefts, weights = refs[: len(turned)], refs[len(turned) : 2 * len(turned)]
    outs, (buffer, sems) = refs[2 * len(turned) : -2], refs[-2:]
    order = (6, 7, 2, 3, 4, 5, 0, 1) if count == 8 else range(count)
    stores = []
    for j in order:
        total = None
        for left, weight, turn in zip(lefts, weights, turned):
            share = (dot_nt if turn else dot_nn)(left[j], weight[...])
            total = share if total is None else total + share
        buffer[j] = total.astype(BF)
        stores.append(pltpu.make_async_copy(buffer.at[j], outs[j], sems.at[j]))
        stores[-1].start()
    for store in stores:
        store.wait()


def parts_of(lefts, weights, turned):
    count, rows = lefts[0].shape[:2]
    width = weights[0].shape[0 if turned[0] else 1]
    return pl.pallas_call(
        functools.partial(parts_kernel, count=count, turned=turned),
        grid=(1,),
        in_specs=[whole_spec(a) for a in (*lefts, *weights)],
        out_specs=[pl.BlockSpec(memory_space=pl.ANY)] * count,
        out_shape=[jax.ShapeDtypeStruct((rows, width), BF)] * count,
        scratch_shapes=[
            pltpu.VMEM((count, rows, width), BF),
            pltpu.SemaphoreType.DMA((count,)),
        ],
        compiler_params=pltpu.CompilerParams(vmem_limit_bytes=VMEM_BYTES),
        cost_estimate=LIGHT,
    )(*lefts, *weights)


def outer_kernel(*refs, count, rights):
    left = jnp.concatenate([ref[...] for ref in refs[:count]], 0)
    left_t = left.T
    for right, out in zip(refs[count : count + rights], refs[count + rights :]):
        out[...] = dot_nn(left_t, right[...]).astype(BF)


def outer_of(pieces, rights):
    count = len(pieces)
    rows, width = pieces[0].shape
    step = min(256, width)
    return pl.pallas_call(
        functools.partial(outer_kernel, count=count, rights=len(rights)),
        grid=(width // step,),
        in_specs=[pl.BlockSpec((rows, step), lambda i: (0, i))] * count
        + [pl.BlockSpec(right.shape, lambda i: (0, 0)) for right in rights],
        out_specs=[pl.BlockSpec((step, right.shape[1]), lambda i: (i, 0)) for right in rights],
        out_shape=[jax.ShapeDtypeStruct((width, right.shape[1]), BF) for right in rights],
        compiler_params=pltpu.CompilerParams(vmem_limit_bytes=VMEM_BYTES),
        cost_estimate=LIGHT,
    )(*pieces, *rights)


def inner_kernel(*refs, count, lefts):
    pieces = refs[lefts : lefts + count]
    outs, lefts_t = refs[lefts + count : 2 * lefts + count], refs[2 * lefts + count :]
    rows = pieces[0].shape[0]

    @pl.when(pl.program_id(0) == 0)
    def _():
        for left, left_t in zip(refs[:lefts], lefts_t):
            for j in range(count):
                span = slice(j * rows, (j + 1) * rows)
                left_t[:, span] = left[span, :].T

    right = jnp.concatenate([piece[...] for piece in pieces], 0)
    for out, left_t in zip(outs, lefts_t):
        out[...] = dot_nn(left_t[...], right).astype(BF)


def inner_of(lefts, pieces):
    count = len(pieces)
    rows, width = pieces[0].shape
    step = min(256, width)
    columns = lefts[0].shape[1]
    return pl.pallas_call(
        functools.partial(inner_kernel, count=count, lefts=len(lefts)),
        grid=(width // step,),
        in_specs=[pl.BlockSpec(left.shape, lambda i: (0, 0)) for left in lefts]
        + [pl.BlockSpec((rows, step), lambda i: (0, i))] * count,
        out_specs=[pl.BlockSpec((columns, step), lambda i: (0, i))] * len(lefts),
        out_shape=[jax.ShapeDtypeStruct((columns, width), BF)] * len(lefts),
        scratch_shapes=[pltpu.VMEM((columns, count * rows), BF)] * len(lefts),
        compiler_params=pltpu.CompilerParams(vmem_limit_bytes=VMEM_BYTES),
        cost_estimate=LIGHT,
    )(*lefts, *pieces)


def widen_kernel(query_ref, out_ref, small_ref, query_f, out_f, key_f, value_f, gains_f):
    width, head = query_ref.shape[2], key_f.shape[1]
    for j in range(query_ref.shape[0]):
        query_f[:, j * width : (j + 1) * width] = query_ref[j].astype(F32)
    out_f[...] = out_ref[...].astype(F32)
    rows = key_f.shape[0]
    key_f[...] = small_ref[:rows, :head].astype(F32)
    value_f[...] = small_ref[:rows, head:].astype(F32)
    gains_f[...] = small_ref[rows:, :].astype(F32)


def widen(query_blocks, out_sum, small, head):
    count, rows, width = query_blocks.shape
    shapes = [(rows, count * width), out_sum.shape, (rows, head), (rows, head)]
    shapes = [jax.ShapeDtypeStruct(shape, F32) for shape in (*shapes, (small.shape[0] - rows, 2 * head))]
    given = [query_blocks, out_sum, small]
    return pl.pallas_call(
        widen_kernel,
        grid=(1,),
        in_specs=[whole_spec(a) for a in given],
        out_specs=[whole_spec(a) for a in shapes],
        out_shape=shapes,
        compiler_params=pltpu.CompilerParams(vmem_limit_bytes=VMEM_BYTES),
        cost_estimate=LIGHT,
    )(*given)


def turn_kernel(blocks_ref, out_ref):
    turned = [blocks_ref[j].astype(F32).T for j in range(blocks_ref.shape[0])]
    out_ref[...] = jnp.concatenate(turned, 1)


def turn_blocks(blocks):
    count, columns, rows = blocks.shape
    step = min(128, rows)
    return pl.pallas_call(
        turn_kernel,
        grid=(rows // step,),
        in_specs=[pl.BlockSpec((count, columns, step), lambda i: (0, 0, i))],
        out_specs=pl.BlockSpec((step, count * columns), lambda i: (i, 0)),
        out_shape=jax.ShapeDtypeStruct((rows, count * columns), F32),
        compiler_params=pltpu.CompilerParams(vmem_limit_bytes=VMEM_BYTES),
        cost_estimate=LIGHT,
    )(blocks)


def spread_rows(share_t, count):
    columns, rows = share_t.shape
    blocks = share_t.reshape(columns, count, rows // count).transpose(1, 0, 2)
    return lax.all_to_all(blocks, "seq", split_axis=0, concat_axis=0, tiled=True)


def pack_kernel(place_ref, gate_ref, up_ref, out_ref):
    count = out_ref.shape[0]
    inner = gate_ref.shape[1] // count
    gate, up = gate_ref[...], up_ref[...]
    for j in range(count):
        columns = slice(j * inner, (j + 1) * inner)
        out_ref[j] = jnp.concatenate([gate[:, columns], up[:, columns]], 1)


def pack_weights(w_gate, w_up, count):
    lines = lax.axis_size("dp")
    rows, columns = w_gate.shape[0] // lines, w_gate.shape[1]
    place = lax.axis_index("dp").astype(jnp.int32).reshape(1)
    share = pl.BlockSpec((rows, columns), lambda i, place: (place[0], 0))
    shape = (count, rows, 2 * columns // count)
    return pl.pallas_call(
        pack_kernel,
        grid_spec=pltpu.PrefetchScalarGridSpec(
            num_scalar_prefetch=1,
            grid=(1,),
            in_specs=[share, share],
            out_specs=pl.BlockSpec(shape, lambda i, place: (0, 0, 0)),
        ),
        out_shape=jax.ShapeDtypeStruct(shape, BF),
        compiler_params=pltpu.CompilerParams(vmem_limit_bytes=VMEM_BYTES),
        cost_estimate=LIGHT,
    )(place, w_gate, w_up)


def share_weights(w_gate, w_up, w_query, count):
    packed = pack_weights(w_gate, w_up, count)
    packed = lax.all_to_all(packed, "seq", split_axis=0, concat_axis=0, tiled=True)
    query = rows_to_columns(w_query + packed[0, 0, 0] * 0)
    return query, lax.all_gather(packed, "dp", axis=0, tiled=False)


def rope_tables(positions, head_width):
    half_width = head_width // 2
    spacing = jnp.exp(
        jnp.arange(half_width).astype(F32) * (-2.0 * math.log(10000.0) / head_width)
    )
    angles = positions.astype(F32)[:, None] * spacing[None, :]
    sines = jnp.sin(angles)
    cosines = jnp.cos(angles)
    return (jnp.concatenate([cosines, cosines], 1), jnp.concatenate([-sines, sines], 1))


def rms_scale(values_in):
    return lax.rsqrt(jnp.mean(values_in * values_in, -1, keepdims=True) + EPSILON)


def norm_back(grad_normed, inputs, scale_rows, gain):
    weighted = grad_normed * gain
    cubed = scale_rows * scale_rows * scale_rows
    return scale_rows * weighted - inputs * cubed * jnp.mean(weighted * inputs, -1, keepdims=True)


def body(
    tokens,
    lengths,
    second_queries,
    cotangent,
    second_cotangent,
    gain_attn,
    w_query,
    w_key,
    w_value,
    w_out,
    gain_mlp,
    w_gate,
    w_up,
    w_down,
):
    count = lax.axis_size("seq")
    rank = lax.axis_index("seq")
    key = order_key(count)
    keys_of = jnp.stack([key, rank]).astype(jnp.int32)
    seqs, chunk, width = tokens.shape
    head = w_key.shape[1]
    rows = seqs * chunk
    all_rows = count * rows
    own_columns = w_query.shape[0]

    query_cols, shares = share_weights(w_gate, w_up, w_query, count)
    gain_rows = jnp.zeros((16, 2 * head), BF)
    gain_rows = gain_rows.at[:2, :own_columns].set(jnp.stack([gain_attn, gain_mlp]))
    packed = jnp.concatenate([jnp.concatenate([w_key, w_value], 1), gain_rows], 0)
    packed = gather_ordered(packed, count)
    kv_mat = packed[:, :own_columns].reshape(width, 2 * head)
    gain_one = packed[:, own_columns, :own_columns].reshape(1, width).astype(F32)
    gain_two = packed[:, own_columns + 1, :own_columns].reshape(1, width).astype(F32)

    local_pos = rank * chunk + jnp.arange(chunk, dtype=jnp.int32)
    valid = (local_pos[None, :] < lengths[:, None]).astype(F32).reshape(rows, 1)
    tables = rope_tables(jnp.arange(count * chunk, dtype=jnp.int32), head)

    last_pair = count // 2 - 1
    inputs = tokens.reshape(rows, width)
    front_of = lambda pair, two, before: front_pair(
        keys_of, two, pair, gain_one, query_cols, kv_mat, tables, seqs, count, before
    )
    near = gather_near(inputs, count)
    normed_one = []
    stacks = []
    far = gather_far(near, count)
    for pair in range(last_pair):
        *normed, queries, key_values = front_of(pair, near[2 * pair : 2 * pair + 2], stacks)
        normed_one += normed
        stacks = [queries, key_values]
    last = gather_last(near, far, count)
    grad_out = cotangent.reshape(rows, width).astype(F32) * valid
    branch_near = gather_near(after(grad_out.astype(BF), far), count, stacks)
    branch_far = gather_far(after(branch_near, stacks), count)
    *normed, queries, key_values = front_of(last_pair, [far, last], stacks)
    normed_one += normed
    attn, lse = attend_forward(queries, key_values, lengths, keys_of, head)
    attn, branch_far = lax.optimization_barrier((attn, branch_far))
    proj_parts = parts_of([attn.reshape(count, rows, -1)], [w_out], (False,))
    inputs_f = inputs.astype(F32)
    scale_one = rms_scale(inputs_f)

    branch_last = gather_last(branch_near, branch_far, count)
    branch = (branch_near if is_cube(count) else branch_near[:-2]) + [branch_far, branch_last]
    grad_second, dkv_second = attend_second(
        after(second_queries, proj_parts), second_cotangent, key_values, lengths, keys_of, head
    )
    proj_sum = scatter_pieces(proj_parts, count, dkv_second)
    proj_sum, shares = lax.optimization_barrier((proj_sum, shares))
    middle = inputs_f + proj_sum.astype(F32)

    scale_two = rms_scale(middle)
    sync = lax.optimization_barrier
    always = lengths[0] > 0
    hidden_of = lambda pair, two, before: tuple(
        hidden_pair(two, branch[2 * pair : 2 * pair + 2], pair, shares, w_down, count, before)
    )
    normed_own = (middle * scale_two * gain_two).astype(BF)

    def middle_pairs(near, stacks):
        for pair in range(1, last_pair):
            stacks = hidden_of(pair, near[2 * pair : 2 * pair + 2], stacks)
        return tuple(stacks)

    if is_cube(count):
        from_x, from_y, from_core = swap(normed_own, 2), swap(normed_own, 4), swap(normed_own, 1)
        stacks = stage(always, lambda *two: hidden_of(0, two, []), normed_own, from_core)
        from_x, from_y, stacks = sync((from_x, from_y, stacks))
        near = [normed_own, from_core, from_x, swap(from_x, 1), from_y, swap(from_y, 1)]
        halves = far_halves(near)
        stacks = stage(always, middle_pairs, near, stacks)
        halves, stacks = sync((halves, stacks))
        far = jnp.concatenate(halves, 0)
        last = swap(far, 1)
    else:
        near = gather_near(normed_own, count)
        stacks = middle_pairs(near, hidden_of(0, near[:2], []))
        far, last = near[-2:]
    stacks = hidden_of(last_pair, [far, last], list(stacks))
    hidden, grad_gate, grad_up = [stack.reshape(all_rows, -1) for stack in stacks]
    normed_two = (near if is_cube(count) else near[:-2]) + [far, last]
    split = queries.shape[-1]
    (w_gate_share,) = inner_of([grad_gate], normed_two)
    gate_sum = lax.psum(w_gate_share, "dp")

    def parts_mlp(stacks):
        parts = [mlp_parts(stacks, pair, shares, w_down) for pair in range(last_pair + 1)]
        normed_parts = [part for step in parts for part in step[:2]]
        return normed_parts, [part for step in parts for part in step[2:]]

    normed_parts, out_parts = stage(always, parts_mlp, stacks)

    def scatter_mlp(normed_parts, hidden):
        return scatter_far(normed_parts, count), inner_of([hidden], branch)[0]

    two_sums, w_down_share = stage(always, scatter_mlp, normed_parts, hidden)
    def sum_mlp(two_sums, grad_up):
        (w_up_share,) = inner_of([grad_up], normed_two)
        grad_normed_two = scatter_near(two_sums, count, w_up_share).astype(F32)
        grad_middle = grad_out + norm_back(grad_normed_two, middle, scale_two, gain_two)
        return grad_middle, jnp.sum(grad_normed_two * (middle * scale_two), 0), w_up_share

    grad_middle, gain_share, w_up_share = stage(always, sum_mlp, two_sums, grad_up)
    grad_middle, w_up_share, w_down_share, gate_sum = sync(
        (grad_middle, w_up_share, w_down_share, gate_sum)
    )
    up_sum, down_sum = lax.psum((w_up_share, w_down_share), "dp")
    proj_of = lambda pair, two, before: proj_pair(two, pair, w_out, attn, count, before)

    def gather_middle(grad_middle):
        near = gather_near(grad_middle.astype(BF), count)
        return near, proj_of(0, near[:2], [])

    near, state = stage(always, gather_middle, grad_middle)

    def project_back(near, state):
        far = gather_far(near, count)
        for pair in range(1, last_pair):
            state = proj_of(pair, near[2 * pair : 2 * pair + 2], state)
        last = gather_last(near, far, count)
        return proj_of(last_pair, [far, last], state)

    grad_attn, w_out_share = stage(always, project_back, near, state)
    grad_attn, gate_sum = sync((grad_attn, gate_sum))
    gate_blocks = spread_rows(gate_sum, count)

    def attention_back(grad_attn, out_parts):
        out_sums = scatter_far(out_parts, count)
        grads = attend_backward(
            queries, grad_attn, attn, key_values, lse, dkv_second, tables, lengths, keys_of, head
        )
        grads = grads.reshape(count, rows, -1)
        one_parts = parts_of(
            [grads[..., :split], grads[..., split:]], [query_cols, kv_mat], (True, True)
        )
        (w_one_share,) = outer_of(normed_one, [grads.reshape(all_rows, -1)])
        return out_sums, one_parts, w_one_share

    out_sums, one_parts, w_one_share = stage(always, attention_back, grad_attn, out_parts)
    one_parts, w_one_share, gate_blocks = sync((one_parts, w_one_share, gate_blocks))
    w_query_share = w_one_share[:, :split].reshape(count, own_columns, split)
    w_query_share = lax.all_to_all(w_query_share, "seq", split_axis=0, concat_axis=0, tiled=True)
    own_gain = gain_attn.shape[0]

    def scatter_attention(one_parts, w_one_share):
        kv_shares = w_one_share[:, split:].reshape(count, own_columns, 2 * head)
        return scatter_far(one_parts, count), small_scatter(kv_shares, count)

    one_sums, w_kv_share = stage(always, scatter_attention, one_parts, w_one_share)

    def sum_attention(one_sums, w_kv_share):
        grad_normed_one = scatter_near(one_sums, count).astype(F32)
        grad_tokens = grad_middle + norm_back(grad_normed_one, inputs_f, scale_one, gain_one)
        gain_shares = jnp.stack([jnp.sum(grad_normed_one * (inputs_f * scale_one), 0), gain_share])
        gain_shares = gain_shares.astype(BF).reshape(2, count, own_gain).transpose(1, 0, 2)
        gain_shares = jnp.pad(gain_shares, ((0, 0), (0, 14), (0, 2 * head - own_gain)))
        small = jnp.concatenate([w_kv_share, small_scatter(gain_shares, count)], 0)
        return grad_tokens, small

    grad_tokens, small = stage(always, sum_attention, one_sums, w_kv_share)
    small, w_query_share, w_out_share, up_sum, down_sum = sync(
        (small, w_query_share, w_out_share, up_sum, down_sum)
    )
    late = lax.psum((w_out_share, w_query_share.reshape(-1, split), small), "dp")

    def sum_rest(out_sums, gate_blocks, down_sum, up_sum):
        up_blocks = spread_rows(up_sum, count)
        out = (middle + scatter_near(out_sums, count).astype(F32)).astype(BF)
        return out, turn_blocks(gate_blocks), turn_blocks(up_blocks), down_sum.astype(F32)

    out, grad_w_gate, grad_w_up, grad_w_down = stage(
        always, sum_rest, out_sums, gate_blocks, down_sum, up_sum
    )
    late, grad_w_up = sync((late, grad_w_up))
    w_out_sum, w_query_sum, small = late
    grad_w_query, w_out_sum, grad_w_key, grad_w_value, grad_gains = widen(
        w_query_sum.reshape(count, own_columns, split), w_out_sum, small, head
    )

    return (
        out.reshape(tokens.shape),
        grad_tokens.reshape(tokens.shape),
        grad_second,
        grad_gains[0, :own_gain],
        grad_w_query,
        grad_w_key,
        grad_w_value,
        w_out_sum.astype(F32),
        grad_gains[1, :own_gain],
        grad_w_gate,
        grad_w_up,
        grad_w_down,
    )


def solution(mesh):
    return jax.shard_map(
        body,
        mesh=mesh,
        in_specs=(
            P("dp", "seq", None),
            P("dp"),
            P("dp", "seq", None),
            P("dp", "seq", None),
            P("dp", "seq", None),
            P("seq"),
            P("seq", None),
            P("seq", None),
            P("seq", None),
            P("seq", None),
            P("seq"),
            P("seq", None),
            P("seq", None),
            P("seq", None),
        ),
        out_specs=(
            P("dp", "seq", None),
            P("dp", "seq", None),
            P("dp", "seq", None),
            P("seq"),
            P("seq", None),
            P("seq", None),
            P("seq", None),
            P("seq", None),
            P("seq"),
            P("seq", None),
            P("seq", None),
            P("seq", None),
        ),
        check_vma=False,
    )
```

```python
import functools
import math

import jax
import jax.numpy as jnp
from jax import lax
from jax.experimental import pallas as pl
from jax.experimental.pallas import tpu as pltpu
from jax.sharding import PartitionSpec as P

EPSILON = 1e-05
BF = jnp.bfloat16
F32 = jnp.float32
QUERY_ROWS = 256
VMEM_BYTES = 32 * 1024 * 1024
LIGHT = pl.CostEstimate(flops=1000, bytes_accessed=1000, transcendentals=0)
MLP_VMEM_BYTES = 48 * 1024 * 1024


def dot_nn(left, right):
    return jnp.dot(left, right, preferred_element_type=F32)


def dot_nt(left, right):
    return lax.dot_general(left, right, (((1,), (1,)), ((), ())), preferred_element_type=F32)


def dot_tn(left, right):
    return lax.dot_general(left, right, (((0,), (0,)), ((), ())), preferred_element_type=F32)


def is_cube(count):
    return count == 8


def order_key(count):
    rank = lax.axis_index("seq")
    return rank if is_cube(count) else jnp.zeros_like(rank)


def swap(array, bit):
    return lax.ppermute(array, "seq", [(i, i ^ bit) for i in range(8)])


def add_rounded(*terms):
    total = terms[0].astype(F32)
    for term in terms[1:]:
        total = total + term.astype(F32)
    return total.astype(BF)


def after(value, *others):
    return lax.optimization_barrier((value, others))[0]


def gather_near(piece, count, *between):
    if not is_cube(count):
        gathered = lax.all_gather(piece, "seq", axis=0, tiled=False)
        return [gathered[j] for j in range(count)]
    from_x = swap(piece, 2)
    from_y = swap(piece, 4)
    from_core = swap(piece, 1)
    from_x, from_y = after([from_x, from_y], *between)
    return [piece, from_core, from_x, swap(from_x, 1), from_y, swap(from_y, 1)]


def far_halves(near):
    half = near[0].shape[0] // 2
    return [swap(near[2][:half], 4), swap(near[4][half:], 2)]


def gather_far(near, count, *window):
    if not is_cube(count):
        return near[-2]
    return jnp.concatenate(after(far_halves(near), *window), 0)


def gather_last(near, far, count):
    return swap(far, 1) if is_cube(count) else near[-1]


def gather_pieces(piece, count):
    near = gather_near(piece, count)
    far = gather_far(near, count)
    last = gather_last(near, far, count)
    return (near if is_cube(count) else near[:-2]) + [far, last]


def scatter_far(parts, count, *window):
    if not is_cube(count):
        return parts
    half = parts[0].shape[0] // 2
    far = add_rounded(parts[6], swap(parts[7], 1))
    far_x = swap(far[:half], 2)
    far_y = swap(far[half:], 4)
    far_x, far_y = after([far_x, far_y], *window)
    near_x = add_rounded(parts[2], swap(parts[3], 1))
    near_y = add_rounded(parts[4], swap(parts[5], 1))
    near_y = jnp.concatenate([add_rounded(near_y[:half], far_x), near_y[half:]], 0)
    near_x = jnp.concatenate([near_x[:half], add_rounded(near_x[half:], far_y)], 0)
    own = add_rounded(parts[0], swap(parts[1], 1))
    return [own, near_x, near_y]


def scatter_near(sums, count, *window):
    if not is_cube(count):
        return lax.psum_scatter(jnp.stack(sums), "seq", scatter_dimension=0, tiled=False)
    own, near_x, near_y = sums
    got_x = swap(near_x, 2)
    got_y = swap(near_y, 4)
    return add_rounded(after(own, *window), got_x, got_y)


def scatter_pieces(parts, count, *window):
    return scatter_near(scatter_far(parts, count), count, *window)


def gather_ordered(piece, count):
    if not is_cube(count):
        return lax.all_gather(piece, "seq", axis=0, tiled=False)
    rank = lax.axis_index("seq")
    held = piece
    for bit in (4, 2, 1):
        other = swap(held, bit)
        upper = (rank & bit) != 0
        held = jnp.stack([jnp.where(upper, other, held), jnp.where(upper, held, other)])
    held = held.transpose(2, 1, 0, *range(3, held.ndim))
    return held.reshape(count, *piece.shape)


def rows_to_columns(weight):
    return lax.all_to_all(weight, "seq", split_axis=1, concat_axis=0, tiled=True)


def columns_to_rows(weight):
    return lax.all_to_all(weight, "seq", split_axis=0, concat_axis=1, tiled=True)


def stage(always, work, *operands):
    shapes = jax.eval_shape(work, *operands)
    empty = lambda *_: jax.tree.map(lambda leaf: jnp.zeros(leaf.shape, leaf.dtype), shapes)
    return lax.cond(always, work, empty, *operands)


def small_scatter(share, count):
    if not is_cube(count):
        return lax.psum_scatter(share, "seq", scatter_dimension=0, tiled=False)
    rank = lax.axis_index("seq")
    for bit in (1, 2, 4):
        upper = (rank & bit) != 0
        pairs = share.reshape(-1, 2, *share.shape[1:])
        low, high = pairs[:, 0], pairs[:, 1]
        share = add_rounded(jnp.where(upper, high, low), swap(jnp.where(upper, low, high), bit))
    return share[0]


def load_keys(key_ref, kv_ref, rows_ref, count, head, column):
    chunk = kv_ref.shape[2]
    for place in range(count):
        rows_ref[place * chunk : (place + 1) * chunk, :] = kv_ref[
            place ^ key_ref, 0, :, column * head : (column + 1) * head
        ]


def transpose_rows(rows_ref, turned_ref):
    step = 128
    for start in range(0, rows_ref.shape[0], step):
        turned_ref[:, start : start + step] = (
            rows_ref[start : start + step, :].astype(F32).T.astype(BF)
        )


def masked_scores(keys, queries, limit):
    scores = dot_nt(keys, queries)
    key_pos = lax.broadcasted_iota(jnp.int32, scores.shape, 0)
    return jnp.where(key_pos <= limit, scores, -jnp.inf)


def forward_kernel(
    lengths_ref, key_ref, q_ref, kv_ref, attn_ref, lse_ref, keys, values, values_t
):
    count, _, chunk, _ = q_ref.shape
    head = keys.shape[1]
    total = keys.shape[0]
    block = min(QUERY_ROWS, total)
    per_block = block // chunk
    key = key_ref[0]
    length = lengths_ref[pl.program_id(0)]
    load_keys(key, kv_ref, keys, count, head, 0)
    load_keys(key, kv_ref, values, count, head, 1)
    transpose_rows(values, values_t)
    for start in range(0, total, block):
        limit_row = start + lax.broadcasted_iota(jnp.int32, (1, block), 1)
        limit = jnp.minimum(limit_row, length - 1)
        seen = start + block
        places = [(start // chunk + i) ^ key for i in range(per_block)]
        for h in range(q_ref.shape[3] // head):
            columns = slice(h * head, (h + 1) * head)
            queries = jnp.concatenate([q_ref[p, 0, :, columns] for p in places], 0)
            scores = masked_scores(keys[:seen, :], queries, limit)
            top = jnp.max(scores, 0, keepdims=True)
            weights = jnp.exp(scores - top)
            norm = jnp.sum(weights, 0, keepdims=True)
            mixed = dot_nn(values_t[:, :seen], weights.astype(BF)) / norm
            rows = mixed.T.astype(BF)
            for i, p in enumerate(places):
                attn_ref[p, 0, :, columns] = rows[i * chunk : (i + 1) * chunk]
            lse_ref[0, h : h + 1, start : start + block] = top + jnp.log(norm)


def attend_forward(queries, key_values, lengths, key, head):
    count, seqs, chunk, width = queries.shape
    total = count * chunk
    heads = width // head
    whole = lambda s, *_: (0, s, 0, 0)
    return pl.pallas_call(
        forward_kernel,
        grid_spec=pltpu.PrefetchScalarGridSpec(
            num_scalar_prefetch=2,
            grid=(seqs,),
            in_specs=[
                pl.BlockSpec((count, 1, chunk, width), whole),
                pl.BlockSpec((count, 1, chunk, 2 * head), whole),
            ],
            out_specs=[
                pl.BlockSpec((count, 1, chunk, width), whole),
                pl.BlockSpec((1, heads, total), lambda s, *_: (s, 0, 0)),
            ],
            scratch_shapes=[
                pltpu.VMEM((total, head), BF),
                pltpu.VMEM((total, head), BF),
                pltpu.VMEM((head, total), BF),
            ],
        ),
        out_shape=[
            jax.ShapeDtypeStruct(queries.shape, BF),
            jax.ShapeDtypeStruct((seqs, heads, total), F32),
        ],
        compiler_params=pltpu.CompilerParams(vmem_limit_bytes=VMEM_BYTES),
        cost_estimate=LIGHT,
    )(lengths, key, queries, key_values)


def second_kernel(
    lengths_ref, key_ref, q_ref, up_ref, kv_ref, dq_ref, dkv_ref, keys, values, keys_t, dk, dv
):
    _, chunk, width = q_ref.shape
    count = kv_ref.shape[0]
    head = keys.shape[1]
    total = keys.shape[0]
    block = min(QUERY_ROWS, total)
    per_block = block // chunk
    key = key_ref[0]
    rank = key_ref[1]
    length = lengths_ref[pl.program_id(0)]
    load_keys(key, kv_ref, keys, count, head, 0)
    load_keys(key, kv_ref, values, count, head, 1)
    transpose_rows(keys, keys_t)
    dk[...] = jnp.zeros_like(dk)
    dv[...] = jnp.zeros_like(dv)
    own = rank * chunk + lax.broadcasted_iota(jnp.int32, (1, block), 1) % chunk
    limit = jnp.minimum(own, length - 1)
    live = rank * chunk + lax.broadcasted_iota(jnp.int32, (chunk, head), 0) < length
    for first in range(0, width // head, per_block):
        spans = [slice((first + i) * head, (first + i + 1) * head) for i in range(per_block)]
        queries = jnp.concatenate([q_ref[0, :, s] for s in spans], 0)
        upstream = jnp.concatenate(
            [jnp.where(live, up_ref[0, :, s].astype(F32), 0.0).astype(BF) for s in spans], 0
        )
        scores = masked_scores(keys[...], queries, limit)
        weights = jnp.exp(scores - jnp.max(scores, 0, keepdims=True))
        probs = weights * (1.0 / jnp.sum(weights, 0, keepdims=True))
        product = probs * dot_nt(values[...], upstream)
        d_scores = (product - probs * jnp.sum(product, 0, keepdims=True)).astype(BF)
        d_queries = dot_nn(keys_t[...], d_scores).T.astype(BF)
        for i, s in enumerate(spans):
            dq_ref[0, :, s] = d_queries[i * chunk : (i + 1) * chunk]
        dk[...] += dot_nn(d_scores, queries)
        dv[...] += dot_nn(probs.astype(BF), upstream)
    for place in range(count):
        rows = slice(place * chunk, (place + 1) * chunk)
        dkv_ref[place ^ key, 0, :, :head] = dk[rows, :]
        dkv_ref[place ^ key, 0, :, head:] = dv[rows, :]


def attend_second(queries, upstream, key_values, lengths, key, head):
    seqs, chunk, width = queries.shape
    count = key_values.shape[0]
    total = count * chunk
    whole = lambda s, *_: (0, s, 0, 0)
    local = pl.BlockSpec((1, chunk, width), lambda s, *_: (s, 0, 0))
    return pl.pallas_call(
        second_kernel,
        grid_spec=pltpu.PrefetchScalarGridSpec(
            num_scalar_prefetch=2,
            grid=(seqs,),
            in_specs=[local, local, pl.BlockSpec((count, 1, chunk, 2 * head), whole)],
            out_specs=[local, pl.BlockSpec((count, 1, chunk, 2 * head), whole)],
            scratch_shapes=[
                pltpu.VMEM((total, head), BF),
                pltpu.VMEM((total, head), BF),
                pltpu.VMEM((head, total), BF),
                pltpu.VMEM((total, head), F32),
                pltpu.VMEM((total, head), F32),
            ],
        ),
        out_shape=[
            jax.ShapeDtypeStruct(queries.shape, BF),
            jax.ShapeDtypeStruct(key_values.shape, F32),
        ],
        compiler_params=pltpu.CompilerParams(vmem_limit_bytes=VMEM_BYTES),
        cost_estimate=LIGHT,
    )(lengths, key, queries, upstream, key_values)


def backward_kernel(
    lengths_ref,
    key_ref,
    q_ref,
    up_ref,
    attn_ref,
    kv_ref,
    lse_ref,
    more_ref,
    cos_ref,
    sin_ref,
    grads_ref,
    keys,
    values,
    keys_t,
    dk,
    dv,
):
    count, _, chunk, width = q_ref.shape
    head = keys.shape[1]
    total = keys.shape[0]
    block = min(QUERY_ROWS, total)
    per_block = block // chunk
    key = key_ref[0]
    length = lengths_ref[pl.program_id(0)]
    scale = 1.0 / math.sqrt(head)
    load_keys(key, kv_ref, keys, count, head, 0)
    load_keys(key, kv_ref, values, count, head, 1)
    transpose_rows(keys, keys_t)
    for place in range(count):
        rows = slice(place * chunk, (place + 1) * chunk)
        dk[rows, :] = more_ref[place ^ key, 0, :, :head]
        dv[rows, :] = more_ref[place ^ key, 0, :, head:]
    for start in range(0, total, block):
        limit_row = start + lax.broadcasted_iota(jnp.int32, (1, block), 1)
        limit = jnp.minimum(limit_row, length - 1)
        seen = start + block
        places = [(start // chunk + i) ^ key for i in range(per_block)]
        for h in range(width // head):
            columns = slice(h * head, (h + 1) * head)
            queries = jnp.concatenate([q_ref[p, 0, :, columns] for p in places], 0)
            upstream = jnp.concatenate([up_ref[p, 0, :, columns] for p in places], 0)
            attn = jnp.concatenate([attn_ref[p, 0, :, columns] for p in places], 0)
            centre = jnp.sum((upstream.astype(F32) * attn.astype(F32)).T, 0, keepdims=True)
            scores = masked_scores(keys[:seen, :], queries, limit)
            probs = jnp.exp(scores - lse_ref[0, h : h + 1, start : start + block])
            d_probs = dot_nt(values[:seen, :], upstream)
            d_scores = (probs * (d_probs - centre)).astype(BF)
            d_queries = dot_nn(keys_t[:, :seen], d_scores).T.astype(BF).astype(F32) * scale
            span = slice(start, start + block)
            d_queries = (
                d_queries * cos_ref[span, :]
                - pltpu.roll(d_queries, head // 2, 1) * sin_ref[span, :]
            ).astype(BF)
            for i, p in enumerate(places):
                grads_ref[p, 0, :, columns] = d_queries[i * chunk : (i + 1) * chunk]
            dk[:seen, :] += dot_nn(d_scores, queries)
            dv[:seen, :] += dot_nn(probs.astype(BF), upstream)
    for place in range(count):
        rows = slice(place * chunk, (place + 1) * chunk)
        turned = dk[rows, :] * cos_ref[rows, :] - pltpu.roll(dk[rows, :], head // 2, 1) * sin_ref[rows, :]
        grads_ref[place ^ key, 0, :, width : width + head] = turned.astype(BF)
        grads_ref[place ^ key, 0, :, width + head :] = dv[rows, :].astype(BF)


def attend_backward(queries, upstream, attn, key_values, lse, more, tables, lengths, key, head):
    count, seqs, chunk, width = queries.shape
    total = count * chunk
    heads = width // head
    whole = lambda s, *_: (0, s, 0, 0)
    by_head = pl.BlockSpec((count, 1, chunk, width), whole)
    shared = pl.BlockSpec((count, 1, chunk, 2 * head), whole)
    return pl.pallas_call(
        backward_kernel,
        grid_spec=pltpu.PrefetchScalarGridSpec(
            num_scalar_prefetch=2,
            grid=(seqs,),
            in_specs=[
                by_head,
                by_head,
                by_head,
                shared,
                pl.BlockSpec((1, heads, total), lambda s, *_: (s, 0, 0)),
                shared,
                pl.BlockSpec((total, head), lambda s, *_: (0, 0)),
                pl.BlockSpec((total, head), lambda s, *_: (0, 0)),
            ],
            out_specs=pl.BlockSpec((count, 1, chunk, width + 2 * head), whole),
            scratch_shapes=[
                pltpu.VMEM((total, head), BF),
                pltpu.VMEM((total, head), BF),
                pltpu.VMEM((head, total), BF),
                pltpu.VMEM((total, head), F32),
                pltpu.VMEM((total, head), F32),
            ],
        ),
        out_shape=jax.ShapeDtypeStruct((count, seqs, chunk, width + 2 * head), BF),
        compiler_params=pltpu.CompilerParams(vmem_limit_bytes=VMEM_BYTES),
        cost_estimate=LIGHT,
    )(lengths, key, queries, upstream, attn, key_values, lse, more, *tables)


def front_kernel(key_ref, a_ref, b_ref, gain_ref, wq_ref, wkv_ref, cos_ref, sin_ref, *rest, first):
    na_ref, nb_ref, q_ref, kv_ref = rest[-4:]
    _, seqs, chunk, width = q_ref.shape
    head = kv_ref.shape[3] // 2
    scale = 1.0 / math.sqrt(head)
    for i, piece in enumerate((a_ref, b_ref)):
        inputs = piece[...].astype(F32)
        normed = (
            inputs
            * lax.rsqrt(jnp.mean(inputs * inputs, -1, keepdims=True) + EPSILON)
            * gain_ref[...]
        ).astype(BF)
        (na_ref, nb_ref)[i][...] = normed
        q_linear = dot_nn(normed, wq_ref[...])
        kv_linear = dot_nn(normed, wkv_ref[...])
        span = pl.ds(pl.multiple_of(((first + i) ^ key_ref[0]) * chunk, chunk), chunk)
        cosine, sine = cos_ref[span, :], sin_ref[span, :]
        turn = lambda v: v * cosine + pltpu.roll(v, head // 2, 1) * sine
        for s in range(seqs):
            rows = slice(s * chunk, (s + 1) * chunk)
            for h in range(width // head):
                columns = slice(h * head, (h + 1) * head)
                q_ref[i, s, :, columns] = (turn(q_linear[rows, columns]) * scale).astype(BF)
            kv_ref[i, s, :, :head] = turn(kv_linear[rows, :head]).astype(BF)
            kv_ref[i, s, :, head:] = kv_linear[rows, head:].astype(BF)


def whole_spec(array):
    return pl.BlockSpec(array.shape, lambda *_: (0,) * array.ndim)


def pair_spec(shape, pair):
    return pl.BlockSpec((2, *shape[1:]), lambda *_: (pair,) + (0,) * (len(shape) - 1))


def front_pair(key, pieces, pair, gain, wq, wkv, tables, seqs, count, before):
    rows, width = pieces[0].shape
    chunk = rows // seqs
    shapes = [
        (count, seqs, chunk, wq.shape[1]),
        (count, seqs, chunk, wkv.shape[1]),
    ]
    given = [*pieces, gain, wq, wkv, *tables]
    return pl.pallas_call(
        functools.partial(front_kernel, first=2 * pair),
        grid_spec=pltpu.PrefetchScalarGridSpec(
            num_scalar_prefetch=1,
            grid=(1,),
            in_specs=[whole_spec(a) for a in given] + [pl.BlockSpec(memory_space=pl.ANY)] * len(before),
            out_specs=[whole_spec(pieces[0])] * 2 + [pair_spec(shape, pair) for shape in shapes],
        ),
        out_shape=[jax.ShapeDtypeStruct((rows, width), BF)] * 2
        + [jax.ShapeDtypeStruct(shape, BF) for shape in shapes],
        input_output_aliases={1 + len(given) + i: 2 + i for i in range(len(before))},
        compiler_params=pltpu.CompilerParams(vmem_limit_bytes=VMEM_BYTES),
        cost_estimate=LIGHT,
    )(key, *given, *before)


def hidden_kernel(*refs, first, pairs):
    pieces, (shares_hbm, down_hbm) = refs[: 4 * pairs], refs[4 * pairs : 4 * pairs + 2]
    hidden_hbm, dgate_hbm, dup_hbm = refs[-11:-8]
    normed, branch, both, down, hidden, dgate, dup, sems = refs[-8:]
    rows = pieces[0].shape[0]
    lines, inner = shares_hbm.shape[0], down_hbm.shape[0]
    used = 0

    def copies(places):
        nonlocal used
        made = [pltpu.make_async_copy(a, b, sems.at[used + i]) for i, (a, b) in enumerate(places)]
        used += len(made)
        return made

    loads = copies([(shares_hbm.at[i], both.at[:, i]) for i in range(lines)])
    loads_normed, loads_branch, loads_down = [], [], []
    low, high = pl.ds(0, rows), pl.ds(rows, rows)
    for p in range(pairs):
        na, nb, ga, gb = pieces[4 * p : 4 * p + 4]
        loads_normed.append(copies([(na, normed.at[p, low]), (nb, normed.at[p, high])]))
        loads_branch.append(copies([(ga, branch.at[p, low]), (gb, branch.at[p, high])]))
        if p == 0:
            loads_down = copies([(down_hbm, down)])
    for load in [*loads, *loads_normed[0], *loads_branch[0], *loads_down]:
        load.start()
    for p in range(1, pairs):
        for load in [*loads_normed[p], *loads_branch[p]]:
            load.start()
    for load in loads:
        load.wait()
    stores = []
    for p in range(pairs):
        for load in loads_normed[p]:
            load.wait()
        gate_up = dot_nn(normed[p], both[...].reshape(-1, 2 * inner))
        gate_pre, up_pre = gate_up[:, :inner], gate_up[:, inner:]
        sigma = jax.nn.sigmoid(gate_pre)
        silu_gate = gate_pre * sigma
        slope = sigma * (1.0 + gate_pre * (1.0 - sigma))
        for load in [*loads_branch[p], *(loads_down if p == 0 else [])]:
            load.wait()
        grad_hidden = dot_nt(branch[p], down[...])
        hidden[p] = (silu_gate * up_pre).astype(BF)
        dgate[p] = (grad_hidden * up_pre * slope).astype(BF)
        dup[p] = (grad_hidden * silu_gate).astype(BF)
        places = []
        for stack, target in ((hidden, hidden_hbm), (dgate, dgate_hbm), (dup, dup_hbm)):
            places += [(stack.at[p, low], target.at[first + 2 * p])]
            places += [(stack.at[p, high], target.at[first + 2 * p + 1])]
        stores += copies(places)
        for store in stores[-6:]:
            store.start()
    for store in stores:
        store.wait()


def hidden_pairs(normed, branch, first, shares, down, count, before):
    rows, width = normed[0].shape
    inner = down.shape[0]
    lines, _, share_rows, _ = shares.shape
    pairs = len(normed) // 2
    given = []
    for p in range(0, 2 * pairs, 2):
        given += [*normed[p : p + 2], *branch[p : p + 2]]
    given += [shares, down]
    anywhere = pl.BlockSpec(memory_space=pl.ANY)
    stacked = jax.ShapeDtypeStruct((count, rows, inner), BF)
    return pl.pallas_call(
        functools.partial(hidden_kernel, first=first, pairs=pairs),
        in_specs=[anywhere] * (len(given) + len(before)),
        out_specs=[anywhere] * 3,
        out_shape=[stacked] * 3,
        scratch_shapes=[pltpu.VMEM((pairs, 2 * rows, width), BF)] * 2
        + [pltpu.VMEM((count, lines, share_rows, 2 * inner), BF), pltpu.VMEM(down.shape, BF)]
        + [pltpu.VMEM((pairs, 2 * rows, inner), BF)] * 3
        + [pltpu.SemaphoreType.DMA((lines + 1 + 10 * pairs,))],
        input_output_aliases={len(given) + i: i for i in range(len(before))},
        compiler_params=pltpu.CompilerParams(vmem_limit_bytes=MLP_VMEM_BYTES),
        cost_estimate=pl.CostEstimate(
            flops=20 * pairs * rows * width * inner,
            bytes_accessed=6 * width * inner + 12 * pairs * rows * width,
            transcendentals=2 * pairs * rows * inner,
        ),
    )(*given, *before)


def mlp_parts_kernel(hidden_hbm, dgate_hbm, dup_hbm, shares_hbm, down_hbm, *rest, first):
    pa_hbm, pb_hbm, oa_hbm, ob_hbm = rest[:4]
    hidden, dgate, dup, both, down, parts, outs, sems = rest[4:]
    rows = pa_hbm.shape[0]
    lines, inner = shares_hbm.shape[0], down_hbm.shape[0]
    low, high = pl.ds(0, rows), pl.ds(rows, rows)
    both_stacks = ((dgate_hbm, dgate), (dup_hbm, dup), (hidden_hbm, hidden))
    places = [(stack.at[pl.ds(first, 2)], target) for stack, target in both_stacks]
    places += [(shares_hbm.at[i], both.at[:, i]) for i in range(lines)]
    places += [(down_hbm, down)]
    loads = [pltpu.make_async_copy(a, b, sems.at[i]) for i, (a, b) in enumerate(places)]
    places = [(parts.at[low], pa_hbm), (parts.at[high], pb_hbm)]
    places += [(outs.at[low], oa_hbm), (outs.at[high], ob_hbm)]
    stores = [
        pltpu.make_async_copy(a, b, sems.at[len(loads) + i]) for i, (a, b) in enumerate(places)
    ]
    for load in loads:
        load.start()
    for load in loads[: lines + 3]:
        load.wait()
    both_cols = both[...].reshape(-1, 2 * inner)
    for i in range(2):
        grads = dot_nt(jnp.concatenate([dgate[i], dup[i]], 1), both_cols)
        parts[i * rows : (i + 1) * rows, :] = grads.astype(BF)
        stores[i].start()
    loads[-1].wait()
    for i in range(2):
        outs[i * rows : (i + 1) * rows, :] = dot_nn(hidden[i], down[...]).astype(BF)
        stores[2 + i].start()
    for store in stores:
        store.wait()


def mlp_parts(stacks, pair, shares, down):
    count, rows, inner = stacks[0].shape
    width = down.shape[1]
    lines, _, share_rows, _ = shares.shape
    anywhere = pl.BlockSpec(memory_space=pl.ANY)
    apart = jax.ShapeDtypeStruct((rows, width), BF)
    return pl.pallas_call(
        functools.partial(mlp_parts_kernel, first=2 * pair),
        in_specs=[anywhere] * 5,
        out_specs=[anywhere] * 4,
        out_shape=[apart] * 4,
        scratch_shapes=[pltpu.VMEM((2, rows, inner), BF)] * 3
        + [pltpu.VMEM((count, lines, share_rows, 2 * inner), BF), pltpu.VMEM(down.shape, BF)]
        + [pltpu.VMEM((2 * rows, width), BF)] * 2
        + [pltpu.SemaphoreType.DMA((lines + 8,))],
        compiler_params=pltpu.CompilerParams(vmem_limit_bytes=MLP_VMEM_BYTES),
        cost_estimate=pl.CostEstimate(
            flops=20 * rows * width * inner,
            bytes_accessed=6 * width * inner + 12 * rows * width,
            transcendentals=0,
        ),
    )(*stacks, shares, down)


def proj_kernel(a_ref, b_ref, w_ref, attn_ref, *rest, last):
    dattn_ref, total_ref = rest[-2:]
    seqs, chunk = attn_ref.shape[1:3]
    total = None if len(rest) == 2 else rest[1][...]
    for i, piece in enumerate((a_ref, b_ref)):
        grads = piece[...]
        d_attn = dot_nt(grads, w_ref[...]).astype(BF)
        for s in range(seqs):
            rows = slice(s * chunk, (s + 1) * chunk)
            dattn_ref[i, s] = d_attn[rows]
            share = dot_tn(attn_ref[i, s], grads[rows])
            total = share if total is None else total + share
    total_ref[...] = total.astype(total_ref.dtype)


def proj_pair(pieces, pair, w_out, attn, count, before):
    last = 2 * pair + 2 == count
    rows, width = pieces[0].shape
    given = [*pieces, w_out]
    extra_specs = []
    aliases = {}
    if before:
        extra_specs = [pl.BlockSpec(memory_space=pl.ANY), whole_spec(before[1])]
        aliases = {4: 0} if last else {4: 0, 5: 1}
    total = jax.ShapeDtypeStruct(w_out.shape, BF if last else F32)
    return pl.pallas_call(
        functools.partial(proj_kernel, last=last),
        grid=(1,),
        in_specs=[whole_spec(a) for a in given] + [pair_spec(attn.shape, pair)] + extra_specs,
        out_specs=[pair_spec(attn.shape, pair), whole_spec(total)],
        out_shape=[jax.ShapeDtypeStruct(attn.shape, BF), total],
        input_output_aliases=aliases,
        compiler_params=pltpu.CompilerParams(vmem_limit_bytes=VMEM_BYTES),
        cost_estimate=LIGHT,
    )(*given, attn, *before)


def parts_kernel(*refs, count, turned):
    lefts, weights = refs[: len(turned)], refs[len(turned) : 2 * len(turned)]
    outs, (buffer, sems) = refs[2 * len(turned) : -2], refs[-2:]
    order = (6, 7, 2, 3, 4, 5, 0, 1) if count == 8 else range(count)
    stores = []
    for j in order:
        total = None
        for left, weight, turn in zip(lefts, weights, turned):
            share = (dot_nt if turn else dot_nn)(left[j], weight[...])
            total = share if total is None else total + share
        buffer[j] = total.astype(BF)
        stores.append(pltpu.make_async_copy(buffer.at[j], outs[j], sems.at[j]))
        stores[-1].start()
    for store in stores:
        store.wait()


def parts_of(lefts, weights, turned):
    count, rows = lefts[0].shape[:2]
    width = weights[0].shape[0 if turned[0] else 1]
    return pl.pallas_call(
        functools.partial(parts_kernel, count=count, turned=turned),
        grid=(1,),
        in_specs=[whole_spec(a) for a in (*lefts, *weights)],
        out_specs=[pl.BlockSpec(memory_space=pl.ANY)] * count,
        out_shape=[jax.ShapeDtypeStruct((rows, width), BF)] * count,
        scratch_shapes=[
            pltpu.VMEM((count, rows, width), BF),
            pltpu.SemaphoreType.DMA((count,)),
        ],
        compiler_params=pltpu.CompilerParams(vmem_limit_bytes=VMEM_BYTES),
        cost_estimate=LIGHT,
    )(*lefts, *weights)


def outer_kernel(*refs, count, rights):
    left = jnp.concatenate([ref[...] for ref in refs[:count]], 0)
    left_t = left.T
    for right, out in zip(refs[count : count + rights], refs[count + rights :]):
        out[...] = dot_nn(left_t, right[...]).astype(BF)


def outer_of(pieces, rights):
    count = len(pieces)
    rows, width = pieces[0].shape
    step = min(256, width)
    return pl.pallas_call(
        functools.partial(outer_kernel, count=count, rights=len(rights)),
        grid=(width // step,),
        in_specs=[pl.BlockSpec((rows, step), lambda i: (0, i))] * count
        + [pl.BlockSpec(right.shape, lambda i: (0, 0)) for right in rights],
        out_specs=[pl.BlockSpec((step, right.shape[1]), lambda i: (i, 0)) for right in rights],
        out_shape=[jax.ShapeDtypeStruct((width, right.shape[1]), BF) for right in rights],
        compiler_params=pltpu.CompilerParams(vmem_limit_bytes=VMEM_BYTES),
        cost_estimate=LIGHT,
    )(*pieces, *rights)


def inner_kernel(*refs, count, lefts):
    pieces = refs[lefts : lefts + count]
    outs, lefts_t = refs[lefts + count : 2 * lefts + count], refs[2 * lefts + count :]
    rows = pieces[0].shape[0]

    @pl.when(pl.program_id(0) == 0)
    def _():
        for left, left_t in zip(refs[:lefts], lefts_t):
            for j in range(count):
                span = slice(j * rows, (j + 1) * rows)
                left_t[:, span] = left[span, :].T

    right = jnp.concatenate([piece[...] for piece in pieces], 0)
    for out, left_t in zip(outs, lefts_t):
        out[...] = dot_nn(left_t[...], right).astype(BF)


def inner_of(lefts, pieces):
    count = len(pieces)
    rows, width = pieces[0].shape
    step = min(256, width)
    columns = lefts[0].shape[1]
    return pl.pallas_call(
        functools.partial(inner_kernel, count=count, lefts=len(lefts)),
        grid=(width // step,),
        in_specs=[pl.BlockSpec(left.shape, lambda i: (0, 0)) for left in lefts]
        + [pl.BlockSpec((rows, step), lambda i: (0, i))] * count,
        out_specs=[pl.BlockSpec((columns, step), lambda i: (0, i))] * len(lefts),
        out_shape=[jax.ShapeDtypeStruct((columns, width), BF)] * len(lefts),
        scratch_shapes=[pltpu.VMEM((columns, count * rows), BF)] * len(lefts),
        compiler_params=pltpu.CompilerParams(vmem_limit_bytes=VMEM_BYTES),
        cost_estimate=LIGHT,
    )(*lefts, *pieces)


def widen_kernel(query_ref, out_ref, small_ref, query_f, out_f, key_f, value_f, gains_f):
    width, head = query_ref.shape[2], key_f.shape[1]
    for j in range(query_ref.shape[0]):
        query_f[:, j * width : (j + 1) * width] = query_ref[j].astype(F32)
    out_f[...] = out_ref[...].astype(F32)
    rows = key_f.shape[0]
    key_f[...] = small_ref[:rows, :head].astype(F32)
    value_f[...] = small_ref[:rows, head:].astype(F32)
    gains_f[...] = small_ref[rows:, :].astype(F32)


def widen(query_blocks, out_sum, small, head):
    count, rows, width = query_blocks.shape
    shapes = [(rows, count * width), out_sum.shape, (rows, head), (rows, head)]
    shapes = [jax.ShapeDtypeStruct(shape, F32) for shape in (*shapes, (small.shape[0] - rows, 2 * head))]
    given = [query_blocks, out_sum, small]
    return pl.pallas_call(
        widen_kernel,
        grid=(1,),
        in_specs=[whole_spec(a) for a in given],
        out_specs=[whole_spec(a) for a in shapes],
        out_shape=shapes,
        compiler_params=pltpu.CompilerParams(vmem_limit_bytes=VMEM_BYTES),
        cost_estimate=LIGHT,
    )(*given)


def turn_kernel(blocks_ref, out_ref):
    turned = [blocks_ref[j].astype(F32).T for j in range(blocks_ref.shape[0])]
    out_ref[...] = jnp.concatenate(turned, 1)


def turn_blocks(blocks):
    count, columns, rows = blocks.shape
    step = min(128, rows)
    return pl.pallas_call(
        turn_kernel,
        grid=(rows // step,),
        in_specs=[pl.BlockSpec((count, columns, step), lambda i: (0, 0, i))],
        out_specs=pl.BlockSpec((step, count * columns), lambda i: (i, 0)),
        out_shape=jax.ShapeDtypeStruct((rows, count * columns), F32),
        compiler_params=pltpu.CompilerParams(vmem_limit_bytes=VMEM_BYTES),
        cost_estimate=LIGHT,
    )(blocks)


def spread_rows(share_t, count):
    columns, rows = share_t.shape
    blocks = share_t.reshape(columns, count, rows // count).transpose(1, 0, 2)
    return lax.all_to_all(blocks, "seq", split_axis=0, concat_axis=0, tiled=True)


def pack_kernel(place_ref, gate_hbm, up_hbm, out_ref, gate_ref, up_ref, sems):
    count, rows, _ = out_ref.shape
    inner = gate_ref.shape[1] // count
    span = pl.ds(pl.multiple_of(place_ref[0] * rows, rows), rows)
    loads = [
        pltpu.make_async_copy(gate_hbm.at[span], gate_ref, sems.at[0]),
        pltpu.make_async_copy(up_hbm.at[span], up_ref, sems.at[1]),
    ]
    for load in loads:
        load.start()
    for load in loads:
        load.wait()
    gate, up = gate_ref[...], up_ref[...]
    for j in range(count):
        columns = slice(j * inner, (j + 1) * inner)
        out_ref[j] = jnp.concatenate([gate[:, columns], up[:, columns]], 1)


def pack_weights(w_gate, w_up, count):
    lines = lax.axis_size("dp")
    rows, columns = w_gate.shape[0] // lines, w_gate.shape[1]
    place = lax.axis_index("dp").astype(jnp.int32).reshape(1)
    anywhere = pl.BlockSpec(memory_space=pl.ANY)
    shape = (count, rows, 2 * columns // count)
    return pl.pallas_call(
        pack_kernel,
        grid_spec=pltpu.PrefetchScalarGridSpec(
            num_scalar_prefetch=1,
            grid=(1,),
            in_specs=[anywhere, anywhere],
            out_specs=pl.BlockSpec(shape, lambda i, place: (0, 0, 0)),
            scratch_shapes=[
                pltpu.VMEM((rows, columns), BF),
                pltpu.VMEM((rows, columns), BF),
                pltpu.SemaphoreType.DMA((2,)),
            ],
        ),
        out_shape=jax.ShapeDtypeStruct(shape, BF),
        compiler_params=pltpu.CompilerParams(vmem_limit_bytes=VMEM_BYTES),
        cost_estimate=LIGHT,
    )(place, w_gate, w_up)


def share_weights(w_gate, w_up, w_query, count):
    packed = pack_weights(w_gate, w_up, count)
    packed = lax.all_to_all(packed, "seq", split_axis=0, concat_axis=0, tiled=True)
    query = rows_to_columns(w_query + packed[0, 0, 0] * 0)
    return query, lax.all_gather(packed, "dp", axis=0, tiled=False)


def rope_tables(positions, head_width):
    half_width = head_width // 2
    spacing = jnp.exp(
        jnp.arange(half_width).astype(F32) * (-2.0 * math.log(10000.0) / head_width)
    )
    angles = positions.astype(F32)[:, None] * spacing[None, :]
    sines = jnp.sin(angles)
    cosines = jnp.cos(angles)
    return (jnp.concatenate([cosines, cosines], 1), jnp.concatenate([-sines, sines], 1))


def rms_scale(values_in):
    return lax.rsqrt(jnp.mean(values_in * values_in, -1, keepdims=True) + EPSILON)


def norm_back(grad_normed, inputs, scale_rows, gain):
    weighted = grad_normed * gain
    cubed = scale_rows * scale_rows * scale_rows
    return scale_rows * weighted - inputs * cubed * jnp.mean(weighted * inputs, -1, keepdims=True)


def body(
    tokens,
    lengths,
    second_queries,
    cotangent,
    second_cotangent,
    gain_attn,
    w_query,
    w_key,
    w_value,
    w_out,
    gain_mlp,
    w_gate,
    w_up,
    w_down,
):
    count = lax.axis_size("seq")
    rank = lax.axis_index("seq")
    key = order_key(count)
    keys_of = jnp.stack([key, rank]).astype(jnp.int32)
    seqs, chunk, width = tokens.shape
    head = w_key.shape[1]
    rows = seqs * chunk
    all_rows = count * rows
    own_columns = w_query.shape[0]

    query_cols, shares = share_weights(w_gate, w_up, w_query, count)
    gain_rows = jnp.zeros((16, 2 * head), BF)
    gain_rows = gain_rows.at[:2, :own_columns].set(jnp.stack([gain_attn, gain_mlp]))
    packed = jnp.concatenate([jnp.concatenate([w_key, w_value], 1), gain_rows], 0)
    packed = gather_ordered(packed, count)
    kv_mat = packed[:, :own_columns].reshape(width, 2 * head)
    gain_one = packed[:, own_columns, :own_columns].reshape(1, width).astype(F32)
    gain_two = packed[:, own_columns + 1, :own_columns].reshape(1, width).astype(F32)

    local_pos = rank * chunk + jnp.arange(chunk, dtype=jnp.int32)
    valid = (local_pos[None, :] < lengths[:, None]).astype(F32).reshape(rows, 1)
    tables = rope_tables(jnp.arange(count * chunk, dtype=jnp.int32), head)

    last_pair = count // 2 - 1
    inputs = tokens.reshape(rows, width)
    front_of = lambda pair, two, before: front_pair(
        keys_of, two, pair, gain_one, query_cols, kv_mat, tables, seqs, count, before
    )
    near = gather_near(inputs, count)
    normed_one = []
    stacks = []
    far = gather_far(near, count)
    for pair in range(last_pair):
        *normed, queries, key_values = front_of(pair, near[2 * pair : 2 * pair + 2], stacks)
        normed_one += normed
        stacks = [queries, key_values]
    last = gather_last(near, far, count)
    grad_out = cotangent.reshape(rows, width).astype(F32) * valid
    branch_near = gather_near(after(grad_out.astype(BF), far), count, stacks)
    branch_far = gather_far(after(branch_near, stacks), count)
    *normed, queries, key_values = front_of(last_pair, [far, last], stacks)
    normed_one += normed
    attn, lse = attend_forward(queries, key_values, lengths, keys_of, head)
    attn, branch_far = lax.optimization_barrier((attn, branch_far))
    proj_parts = parts_of([attn.reshape(count, rows, -1)], [w_out], (False,))
    inputs_f = inputs.astype(F32)
    scale_one = rms_scale(inputs_f)

    branch_last = gather_last(branch_near, branch_far, count)
    branch = (branch_near if is_cube(count) else branch_near[:-2]) + [branch_far, branch_last]
    grad_second, dkv_second = attend_second(
        after(second_queries, proj_parts), second_cotangent, key_values, lengths, keys_of, head
    )
    proj_sum = scatter_pieces(proj_parts, count, dkv_second)
    proj_sum, shares = lax.optimization_barrier((proj_sum, shares))
    middle = inputs_f + proj_sum.astype(F32)

    scale_two = rms_scale(middle)
    sync = lax.optimization_barrier
    always = lengths[0] > 0
    hidden_of = lambda first, pieces, before: tuple(
        hidden_pairs(pieces, branch[first : first + len(pieces)], first, shares, w_down, count, before)
    )
    normed_own = (middle * scale_two * gain_two).astype(BF)

    def middle_pairs(near, stacks):
        for first in range(2, 2 * last_pair, 4):
            stacks = hidden_of(first, near[first : min(first + 4, 2 * last_pair)], stacks)
        return tuple(stacks)

    if is_cube(count):
        from_x, from_y, from_core = swap(normed_own, 2), swap(normed_own, 4), swap(normed_own, 1)
        stacks = stage(always, lambda *two: hidden_of(0, two, []), normed_own, from_core)
        from_x, from_y, stacks = sync((from_x, from_y, stacks))
        near = [normed_own, from_core, from_x, swap(from_x, 1), from_y, swap(from_y, 1)]
        halves = far_halves(near)
        stacks = stage(always, middle_pairs, near, stacks)
        halves, stacks = sync((halves, stacks))
        far = jnp.concatenate(halves, 0)
        last = swap(far, 1)
    else:
        near = gather_near(normed_own, count)
        stacks = middle_pairs(near, hidden_of(0, near[:2], []))
        far, last = near[-2:]
    stacks = hidden_of(2 * last_pair, [far, last], list(stacks))
    hidden, grad_gate, grad_up = [stack.reshape(all_rows, -1) for stack in stacks]
    normed_two = (near if is_cube(count) else near[:-2]) + [far, last]
    split = queries.shape[-1]
    (w_gate_share,) = inner_of([grad_gate], normed_two)
    gate_sum = lax.psum(w_gate_share, "dp")

    def parts_mlp(stacks):
        parts = [mlp_parts(stacks, pair, shares, w_down) for pair in range(last_pair + 1)]
        normed_parts = [part for step in parts for part in step[:2]]
        return normed_parts, [part for step in parts for part in step[2:]]

    normed_parts, out_parts = stage(always, parts_mlp, stacks)

    def scatter_mlp(normed_parts, hidden):
        return scatter_far(normed_parts, count), inner_of([hidden], branch)[0]

    two_sums, w_down_share = stage(always, scatter_mlp, normed_parts, hidden)
    def sum_mlp(two_sums, grad_up):
        (w_up_share,) = inner_of([grad_up], normed_two)
        grad_normed_two = scatter_near(two_sums, count, w_up_share).astype(F32)
        grad_middle = grad_out + norm_back(grad_normed_two, middle, scale_two, gain_two)
        return grad_middle, jnp.sum(grad_normed_two * (middle * scale_two), 0), w_up_share

    grad_middle, gain_share, w_up_share = stage(always, sum_mlp, two_sums, grad_up)
    grad_middle, w_up_share, w_down_share, gate_sum = sync(
        (grad_middle, w_up_share, w_down_share, gate_sum)
    )
    up_sum, down_sum = lax.psum((w_up_share, w_down_share), "dp")
    proj_of = lambda pair, two, before: proj_pair(two, pair, w_out, attn, count, before)

    def gather_middle(grad_middle):
        near = gather_near(grad_middle.astype(BF), count)
        return near, proj_of(0, near[:2], [])

    near, state = stage(always, gather_middle, grad_middle)

    def project_back(near, state):
        far = gather_far(near, count)
        for pair in range(1, last_pair):
            state = proj_of(pair, near[2 * pair : 2 * pair + 2], state)
        last = gather_last(near, far, count)
        return proj_of(last_pair, [far, last], state)

    grad_attn, w_out_share = stage(always, project_back, near, state)
    grad_attn, gate_sum = sync((grad_attn, gate_sum))
    gate_blocks = spread_rows(gate_sum, count)

    def attention_back(grad_attn, out_parts):
        out_sums = scatter_far(out_parts, count)
        grads = attend_backward(
            queries, grad_attn, attn, key_values, lse, dkv_second, tables, lengths, keys_of, head
        )
        grads = grads.reshape(count, rows, -1)
        one_parts = parts_of(
            [grads[..., :split], grads[..., split:]], [query_cols, kv_mat], (True, True)
        )
        (w_one_share,) = outer_of(normed_one, [grads.reshape(all_rows, -1)])
        return out_sums, one_parts, w_one_share

    out_sums, one_parts, w_one_share = stage(always, attention_back, grad_attn, out_parts)
    one_parts, w_one_share, gate_blocks = sync((one_parts, w_one_share, gate_blocks))
    w_query_share = w_one_share[:, :split].reshape(count, own_columns, split)
    w_query_share = lax.all_to_all(w_query_share, "seq", split_axis=0, concat_axis=0, tiled=True)
    own_gain = gain_attn.shape[0]

    def scatter_attention(one_parts, w_one_share):
        kv_shares = w_one_share[:, split:].reshape(count, own_columns, 2 * head)
        return scatter_far(one_parts, count), small_scatter(kv_shares, count)

    one_sums, w_kv_share = stage(always, scatter_attention, one_parts, w_one_share)

    def sum_attention(one_sums, w_kv_share):
        grad_normed_one = scatter_near(one_sums, count).astype(F32)
        grad_tokens = grad_middle + norm_back(grad_normed_one, inputs_f, scale_one, gain_one)
        gain_shares = jnp.stack([jnp.sum(grad_normed_one * (inputs_f * scale_one), 0), gain_share])
        gain_shares = gain_shares.astype(BF).reshape(2, count, own_gain).transpose(1, 0, 2)
        gain_shares = jnp.pad(gain_shares, ((0, 0), (0, 14), (0, 2 * head - own_gain)))
        small = jnp.concatenate([w_kv_share, small_scatter(gain_shares, count)], 0)
        return grad_tokens, small

    grad_tokens, small = stage(always, sum_attention, one_sums, w_kv_share)
    small, w_query_share, w_out_share, up_sum, down_sum = sync(
        (small, w_query_share, w_out_share, up_sum, down_sum)
    )
    late = lax.psum((w_out_share, w_query_share.reshape(-1, split), small), "dp")

    def sum_rest(out_sums, gate_blocks, down_sum, up_sum):
        up_blocks = spread_rows(up_sum, count)
        out = (middle + scatter_near(out_sums, count).astype(F32)).astype(BF)
        return out, turn_blocks(gate_blocks), turn_blocks(up_blocks), down_sum.astype(F32)

    out, grad_w_gate, grad_w_up, grad_w_down = stage(
        always, sum_rest, out_sums, gate_blocks, down_sum, up_sum
    )
    late, grad_w_up = sync((late, grad_w_up))
    w_out_sum, w_query_sum, small = late
    grad_w_query, w_out_sum, grad_w_key, grad_w_value, grad_gains = widen(
        w_query_sum.reshape(count, own_columns, split), w_out_sum, small, head
    )

    return (
        out.reshape(tokens.shape),
        grad_tokens.reshape(tokens.shape),
        grad_second,
        grad_gains[0, :own_gain],
        grad_w_query,
        grad_w_key,
        grad_w_value,
        w_out_sum.astype(F32),
        grad_gains[1, :own_gain],
        grad_w_gate,
        grad_w_up,
        grad_w_down,
    )


def solution(mesh):
    return jax.shard_map(
        body,
        mesh=mesh,
        in_specs=(
            P("dp", "seq", None),
            P("dp"),
            P("dp", "seq", None),
            P("dp", "seq", None),
            P("dp", "seq", None),
            P("seq"),
            P("seq", None),
            P("seq", None),
            P("seq", None),
            P("seq", None),
            P("seq"),
            P("seq", None),
            P("seq", None),
            P("seq", None),
        ),
        out_specs=(
            P("dp", "seq", None),
            P("dp", "seq", None),
            P("dp", "seq", None),
            P("seq"),
            P("seq", None),
            P("seq", None),
            P("seq", None),
            P("seq", None),
            P("seq"),
            P("seq", None),
            P("seq", None),
            P("seq", None),
        ),
        check_vma=False,
    )
```

```python
import functools
import math

import jax
import jax.numpy as jnp
from jax import lax
from jax.experimental import pallas as pl
from jax.experimental.pallas import tpu as pltpu
from jax.sharding import PartitionSpec as P

EPSILON = 1e-05
BF = jnp.bfloat16
F32 = jnp.float32
QUERY_ROWS = 256
VMEM_BYTES = 32 * 1024 * 1024
LIGHT = pl.CostEstimate(flops=1000, bytes_accessed=1000, transcendentals=0)
MLP_VMEM_BYTES = 48 * 1024 * 1024


def dot_nn(left, right):
    return jnp.dot(left, right, preferred_element_type=F32)


def dot_nt(left, right):
    return lax.dot_general(left, right, (((1,), (1,)), ((), ())), preferred_element_type=F32)


def dot_tn(left, right):
    return lax.dot_general(left, right, (((0,), (0,)), ((), ())), preferred_element_type=F32)


def is_cube(count):
    return count == 8


def order_key(count):
    rank = lax.axis_index("seq")
    return rank if is_cube(count) else jnp.zeros_like(rank)


def swap(array, bit):
    return lax.ppermute(array, "seq", [(i, i ^ bit) for i in range(8)])


def add_rounded(*terms):
    total = terms[0].astype(F32)
    for term in terms[1:]:
        total = total + term.astype(F32)
    return total.astype(BF)


def after(value, *others):
    return lax.optimization_barrier((value, others))[0]


def gather_near(piece, count, *between):
    if not is_cube(count):
        gathered = lax.all_gather(piece, "seq", axis=0, tiled=False)
        return [gathered[j] for j in range(count)]
    from_x = swap(piece, 2)
    from_y = swap(piece, 4)
    from_core = swap(piece, 1)
    from_x, from_y = after([from_x, from_y], *between)
    return [piece, from_core, from_x, swap(from_x, 1), from_y, swap(from_y, 1)]


def far_halves(near):
    half = near[0].shape[0] // 2
    return [swap(near[2][:half], 4), swap(near[4][half:], 2)]


def gather_far(near, count, *window):
    if not is_cube(count):
        return near[-2]
    return jnp.concatenate(after(far_halves(near), *window), 0)


def gather_last(near, far, count):
    return swap(far, 1) if is_cube(count) else near[-1]


def gather_pieces(piece, count):
    near = gather_near(piece, count)
    far = gather_far(near, count)
    last = gather_last(near, far, count)
    return (near if is_cube(count) else near[:-2]) + [far, last]


def scatter_far(parts, count, *window):
    if not is_cube(count):
        return parts
    half = parts[0].shape[0] // 2
    far = add_rounded(parts[6], swap(parts[7], 1))
    far_x = swap(far[:half], 2)
    far_y = swap(far[half:], 4)
    far_x, far_y = after([far_x, far_y], *window)
    near_x = add_rounded(parts[2], swap(parts[3], 1))
    near_y = add_rounded(parts[4], swap(parts[5], 1))
    near_y = jnp.concatenate([add_rounded(near_y[:half], far_x), near_y[half:]], 0)
    near_x = jnp.concatenate([near_x[:half], add_rounded(near_x[half:], far_y)], 0)
    own = add_rounded(parts[0], swap(parts[1], 1))
    return [own, near_x, near_y]


def scatter_near(sums, count, *window):
    if not is_cube(count):
        return lax.psum_scatter(jnp.stack(sums), "seq", scatter_dimension=0, tiled=False)
    own, near_x, near_y = sums
    got_x = swap(near_x, 2)
    got_y = swap(near_y, 4)
    return add_rounded(after(own, *window), got_x, got_y)


def scatter_pieces(parts, count, *window):
    return scatter_near(scatter_far(parts, count), count, *window)


def gather_ordered(piece, count):
    if not is_cube(count):
        return lax.all_gather(piece, "seq", axis=0, tiled=False)
    rank = lax.axis_index("seq")
    held = piece
    for bit in (4, 2, 1):
        other = swap(held, bit)
        upper = (rank & bit) != 0
        held = jnp.stack([jnp.where(upper, other, held), jnp.where(upper, held, other)])
    held = held.transpose(2, 1, 0, *range(3, held.ndim))
    return held.reshape(count, *piece.shape)


def rows_to_columns(weight):
    return lax.all_to_all(weight, "seq", split_axis=1, concat_axis=0, tiled=True)


def columns_to_rows(weight):
    return lax.all_to_all(weight, "seq", split_axis=0, concat_axis=1, tiled=True)


def stage(always, work, *operands):
    shapes = jax.eval_shape(work, *operands)
    empty = lambda *_: jax.tree.map(lambda leaf: jnp.zeros(leaf.shape, leaf.dtype), shapes)
    return lax.cond(always, work, empty, *operands)


def small_scatter(share, count):
    if not is_cube(count):
        return lax.psum_scatter(share, "seq", scatter_dimension=0, tiled=False)
    rank = lax.axis_index("seq")
    for bit in (1, 2, 4):
        upper = (rank & bit) != 0
        pairs = share.reshape(-1, 2, *share.shape[1:])
        low, high = pairs[:, 0], pairs[:, 1]
        share = add_rounded(jnp.where(upper, high, low), swap(jnp.where(upper, low, high), bit))
    return share[0]


def load_keys(key_ref, kv_ref, rows_ref, count, head, column):
    chunk = kv_ref.shape[2]
    for place in range(count):
        rows_ref[place * chunk : (place + 1) * chunk, :] = kv_ref[
            place ^ key_ref, 0, :, column * head : (column + 1) * head
        ]


def transpose_rows(rows_ref, turned_ref):
    step = 128
    for start in range(0, rows_ref.shape[0], step):
        turned_ref[:, start : start + step] = (
            rows_ref[start : start + step, :].astype(F32).T.astype(BF)
        )


def masked_scores(keys, queries, limit):
    scores = dot_nt(keys, queries)
    key_pos = lax.broadcasted_iota(jnp.int32, scores.shape, 0)
    return jnp.where(key_pos <= limit, scores, -jnp.inf)


def forward_kernel(
    lengths_ref, key_ref, q_ref, kv_ref, attn_ref, lse_ref, keys, values, values_t
):
    count, _, chunk, _ = q_ref.shape
    head = keys.shape[1]
    total = keys.shape[0]
    block = min(QUERY_ROWS, total)
    per_block = block // chunk
    key = key_ref[0]
    length = lengths_ref[pl.program_id(0)]
    load_keys(key, kv_ref, keys, count, head, 0)
    load_keys(key, kv_ref, values, count, head, 1)
    transpose_rows(values, values_t)
    for start in range(0, total, block):
        limit_row = start + lax.broadcasted_iota(jnp.int32, (1, block), 1)
        limit = jnp.minimum(limit_row, length - 1)
        seen = start + block
        places = [(start // chunk + i) ^ key for i in range(per_block)]
        for h in range(q_ref.shape[3] // head):
            columns = slice(h * head, (h + 1) * head)
            queries = jnp.concatenate([q_ref[p, 0, :, columns] for p in places], 0)
            scores = masked_scores(keys[:seen, :], queries, limit)
            top = jnp.max(scores, 0, keepdims=True)
            weights = jnp.exp(scores - top)
            norm = jnp.sum(weights, 0, keepdims=True)
            mixed = dot_nn(values_t[:, :seen], weights.astype(BF)) / norm
            rows = mixed.T.astype(BF)
            for i, p in enumerate(places):
                attn_ref[p, 0, :, columns] = rows[i * chunk : (i + 1) * chunk]
            lse_ref[0, h : h + 1, start : start + block] = top + jnp.log(norm)


def attend_forward(queries, key_values, lengths, key, head):
    count, seqs, chunk, width = queries.shape
    total = count * chunk
    heads = width // head
    whole = lambda s, *_: (0, s, 0, 0)
    return pl.pallas_call(
        forward_kernel,
        grid_spec=pltpu.PrefetchScalarGridSpec(
            num_scalar_prefetch=2,
            grid=(seqs,),
            in_specs=[
                pl.BlockSpec((count, 1, chunk, width), whole),
                pl.BlockSpec((count, 1, chunk, 2 * head), whole),
            ],
            out_specs=[
                pl.BlockSpec((count, 1, chunk, width), whole),
                pl.BlockSpec((1, heads, total), lambda s, *_: (s, 0, 0)),
            ],
            scratch_shapes=[
                pltpu.VMEM((total, head), BF),
                pltpu.VMEM((total, head), BF),
                pltpu.VMEM((head, total), BF),
            ],
        ),
        out_shape=[
            jax.ShapeDtypeStruct(queries.shape, BF),
            jax.ShapeDtypeStruct((seqs, heads, total), F32),
        ],
        compiler_params=pltpu.CompilerParams(vmem_limit_bytes=VMEM_BYTES),
        cost_estimate=LIGHT,
    )(lengths, key, queries, key_values)


def second_kernel(
    lengths_ref, key_ref, q_ref, up_ref, kv_ref, dq_ref, dkv_ref, keys, values, keys_t, dk, dv
):
    _, chunk, width = q_ref.shape
    count = kv_ref.shape[0]
    head = keys.shape[1]
    total = keys.shape[0]
    block = min(QUERY_ROWS, total)
    per_block = block // chunk
    key = key_ref[0]
    rank = key_ref[1]
    length = lengths_ref[pl.program_id(0)]
    load_keys(key, kv_ref, keys, count, head, 0)
    load_keys(key, kv_ref, values, count, head, 1)
    transpose_rows(keys, keys_t)
    dk[...] = jnp.zeros_like(dk)
    dv[...] = jnp.zeros_like(dv)
    own = rank * chunk + lax.broadcasted_iota(jnp.int32, (1, block), 1) % chunk
    limit = jnp.minimum(own, length - 1)
    live = rank * chunk + lax.broadcasted_iota(jnp.int32, (chunk, head), 0) < length
    def heads(turn, carry):
        starts = [(turn * per_block + i) * head for i in range(per_block)]
        spans = [pl.ds(pl.multiple_of(start, head), head) for start in starts]
        queries = jnp.concatenate([q_ref[0, :, s] for s in spans], 0)
        upstream = jnp.concatenate(
            [jnp.where(live, up_ref[0, :, s].astype(F32), 0.0).astype(BF) for s in spans], 0
        )
        scores = masked_scores(keys[...], queries, limit)
        weights = jnp.exp(scores - jnp.max(scores, 0, keepdims=True))
        probs = weights * (1.0 / jnp.sum(weights, 0, keepdims=True))
        product = probs * dot_nt(values[...], upstream)
        d_scores = (product - probs * jnp.sum(product, 0, keepdims=True)).astype(BF)
        d_queries = dot_nn(keys_t[...], d_scores).T.astype(BF)
        for i, s in enumerate(spans):
            dq_ref[0, :, s] = d_queries[i * chunk : (i + 1) * chunk]
        dk[...] += dot_nn(d_scores, queries)
        dv[...] += dot_nn(probs.astype(BF), upstream)
        return carry

    lax.fori_loop(0, width // head // per_block, heads, 0)
    for place in range(count):
        rows = slice(place * chunk, (place + 1) * chunk)
        dkv_ref[place ^ key, 0, :, :head] = dk[rows, :]
        dkv_ref[place ^ key, 0, :, head:] = dv[rows, :]


def attend_second(queries, upstream, key_values, lengths, key, head):
    seqs, chunk, width = queries.shape
    count = key_values.shape[0]
    total = count * chunk
    whole = lambda s, *_: (0, s, 0, 0)
    local = pl.BlockSpec((1, chunk, width), lambda s, *_: (s, 0, 0))
    return pl.pallas_call(
        second_kernel,
        grid_spec=pltpu.PrefetchScalarGridSpec(
            num_scalar_prefetch=2,
            grid=(seqs,),
            in_specs=[local, local, pl.BlockSpec((count, 1, chunk, 2 * head), whole)],
            out_specs=[local, pl.BlockSpec((count, 1, chunk, 2 * head), whole)],
            scratch_shapes=[
                pltpu.VMEM((total, head), BF),
                pltpu.VMEM((total, head), BF),
                pltpu.VMEM((head, total), BF),
                pltpu.VMEM((total, head), F32),
                pltpu.VMEM((total, head), F32),
            ],
        ),
        out_shape=[
            jax.ShapeDtypeStruct(queries.shape, BF),
            jax.ShapeDtypeStruct(key_values.shape, F32),
        ],
        compiler_params=pltpu.CompilerParams(vmem_limit_bytes=VMEM_BYTES),
        cost_estimate=LIGHT,
    )(lengths, key, queries, upstream, key_values)


def backward_kernel(
    lengths_ref,
    key_ref,
    q_ref,
    up_ref,
    attn_ref,
    kv_ref,
    lse_ref,
    more_ref,
    cos_ref,
    sin_ref,
    grads_ref,
    keys,
    values,
    keys_t,
    dk,
    dv,
):
    count, _, chunk, width = q_ref.shape
    head = keys.shape[1]
    total = keys.shape[0]
    block = min(QUERY_ROWS, total)
    per_block = block // chunk
    key = key_ref[0]
    length = lengths_ref[pl.program_id(0)]
    scale = 1.0 / math.sqrt(head)
    load_keys(key, kv_ref, keys, count, head, 0)
    load_keys(key, kv_ref, values, count, head, 1)
    transpose_rows(keys, keys_t)
    for place in range(count):
        rows = slice(place * chunk, (place + 1) * chunk)
        dk[rows, :] = more_ref[place ^ key, 0, :, :head]
        dv[rows, :] = more_ref[place ^ key, 0, :, head:]
    for start in range(0, total, block):
        limit_row = start + lax.broadcasted_iota(jnp.int32, (1, block), 1)
        limit = jnp.minimum(limit_row, length - 1)
        seen = start + block
        places = [(start // chunk + i) ^ key for i in range(per_block)]
        for h in range(width // head):
            columns = slice(h * head, (h + 1) * head)
            queries = jnp.concatenate([q_ref[p, 0, :, columns] for p in places], 0)
            upstream = jnp.concatenate([up_ref[p, 0, :, columns] for p in places], 0)
            attn = jnp.concatenate([attn_ref[p, 0, :, columns] for p in places], 0)
            centre = jnp.sum((upstream.astype(F32) * attn.astype(F32)).T, 0, keepdims=True)
            scores = masked_scores(keys[:seen, :], queries, limit)
            probs = jnp.exp(scores - lse_ref[0, h : h + 1, start : start + block])
            d_probs = dot_nt(values[:seen, :], upstream)
            d_scores = (probs * (d_probs - centre)).astype(BF)
            d_queries = dot_nn(keys_t[:, :seen], d_scores).T.astype(BF).astype(F32) * scale
            span = slice(start, start + block)
            d_queries = (
                d_queries * cos_ref[span, :]
                - pltpu.roll(d_queries, head // 2, 1) * sin_ref[span, :]
            ).astype(BF)
            for i, p in enumerate(places):
                grads_ref[p, 0, :, columns] = d_queries[i * chunk : (i + 1) * chunk]
            dk[:seen, :] += dot_nn(d_scores, queries)
            dv[:seen, :] += dot_nn(probs.astype(BF), upstream)
    for place in range(count):
        rows = slice(place * chunk, (place + 1) * chunk)
        turned = dk[rows, :] * cos_ref[rows, :] - pltpu.roll(dk[rows, :], head // 2, 1) * sin_ref[rows, :]
        grads_ref[place ^ key, 0, :, width : width + head] = turned.astype(BF)
        grads_ref[place ^ key, 0, :, width + head :] = dv[rows, :].astype(BF)


def attend_backward(queries, upstream, attn, key_values, lse, more, tables, lengths, key, head):
    count, seqs, chunk, width = queries.shape
    total = count * chunk
    heads = width // head
    whole = lambda s, *_: (0, s, 0, 0)
    by_head = pl.BlockSpec((count, 1, chunk, width), whole)
    shared = pl.BlockSpec((count, 1, chunk, 2 * head), whole)
    return pl.pallas_call(
        backward_kernel,
        grid_spec=pltpu.PrefetchScalarGridSpec(
            num_scalar_prefetch=2,
            grid=(seqs,),
            in_specs=[
                by_head,
                by_head,
                by_head,
                shared,
                pl.BlockSpec((1, heads, total), lambda s, *_: (s, 0, 0)),
                shared,
                pl.BlockSpec((total, head), lambda s, *_: (0, 0)),
                pl.BlockSpec((total, head), lambda s, *_: (0, 0)),
            ],
            out_specs=pl.BlockSpec((count, 1, chunk, width + 2 * head), whole),
            scratch_shapes=[
                pltpu.VMEM((total, head), BF),
                pltpu.VMEM((total, head), BF),
                pltpu.VMEM((head, total), BF),
                pltpu.VMEM((total, head), F32),
                pltpu.VMEM((total, head), F32),
            ],
        ),
        out_shape=jax.ShapeDtypeStruct((count, seqs, chunk, width + 2 * head), BF),
        compiler_params=pltpu.CompilerParams(vmem_limit_bytes=VMEM_BYTES),
        cost_estimate=LIGHT,
    )(lengths, key, queries, upstream, attn, key_values, lse, more, *tables)


def front_kernel(key_ref, a_ref, b_ref, gain_ref, wq_ref, wkv_ref, cos_ref, sin_ref, *rest, first):
    na_ref, nb_ref, q_ref, kv_ref = rest[-4:]
    _, seqs, chunk, width = q_ref.shape
    head = kv_ref.shape[3] // 2
    scale = 1.0 / math.sqrt(head)
    for i, piece in enumerate((a_ref, b_ref)):
        inputs = piece[...].astype(F32)
        normed = (
            inputs
            * lax.rsqrt(jnp.mean(inputs * inputs, -1, keepdims=True) + EPSILON)
            * gain_ref[...]
        ).astype(BF)
        (na_ref, nb_ref)[i][...] = normed
        q_linear = dot_nn(normed, wq_ref[...])
        kv_linear = dot_nn(normed, wkv_ref[...])
        span = pl.ds(pl.multiple_of(((first + i) ^ key_ref[0]) * chunk, chunk), chunk)
        cosine, sine = cos_ref[span, :], sin_ref[span, :]
        turn = lambda v: v * cosine + pltpu.roll(v, head // 2, 1) * sine
        for s in range(seqs):
            rows = slice(s * chunk, (s + 1) * chunk)
            for h in range(width // head):
                columns = slice(h * head, (h + 1) * head)
                q_ref[i, s, :, columns] = (turn(q_linear[rows, columns]) * scale).astype(BF)
            kv_ref[i, s, :, :head] = turn(kv_linear[rows, :head]).astype(BF)
            kv_ref[i, s, :, head:] = kv_linear[rows, head:].astype(BF)


def whole_spec(array):
    return pl.BlockSpec(array.shape, lambda *_: (0,) * array.ndim)


def pair_spec(shape, pair):
    return pl.BlockSpec((2, *shape[1:]), lambda *_: (pair,) + (0,) * (len(shape) - 1))


def front_pair(key, pieces, pair, gain, wq, wkv, tables, seqs, count, before):
    rows, width = pieces[0].shape
    chunk = rows // seqs
    shapes = [
        (count, seqs, chunk, wq.shape[1]),
        (count, seqs, chunk, wkv.shape[1]),
    ]
    given = [*pieces, gain, wq, wkv, *tables]
    return pl.pallas_call(
        functools.partial(front_kernel, first=2 * pair),
        grid_spec=pltpu.PrefetchScalarGridSpec(
            num_scalar_prefetch=1,
            grid=(1,),
            in_specs=[whole_spec(a) for a in given] + [pl.BlockSpec(memory_space=pl.ANY)] * len(before),
            out_specs=[whole_spec(pieces[0])] * 2 + [pair_spec(shape, pair) for shape in shapes],
        ),
        out_shape=[jax.ShapeDtypeStruct((rows, width), BF)] * 2
        + [jax.ShapeDtypeStruct(shape, BF) for shape in shapes],
        input_output_aliases={1 + len(given) + i: 2 + i for i in range(len(before))},
        compiler_params=pltpu.CompilerParams(vmem_limit_bytes=VMEM_BYTES),
        cost_estimate=LIGHT,
    )(key, *given, *before)


def hidden_kernel(*refs, first, pairs):
    pieces, (shares_hbm, down_hbm) = refs[: 4 * pairs], refs[4 * pairs : 4 * pairs + 2]
    hidden_hbm, dgate_hbm, dup_hbm = refs[-11:-8]
    normed, branch, both, down, hidden, dgate, dup, sems = refs[-8:]
    rows = pieces[0].shape[0]
    lines, inner = shares_hbm.shape[0], down_hbm.shape[0]
    used = 0

    def copies(places):
        nonlocal used
        made = [pltpu.make_async_copy(a, b, sems.at[used + i]) for i, (a, b) in enumerate(places)]
        used += len(made)
        return made

    loads = copies([(shares_hbm.at[i], both.at[:, i]) for i in range(lines)])
    loads_normed, loads_branch, loads_down = [], [], []
    low, high = pl.ds(0, rows), pl.ds(rows, rows)
    for p in range(pairs):
        na, nb, ga, gb = pieces[4 * p : 4 * p + 4]
        loads_normed.append(copies([(na, normed.at[p, low]), (nb, normed.at[p, high])]))
        loads_branch.append(copies([(ga, branch.at[p, low]), (gb, branch.at[p, high])]))
        if p == 0:
            loads_down = copies([(down_hbm, down)])
    for load in [*loads, *loads_normed[0], *loads_branch[0], *loads_down]:
        load.start()
    for p in range(1, pairs):
        for load in [*loads_normed[p], *loads_branch[p]]:
            load.start()
    for load in loads:
        load.wait()
    stores = []
    for p in range(pairs):
        for load in loads_normed[p]:
            load.wait()
        gate_up = dot_nn(normed[p], both[...].reshape(-1, 2 * inner))
        gate_pre, up_pre = gate_up[:, :inner], gate_up[:, inner:]
        sigma = jax.nn.sigmoid(gate_pre)
        silu_gate = gate_pre * sigma
        slope = sigma * (1.0 + gate_pre * (1.0 - sigma))
        for load in [*loads_branch[p], *(loads_down if p == 0 else [])]:
            load.wait()
        grad_hidden = dot_nt(branch[p], down[...])
        hidden[p] = (silu_gate * up_pre).astype(BF)
        dgate[p] = (grad_hidden * up_pre * slope).astype(BF)
        dup[p] = (grad_hidden * silu_gate).astype(BF)
        places = []
        for stack, target in ((hidden, hidden_hbm), (dgate, dgate_hbm), (dup, dup_hbm)):
            places += [(stack.at[p, low], target.at[first + 2 * p])]
            places += [(stack.at[p, high], target.at[first + 2 * p + 1])]
        stores += copies(places)
        for store in stores[-6:]:
            store.start()
    for store in stores:
        store.wait()


def hidden_pairs(normed, branch, first, shares, down, count, before):
    rows, width = normed[0].shape
    inner = down.shape[0]
    lines, _, share_rows, _ = shares.shape
    pairs = len(normed) // 2
    given = []
    for p in range(0, 2 * pairs, 2):
        given += [*normed[p : p + 2], *branch[p : p + 2]]
    given += [shares, down]
    anywhere = pl.BlockSpec(memory_space=pl.ANY)
    stacked = jax.ShapeDtypeStruct((count, rows, inner), BF)
    return pl.pallas_call(
        functools.partial(hidden_kernel, first=first, pairs=pairs),
        in_specs=[anywhere] * (len(given) + len(before)),
        out_specs=[anywhere] * 3,
        out_shape=[stacked] * 3,
        scratch_shapes=[pltpu.VMEM((pairs, 2 * rows, width), BF)] * 2
        + [pltpu.VMEM((count, lines, share_rows, 2 * inner), BF), pltpu.VMEM(down.shape, BF)]
        + [pltpu.VMEM((pairs, 2 * rows, inner), BF)] * 3
        + [pltpu.SemaphoreType.DMA((lines + 1 + 10 * pairs,))],
        input_output_aliases={len(given) + i: i for i in range(len(before))},
        compiler_params=pltpu.CompilerParams(vmem_limit_bytes=MLP_VMEM_BYTES),
        cost_estimate=pl.CostEstimate(
            flops=20 * pairs * rows * width * inner,
            bytes_accessed=6 * width * inner + 12 * pairs * rows * width,
            transcendentals=2 * pairs * rows * inner,
        ),
    )(*given, *before)


def mlp_parts_kernel(hidden_hbm, dgate_hbm, dup_hbm, shares_hbm, down_hbm, *rest, first):
    pa_hbm, pb_hbm, oa_hbm, ob_hbm = rest[:4]
    hidden, dgate, dup, both, down, parts, outs, sems = rest[4:]
    rows = pa_hbm.shape[0]
    lines, inner = shares_hbm.shape[0], down_hbm.shape[0]
    low, high = pl.ds(0, rows), pl.ds(rows, rows)
    both_stacks = ((dgate_hbm, dgate), (dup_hbm, dup), (hidden_hbm, hidden))
    places = [(stack.at[pl.ds(first, 2)], target) for stack, target in both_stacks]
    places += [(shares_hbm.at[i], both.at[:, i]) for i in range(lines)]
    places += [(down_hbm, down)]
    loads = [pltpu.make_async_copy(a, b, sems.at[i]) for i, (a, b) in enumerate(places)]
    places = [(parts.at[low], pa_hbm), (parts.at[high], pb_hbm)]
    places += [(outs.at[low], oa_hbm), (outs.at[high], ob_hbm)]
    stores = [
        pltpu.make_async_copy(a, b, sems.at[len(loads) + i]) for i, (a, b) in enumerate(places)
    ]
    for load in loads:
        load.start()
    for load in loads[: lines + 3]:
        load.wait()
    both_cols = both[...].reshape(-1, 2 * inner)
    for i in range(2):
        grads = dot_nt(jnp.concatenate([dgate[i], dup[i]], 1), both_cols)
        parts[i * rows : (i + 1) * rows, :] = grads.astype(BF)
        stores[i].start()
    loads[-1].wait()
    for i in range(2):
        outs[i * rows : (i + 1) * rows, :] = dot_nn(hidden[i], down[...]).astype(BF)
        stores[2 + i].start()
    for store in stores:
        store.wait()


def mlp_parts(stacks, pair, shares, down):
    count, rows, inner = stacks[0].shape
    width = down.shape[1]
    lines, _, share_rows, _ = shares.shape
    anywhere = pl.BlockSpec(memory_space=pl.ANY)
    apart = jax.ShapeDtypeStruct((rows, width), BF)
    return pl.pallas_call(
        functools.partial(mlp_parts_kernel, first=2 * pair),
        in_specs=[anywhere] * 5,
        out_specs=[anywhere] * 4,
        out_shape=[apart] * 4,
        scratch_shapes=[pltpu.VMEM((2, rows, inner), BF)] * 3
        + [pltpu.VMEM((count, lines, share_rows, 2 * inner), BF), pltpu.VMEM(down.shape, BF)]
        + [pltpu.VMEM((2 * rows, width), BF)] * 2
        + [pltpu.SemaphoreType.DMA((lines + 8,))],
        compiler_params=pltpu.CompilerParams(vmem_limit_bytes=MLP_VMEM_BYTES),
        cost_estimate=pl.CostEstimate(
            flops=20 * rows * width * inner,
            bytes_accessed=6 * width * inner + 12 * rows * width,
            transcendentals=0,
        ),
    )(*stacks, shares, down)


def proj_kernel(a_ref, b_ref, w_ref, attn_ref, *rest, last):
    dattn_ref, total_ref = rest[-2:]
    seqs, chunk = attn_ref.shape[1:3]
    total = None if len(rest) == 2 else rest[1][...]
    for i, piece in enumerate((a_ref, b_ref)):
        grads = piece[...]
        d_attn = dot_nt(grads, w_ref[...]).astype(BF)
        for s in range(seqs):
            rows = slice(s * chunk, (s + 1) * chunk)
            dattn_ref[i, s] = d_attn[rows]
            share = dot_tn(attn_ref[i, s], grads[rows])
            total = share if total is None else total + share
    total_ref[...] = total.astype(total_ref.dtype)


def proj_pair(pieces, pair, w_out, attn, count, before):
    last = 2 * pair + 2 == count
    rows, width = pieces[0].shape
    given = [*pieces, w_out]
    extra_specs = []
    aliases = {}
    if before:
        extra_specs = [pl.BlockSpec(memory_space=pl.ANY), whole_spec(before[1])]
        aliases = {4: 0} if last else {4: 0, 5: 1}
    total = jax.ShapeDtypeStruct(w_out.shape, BF if last else F32)
    return pl.pallas_call(
        functools.partial(proj_kernel, last=last),
        grid=(1,),
        in_specs=[whole_spec(a) for a in given] + [pair_spec(attn.shape, pair)] + extra_specs,
        out_specs=[pair_spec(attn.shape, pair), whole_spec(total)],
        out_shape=[jax.ShapeDtypeStruct(attn.shape, BF), total],
        input_output_aliases=aliases,
        compiler_params=pltpu.CompilerParams(vmem_limit_bytes=VMEM_BYTES),
        cost_estimate=LIGHT,
    )(*given, attn, *before)


def parts_kernel(*refs, count, turned):
    lefts, weights = refs[: len(turned)], refs[len(turned) : 2 * len(turned)]
    outs, (buffer, sems) = refs[2 * len(turned) : -2], refs[-2:]
    order = (6, 7, 2, 3, 4, 5, 0, 1) if count == 8 else range(count)
    stores = []
    for j in order:
        total = None
        for left, weight, turn in zip(lefts, weights, turned):
            share = (dot_nt if turn else dot_nn)(left[j], weight[...])
            total = share if total is None else total + share
        buffer[j] = total.astype(BF)
        stores.append(pltpu.make_async_copy(buffer.at[j], outs[j], sems.at[j]))
        stores[-1].start()
    for store in stores:
        store.wait()


def parts_of(lefts, weights, turned):
    count, rows = lefts[0].shape[:2]
    width = weights[0].shape[0 if turned[0] else 1]
    return pl.pallas_call(
        functools.partial(parts_kernel, count=count, turned=turned),
        grid=(1,),
        in_specs=[whole_spec(a) for a in (*lefts, *weights)],
        out_specs=[pl.BlockSpec(memory_space=pl.ANY)] * count,
        out_shape=[jax.ShapeDtypeStruct((rows, width), BF)] * count,
        scratch_shapes=[
            pltpu.VMEM((count, rows, width), BF),
            pltpu.SemaphoreType.DMA((count,)),
        ],
        compiler_params=pltpu.CompilerParams(vmem_limit_bytes=VMEM_BYTES),
        cost_estimate=LIGHT,
    )(*lefts, *weights)


def outer_kernel(*refs, count, rights):
    left = jnp.concatenate([ref[...] for ref in refs[:count]], 0)
    left_t = left.T
    for right, out in zip(refs[count : count + rights], refs[count + rights :]):
        out[...] = dot_nn(left_t, right[...]).astype(BF)


def outer_of(pieces, rights):
    count = len(pieces)
    rows, width = pieces[0].shape
    step = min(256, width)
    return pl.pallas_call(
        functools.partial(outer_kernel, count=count, rights=len(rights)),
        grid=(width // step,),
        in_specs=[pl.BlockSpec((rows, step), lambda i: (0, i))] * count
        + [pl.BlockSpec(right.shape, lambda i: (0, 0)) for right in rights],
        out_specs=[pl.BlockSpec((step, right.shape[1]), lambda i: (i, 0)) for right in rights],
        out_shape=[jax.ShapeDtypeStruct((width, right.shape[1]), BF) for right in rights],
        compiler_params=pltpu.CompilerParams(vmem_limit_bytes=VMEM_BYTES),
        cost_estimate=LIGHT,
    )(*pieces, *rights)


def inner_kernel(*refs, count, lefts):
    pieces = refs[lefts : lefts + count]
    outs, lefts_t = refs[lefts + count : 2 * lefts + count], refs[2 * lefts + count :]
    rows = pieces[0].shape[0]

    @pl.when(pl.program_id(0) == 0)
    def _():
        for left, left_t in zip(refs[:lefts], lefts_t):
            for j in range(count):
                span = slice(j * rows, (j + 1) * rows)
                left_t[:, span] = left[span, :].T

    right = jnp.concatenate([piece[...] for piece in pieces], 0)
    for out, left_t in zip(outs, lefts_t):
        out[...] = dot_nn(left_t[...], right).astype(BF)


def inner_of(lefts, pieces):
    count = len(pieces)
    rows, width = pieces[0].shape
    step = min(256, width)
    columns = lefts[0].shape[1]
    return pl.pallas_call(
        functools.partial(inner_kernel, count=count, lefts=len(lefts)),
        grid=(width // step,),
        in_specs=[pl.BlockSpec(left.shape, lambda i: (0, 0)) for left in lefts]
        + [pl.BlockSpec((rows, step), lambda i: (0, i))] * count,
        out_specs=[pl.BlockSpec((columns, step), lambda i: (0, i))] * len(lefts),
        out_shape=[jax.ShapeDtypeStruct((columns, width), BF)] * len(lefts),
        scratch_shapes=[pltpu.VMEM((columns, count * rows), BF)] * len(lefts),
        compiler_params=pltpu.CompilerParams(vmem_limit_bytes=VMEM_BYTES),
        cost_estimate=LIGHT,
    )(*lefts, *pieces)


def widen_kernel(query_ref, out_ref, small_ref, query_f, out_f, key_f, value_f, gains_f):
    width, head = query_ref.shape[2], key_f.shape[1]
    for j in range(query_ref.shape[0]):
        query_f[:, j * width : (j + 1) * width] = query_ref[j].astype(F32)
    out_f[...] = out_ref[...].astype(F32)
    rows = key_f.shape[0]
    key_f[...] = small_ref[:rows, :head].astype(F32)
    value_f[...] = small_ref[:rows, head:].astype(F32)
    gains_f[...] = small_ref[rows:, :].astype(F32)


def widen(query_blocks, out_sum, small, head):
    count, rows, width = query_blocks.shape
    shapes = [(rows, count * width), out_sum.shape, (rows, head), (rows, head)]
    shapes = [jax.ShapeDtypeStruct(shape, F32) for shape in (*shapes, (small.shape[0] - rows, 2 * head))]
    given = [query_blocks, out_sum, small]
    return pl.pallas_call(
        widen_kernel,
        grid=(1,),
        in_specs=[whole_spec(a) for a in given],
        out_specs=[whole_spec(a) for a in shapes],
        out_shape=shapes,
        compiler_params=pltpu.CompilerParams(vmem_limit_bytes=VMEM_BYTES),
        cost_estimate=LIGHT,
    )(*given)


def turn_kernel(blocks_ref, out_ref):
    turned = [blocks_ref[j].astype(F32).T for j in range(blocks_ref.shape[0])]
    out_ref[...] = jnp.concatenate(turned, 1)


def turn_blocks(blocks):
    count, columns, rows = blocks.shape
    step = min(128, rows)
    return pl.pallas_call(
        turn_kernel,
        grid=(rows // step,),
        in_specs=[pl.BlockSpec((count, columns, step), lambda i: (0, 0, i))],
        out_specs=pl.BlockSpec((step, count * columns), lambda i: (i, 0)),
        out_shape=jax.ShapeDtypeStruct((rows, count * columns), F32),
        compiler_params=pltpu.CompilerParams(vmem_limit_bytes=VMEM_BYTES),
        cost_estimate=LIGHT,
    )(blocks)


def spread_rows(share_t, count):
    columns, rows = share_t.shape
    blocks = share_t.reshape(columns, count, rows // count).transpose(1, 0, 2)
    return lax.all_to_all(blocks, "seq", split_axis=0, concat_axis=0, tiled=True)


def pack_kernel(place_ref, gate_hbm, up_hbm, out_ref, gate_ref, up_ref, sems):
    count, rows, _ = out_ref.shape
    inner = gate_ref.shape[1] // count
    span = pl.ds(pl.multiple_of(place_ref[0] * rows, rows), rows)
    loads = [
        pltpu.make_async_copy(gate_hbm.at[span], gate_ref, sems.at[0]),
        pltpu.make_async_copy(up_hbm.at[span], up_ref, sems.at[1]),
    ]
    for load in loads:
        load.start()
    for load in loads:
        load.wait()
    gate, up = gate_ref[...], up_ref[...]
    for j in range(count):
        columns = slice(j * inner, (j + 1) * inner)
        out_ref[j] = jnp.concatenate([gate[:, columns], up[:, columns]], 1)


def pack_weights(w_gate, w_up, count):
    lines = lax.axis_size("dp")
    rows, columns = w_gate.shape[0] // lines, w_gate.shape[1]
    place = lax.axis_index("dp").astype(jnp.int32).reshape(1)
    anywhere = pl.BlockSpec(memory_space=pl.ANY)
    shape = (count, rows, 2 * columns // count)
    return pl.pallas_call(
        pack_kernel,
        grid_spec=pltpu.PrefetchScalarGridSpec(
            num_scalar_prefetch=1,
            grid=(1,),
            in_specs=[anywhere, anywhere],
            out_specs=pl.BlockSpec(shape, lambda i, place: (0, 0, 0)),
            scratch_shapes=[
                pltpu.VMEM((rows, columns), BF),
                pltpu.VMEM((rows, columns), BF),
                pltpu.SemaphoreType.DMA((2,)),
            ],
        ),
        out_shape=jax.ShapeDtypeStruct(shape, BF),
        compiler_params=pltpu.CompilerParams(vmem_limit_bytes=VMEM_BYTES),
        cost_estimate=LIGHT,
    )(place, w_gate, w_up)


def share_weights(w_gate, w_up, w_query, count):
    packed = pack_weights(w_gate, w_up, count)
    packed = lax.all_to_all(packed, "seq", split_axis=0, concat_axis=0, tiled=True)
    query = rows_to_columns(w_query + packed[0, 0, 0] * 0)
    return query, lax.all_gather(packed, "dp", axis=0, tiled=False)


def rope_tables(positions, head_width):
    half_width = head_width // 2
    spacing = jnp.exp(
        jnp.arange(half_width).astype(F32) * (-2.0 * math.log(10000.0) / head_width)
    )
    angles = positions.astype(F32)[:, None] * spacing[None, :]
    sines = jnp.sin(angles)
    cosines = jnp.cos(angles)
    return (jnp.concatenate([cosines, cosines], 1), jnp.concatenate([-sines, sines], 1))


def rms_scale(values_in):
    return lax.rsqrt(jnp.mean(values_in * values_in, -1, keepdims=True) + EPSILON)


def norm_back(grad_normed, inputs, scale_rows, gain):
    weighted = grad_normed * gain
    cubed = scale_rows * scale_rows * scale_rows
    return scale_rows * weighted - inputs * cubed * jnp.mean(weighted * inputs, -1, keepdims=True)


def body(
    tokens,
    lengths,
    second_queries,
    cotangent,
    second_cotangent,
    gain_attn,
    w_query,
    w_key,
    w_value,
    w_out,
    gain_mlp,
    w_gate,
    w_up,
    w_down,
):
    count = lax.axis_size("seq")
    rank = lax.axis_index("seq")
    key = order_key(count)
    keys_of = jnp.stack([key, rank]).astype(jnp.int32)
    seqs, chunk, width = tokens.shape
    head = w_key.shape[1]
    rows = seqs * chunk
    all_rows = count * rows
    own_columns = w_query.shape[0]

    query_cols, shares = share_weights(w_gate, w_up, w_query, count)
    gain_rows = jnp.zeros((16, 2 * head), BF)
    gain_rows = gain_rows.at[:2, :own_columns].set(jnp.stack([gain_attn, gain_mlp]))
    packed = jnp.concatenate([jnp.concatenate([w_key, w_value], 1), gain_rows], 0)
    packed = gather_ordered(packed, count)
    kv_mat = packed[:, :own_columns].reshape(width, 2 * head)
    gain_one = packed[:, own_columns, :own_columns].reshape(1, width).astype(F32)
    gain_two = packed[:, own_columns + 1, :own_columns].reshape(1, width).astype(F32)

    local_pos = rank * chunk + jnp.arange(chunk, dtype=jnp.int32)
    valid = (local_pos[None, :] < lengths[:, None]).astype(F32).reshape(rows, 1)
    tables = rope_tables(jnp.arange(count * chunk, dtype=jnp.int32), head)

    last_pair = count // 2 - 1
    inputs = tokens.reshape(rows, width)
    front_of = lambda pair, two, before: front_pair(
        keys_of, two, pair, gain_one, query_cols, kv_mat, tables, seqs, count, before
    )
    near = gather_near(inputs, count)
    normed_one = []
    stacks = []
    far = gather_far(near, count)
    for pair in range(last_pair):
        *normed, queries, key_values = front_of(pair, near[2 * pair : 2 * pair + 2], stacks)
        normed_one += normed
        stacks = [queries, key_values]
    last = gather_last(near, far, count)
    grad_out = cotangent.reshape(rows, width).astype(F32) * valid
    branch_near = gather_near(after(grad_out.astype(BF), far), count, stacks)
    branch_far = gather_far(after(branch_near, stacks), count)
    *normed, queries, key_values = front_of(last_pair, [far, last], stacks)
    normed_one += normed
    attn, lse = attend_forward(queries, key_values, lengths, keys_of, head)
    attn, branch_far = lax.optimization_barrier((attn, branch_far))
    proj_parts = parts_of([attn.reshape(count, rows, -1)], [w_out], (False,))
    inputs_f = inputs.astype(F32)
    scale_one = rms_scale(inputs_f)

    branch_last = gather_last(branch_near, branch_far, count)
    branch = (branch_near if is_cube(count) else branch_near[:-2]) + [branch_far, branch_last]
    grad_second, dkv_second = attend_second(
        after(second_queries, proj_parts), second_cotangent, key_values, lengths, keys_of, head
    )
    proj_sum = scatter_pieces(proj_parts, count, dkv_second)
    proj_sum, shares = lax.optimization_barrier((proj_sum, shares))
    middle = inputs_f + proj_sum.astype(F32)

    scale_two = rms_scale(middle)
    sync = lax.optimization_barrier
    always = lengths[0] > 0
    hidden_of = lambda first, pieces, before: tuple(
        hidden_pairs(pieces, branch[first : first + len(pieces)], first, shares, w_down, count, before)
    )
    normed_own = (middle * scale_two * gain_two).astype(BF)

    def middle_pairs(near, stacks):
        for first in range(2, 2 * last_pair, 4):
            stacks = hidden_of(first, near[first : min(first + 4, 2 * last_pair)], stacks)
        return tuple(stacks)

    if is_cube(count):
        from_x, from_y, from_core = swap(normed_own, 2), swap(normed_own, 4), swap(normed_own, 1)
        stacks = stage(always, lambda *two: hidden_of(0, two, []), normed_own, from_core)
        from_x, from_y, stacks = sync((from_x, from_y, stacks))
        near = [normed_own, from_core, from_x, swap(from_x, 1), from_y, swap(from_y, 1)]
        halves = far_halves(near)
        stacks = stage(always, middle_pairs, near, stacks)
        halves, stacks = sync((halves, stacks))
        far = jnp.concatenate(halves, 0)
        last = swap(far, 1)
    else:
        near = gather_near(normed_own, count)
        stacks = middle_pairs(near, hidden_of(0, near[:2], []))
        far, last = near[-2:]
    stacks = hidden_of(2 * last_pair, [far, last], list(stacks))
    hidden, grad_gate, grad_up = [stack.reshape(all_rows, -1) for stack in stacks]
    normed_two = (near if is_cube(count) else near[:-2]) + [far, last]
    split = queries.shape[-1]
    (w_gate_share,) = inner_of([grad_gate], normed_two)
    gate_sum = lax.psum(w_gate_share, "dp")

    def parts_mlp(stacks):
        parts = [mlp_parts(stacks, pair, shares, w_down) for pair in range(last_pair + 1)]
        normed_parts = [part for step in parts for part in step[:2]]
        return normed_parts, [part for step in parts for part in step[2:]]

    normed_parts, out_parts = stage(always, parts_mlp, stacks)

    def scatter_mlp(normed_parts, hidden):
        return scatter_far(normed_parts, count), inner_of([hidden], branch)[0]

    two_sums, w_down_share = stage(always, scatter_mlp, normed_parts, hidden)
    def sum_mlp(two_sums, grad_up):
        (w_up_share,) = inner_of([grad_up], normed_two)
        grad_normed_two = scatter_near(two_sums, count, w_up_share).astype(F32)
        grad_middle = grad_out + norm_back(grad_normed_two, middle, scale_two, gain_two)
        return grad_middle, jnp.sum(grad_normed_two * (middle * scale_two), 0), w_up_share

    grad_middle, gain_share, w_up_share = stage(always, sum_mlp, two_sums, grad_up)
    grad_middle, w_up_share, w_down_share, gate_sum = sync(
        (grad_middle, w_up_share, w_down_share, gate_sum)
    )
    up_sum, down_sum = lax.psum((w_up_share, w_down_share), "dp")
    proj_of = lambda pair, two, before: proj_pair(two, pair, w_out, attn, count, before)

    def gather_middle(grad_middle):
        near = gather_near(grad_middle.astype(BF), count)
        return near, proj_of(0, near[:2], [])

    near, state = stage(always, gather_middle, grad_middle)

    def project_back(near, state):
        far = gather_far(near, count)
        for pair in range(1, last_pair):
            state = proj_of(pair, near[2 * pair : 2 * pair + 2], state)
        last = gather_last(near, far, count)
        return proj_of(last_pair, [far, last], state)

    grad_attn, w_out_share = stage(always, project_back, near, state)
    grad_attn, gate_sum = sync((grad_attn, gate_sum))
    gate_blocks = spread_rows(gate_sum, count)

    def attention_back(grad_attn, out_parts):
        out_sums = scatter_far(out_parts, count)
        grads = attend_backward(
            queries, grad_attn, attn, key_values, lse, dkv_second, tables, lengths, keys_of, head
        )
        grads = grads.reshape(count, rows, -1)
        one_parts = parts_of(
            [grads[..., :split], grads[..., split:]], [query_cols, kv_mat], (True, True)
        )
        (w_one_share,) = outer_of(normed_one, [grads.reshape(all_rows, -1)])
        return out_sums, one_parts, w_one_share

    out_sums, one_parts, w_one_share = stage(always, attention_back, grad_attn, out_parts)
    one_parts, w_one_share, gate_blocks = sync((one_parts, w_one_share, gate_blocks))
    w_query_share = w_one_share[:, :split].reshape(count, own_columns, split)
    w_query_share = lax.all_to_all(w_query_share, "seq", split_axis=0, concat_axis=0, tiled=True)
    own_gain = gain_attn.shape[0]

    def scatter_attention(one_parts, w_one_share):
        kv_shares = w_one_share[:, split:].reshape(count, own_columns, 2 * head)
        return scatter_far(one_parts, count), small_scatter(kv_shares, count)

    one_sums, w_kv_share = stage(always, scatter_attention, one_parts, w_one_share)

    def sum_attention(one_sums, w_kv_share):
        grad_normed_one = scatter_near(one_sums, count).astype(F32)
        grad_tokens = grad_middle + norm_back(grad_normed_one, inputs_f, scale_one, gain_one)
        gain_shares = jnp.stack([jnp.sum(grad_normed_one * (inputs_f * scale_one), 0), gain_share])
        gain_shares = gain_shares.astype(BF).reshape(2, count, own_gain).transpose(1, 0, 2)
        gain_shares = jnp.pad(gain_shares, ((0, 0), (0, 14), (0, 2 * head - own_gain)))
        small = jnp.concatenate([w_kv_share, small_scatter(gain_shares, count)], 0)
        return grad_tokens, small

    grad_tokens, small = stage(always, sum_attention, one_sums, w_kv_share)
    small, w_query_share, w_out_share, up_sum, down_sum = sync(
        (small, w_query_share, w_out_share, up_sum, down_sum)
    )
    late = lax.psum((w_out_share, w_query_share.reshape(-1, split), small), "dp")

    def sum_rest(out_sums, gate_blocks, down_sum, up_sum):
        up_blocks = spread_rows(up_sum, count)
        out = (middle + scatter_near(out_sums, count).astype(F32)).astype(BF)
        return out, turn_blocks(gate_blocks), turn_blocks(up_blocks), down_sum.astype(F32)

    out, grad_w_gate, grad_w_up, grad_w_down = stage(
        always, sum_rest, out_sums, gate_blocks, down_sum, up_sum
    )
    late, grad_w_up = sync((late, grad_w_up))
    w_out_sum, w_query_sum, small = late
    grad_w_query, w_out_sum, grad_w_key, grad_w_value, grad_gains = widen(
        w_query_sum.reshape(count, own_columns, split), w_out_sum, small, head
    )

    return (
        out.reshape(tokens.shape),
        grad_tokens.reshape(tokens.shape),
        grad_second,
        grad_gains[0, :own_gain],
        grad_w_query,
        grad_w_key,
        grad_w_value,
        w_out_sum.astype(F32),
        grad_gains[1, :own_gain],
        grad_w_gate,
        grad_w_up,
        grad_w_down,
    )


def solution(mesh):
    return jax.shard_map(
        body,
        mesh=mesh,
        in_specs=(
            P("dp", "seq", None),
            P("dp"),
            P("dp", "seq", None),
            P("dp", "seq", None),
            P("dp", "seq", None),
            P("seq"),
            P("seq", None),
            P("seq", None),
            P("seq", None),
            P("seq", None),
            P("seq"),
            P("seq", None),
            P("seq", None),
            P("seq", None),
        ),
        out_specs=(
            P("dp", "seq", None),
            P("dp", "seq", None),
            P("dp", "seq", None),
            P("seq"),
            P("seq", None),
            P("seq", None),
            P("seq", None),
            P("seq", None),
            P("seq"),
            P("seq", None),
            P("seq", None),
            P("seq", None),
        ),
        check_vma=False,
    )
```
